32 devices in a mesh: dp: 4 (over x, core), seq: 8 (over z, y).
Axes of the slice: x: 2, y: 2, z: 4, core: 2. Of those that a mesh axis runs over, the one named last changes fastest.
Arguments:
- tokens: bfloat16 [16, 2048, 768], P('dp', 'seq'), may hold values from -6 to 6
- lengths: int32 [16], P('dp'), may hold values from 32 to 2048, as said below
- cotangent: bfloat16 [16, 2048, 768], P('dp', 'seq'), may hold values from -6 to 6
- norm_gain: bfloat16 [2, 768], P(None, 'dp'), may hold values from 0.25 to 1.75
- norm_bias: bfloat16 [2, 768], P(None, 'dp'), may hold values from -1.5 to 1.5
- in_weight: bfloat16 [3, 4, 192, 192], P(None, None, 'dp'), may hold values from -0.4375 to 0.4375
- conv_taps: bfloat16 [3, 3, 768], P(None, None, 'dp'), may hold values from -3 to 3
- filter_in: bfloat16 [5, 128], P(None, 'dp'), may hold values from -2.5 to 2.5
- filter_mid: bfloat16 [128, 128], P('dp'), may hold values from -0.5 to 0.5
- filter_bias: bfloat16 [2, 128], P(None, 'dp'), may hold values from -1.5 to 1.5
- filter_out: bfloat16 [128, 768], P('dp', 'seq'), may hold values from -0.0234375 to 0.0234375
- out_weight: bfloat16 [4, 192, 192], P(None, 'dp'), may hold values from -0.4375 to 0.4375
- up_weight: bfloat16 [2, 4, 192, 768], P(None, None, 'dp'), may hold values from -0.4375 to 0.4375
- down_weight: bfloat16 [4, 768, 192], P(None, 'dp'), may hold values from -0.21875 to 0.21875
Outputs:
- out_tokens: bfloat16 [16, 2048, 768], P('dp', 'seq')
- grad_tokens: float32 [16, 2048, 768], P('dp', 'seq')
- grad_norm_gain: float32 [2, 768], P(None, 'dp')
- grad_norm_bias: float32 [2, 768], P(None, 'dp')
- grad_in_weight: float32 [3, 4, 192, 192], P(None, None, 'dp')
- grad_conv_taps: float32 [3, 3, 768], P(None, None, 'dp')
- grad_filter_in: float32 [5, 128], P(None, 'dp')
- grad_filter_mid: float32 [128, 128], P('dp')
- grad_filter_bias: float32 [2, 128], P(None, 'dp')
- grad_filter_out: float32 [128, 768], P('dp', 'seq')
- grad_out_weight: float32 [4, 192, 192], P(None, 'dp')
- grad_up_weight: float32 [2, 4, 192, 768], P(None, None, 'dp')
- grad_down_weight: float32 [4, 768, 192], P(None, 'dp')
The draws below stay inside these ranges and needn't reach their ends.
Inputs may be any that keep to these rules, and one draw needn't show every extreme that they name: Each aligned block of 4 rows (the sequences of one index of dp) holds exactly one sequence of length 2048; the other lengths are shorter and have a heavy tail.
All inputs are finite; a program needn't handle non-finite values.
Results may differ from the reference program's by a relative error of at most 0.024.
Values may be sent and summed in bfloat16 or wider, within the bound.
No kernel may reach another device: no remote copies, remote signals or barrier semaphores. Data moves between devices by JAX's collectives and lax.ppermute only.
A program may use at most 192 MiB of HBM per device.

```python
import math
import jax
import jax.numpy as jnp
from jax import lax

D = 768
FF = 3072
NB = 4
FILTER = 128
EMB = 5
SEQ = 2048
MB = 4
B_MB = 1
BATCH = 16


def draw_lengths(key, part):
    key = jax.random.fold_in(key, 11)
    first_key, second_key, third_key = jax.random.split(key, 3)
    levels = (SEQ // 32).bit_length() - 1
    exponent = jax.random.randint(first_key, (BATCH,), 0, levels)
    lowest = 32 * jnp.left_shift(jnp.ones((BATCH,), jnp.int32), exponent)
    surplus = jax.random.randint(second_key, (BATCH,), 0, lowest)
    lengths_raw = jnp.minimum(lowest + surplus, SEQ - 1)
    group_rows = MB * B_MB
    chosen = jax.random.randint(third_key, (BATCH // group_rows,), 0, group_rows)
    longest = jnp.arange(BATCH, dtype=jnp.int32) % group_rows == jnp.repeat(chosen, group_rows)
    return jnp.where(longest, SEQ, lengths_raw).astype(jnp.int32)


def signed_magnitude(key, array_shape, ceiling, low_share):
    sign_key, size_key = jax.random.split(key)
    sign_part = jnp.where(jax.random.bernoulli(sign_key, 0.5, array_shape), 1.0, -1.0).astype(jnp.float32)
    size_part = jax.random.uniform(size_key, array_shape, jnp.float32, low_share, 1.0)
    return ceiling * sign_part * size_part


def draw_filter_in(key, part):
    key = jax.random.fold_in(key, 23)
    values = signed_magnitude(key, (EMB, FILTER), 2.5, 0.6)
    return values.astype(jnp.bfloat16)


def draw_filter_mid(key, part):
    key = jax.random.fold_in(key, 37)
    values = signed_magnitude(key, (FILTER, FILTER), 0.5, 0.7)
    return values.astype(jnp.bfloat16)


def level_of(key, shape, pieces, least, top_value):
    def one(axis_at, blocks):
        draws = jax.random.uniform(jax.random.fold_in(jax.random.fold_in(key, 6), axis_at), (blocks,), jnp.float32, least / len(pieces), top_value / len(pieces))
        return jnp.repeat(jnp.exp(draws), shape[axis_at] // blocks).reshape((-1,) + (1,) * (len(shape) - axis_at - 1))

    factor_of = one(*pieces[0])
    for cut in pieces[1:]:
        factor_of = factor_of * one(*cut)
    return factor_of


def scatter_about(stream_key, extent, scale, most, shards=(), held_as=jnp.bfloat16):
    gain = level_of(stream_key, extent, shards, -0.22, 0.18) if shards else 1.0
    values = jax.random.normal(stream_key, extent, jnp.float32) * scale * gain
    return jnp.minimum(jnp.maximum(values, -most), most).astype(held_as)


def setup_inputs(seed: int = 0) -> dict:
    key_list = jax.random.split(jax.random.key(seed), 15)
    return {
        "tokens": scatter_about(key_list[0], (BATCH, SEQ, D), 1.0, 6.0, ((0, 4), (1, 8))),
        "lengths": draw_lengths(jax.random.fold_in(key_list[14], 71), 0),
        "cotangent": scatter_about(key_list[2], (BATCH, SEQ, D), 1.0, 6.0, ((0, 4), (1, 8))),
        "norm_gain": jnp.clip(1.0 + 0.15 * jax.random.normal(key_list[3], (2, D), jnp.float32), 0.25, 1.75).astype(jnp.bfloat16),
        "norm_bias": scatter_about(key_list[4], (2, D), 0.3, 1.5, ((1, 4),)),
        "in_weight": scatter_about(key_list[5], (3, NB, D // NB, D // NB), (D // NB) ** -0.5, 0.4375, ((2, 4),)),
        "conv_taps": scatter_about(key_list[6], (3, 3, D), 0.6, 3.0, ((2, 4),)),
        "filter_in": draw_filter_in(jax.random.fold_in(key_list[14], 71), 0),
        "filter_mid": draw_filter_mid(jax.random.fold_in(key_list[14], 71), 0),
        "filter_bias": scatter_about(key_list[9], (2, FILTER), 0.3, 1.5, ((1, 4),)),
        "filter_out": scatter_about(key_list[10], (FILTER, D), (FILTER * SEQ // 4) ** -0.5, 0.0234375, ((0, 4), (1, 8))),
        "out_weight": scatter_about(key_list[11], (NB, D // NB, D // NB), (D // NB) ** -0.5, 0.4375, ((1, 4),)),
        "up_weight": scatter_about(key_list[12], (2, NB, D // NB, FF // NB), (D // NB) ** -0.5, 0.4375, ((2, 4),)),
        "down_weight": scatter_about(key_list[13], (NB, FF // NB, D // NB), (FF // NB) ** -0.5, 0.21875, ((1, 4),)),
    }


HIGH = lax.Precision.HIGHEST
EPS = 1e-05
SINE_FREQ = 10.0

@jax.custom_vjp
def low(v):
    return lax.optimization_barrier(v.astype(jnp.bfloat16)).astype(jnp.float32)

@jax.custom_vjp
def low_back(v):
    return v

def low_keep(v):
    return (low(v), None)

def low_pass(kept, grad):
    return (grad,)

def back_keep(v):
    return (v, None)

def back_low(kept, grad):
    return (low(grad),)
low.defvjp(low_keep, low_pass)
low_back.defvjp(back_keep, back_low)

def layer_norm(values, scales, offsets):
    average = lax.optimization_barrier(jnp.mean(values, axis=-1, keepdims=True))
    centred = values - average
    variance = lax.optimization_barrier(jnp.mean(centred * centred, axis=-1, keepdims=True))
    return centred * lax.rsqrt(variance + EPS) * scales + offsets

def block_product(inputs, weights):
    blocked = inputs.reshape(inputs.shape[0], weights.shape[0], -1)
    return jnp.einsum('rnb,nbo->rno', blocked, weights, precision=HIGH).reshape(inputs.shape[0], -1)

def lag_features(seq_length, size_fft):
    lags = jnp.arange(size_fft, dtype=jnp.int32)
    signed = jnp.where(lags < seq_length, lags, lags - size_fft)
    scaled = signed.astype(jnp.float32) / float(seq_length)
    feats = jnp.stack([scaled, jnp.cos(math.pi * scaled), jnp.sin(math.pi * scaled), jnp.cos(2.0 * math.pi * scaled), jnp.sin(2.0 * math.pi * scaled)], axis=1)
    return (feats, jnp.abs(scaled))

def decay_rates(channel_ids, width):
    fast = math.log(100.0) / 0.3
    slow = math.log(100.0) / 1.5
    return slow + (fast - slow) * channel_ids.astype(jnp.float32) / float(width - 1)

def filter_values(feats, distance, rates, filter_in, filter_mid, filter_bias, filter_out):
    first = jnp.sin(SINE_FREQ * (jnp.dot(feats, filter_in, precision=HIGH) + filter_bias[0]))
    second = jnp.sin(SINE_FREQ * (jnp.dot(first, filter_mid, precision=HIGH) + filter_bias[1]))
    raw = jnp.dot(second, filter_out, precision=HIGH)
    return (raw * jnp.exp(-distance[:, None] * rates[None, :])).T

def layer(inputs, keep_mask, norm_gain, norm_bias, in_weight, conv_taps, filter_in, filter_mid, filter_bias, filter_out, out_weight, up_weight, down_weight):
    seq_length = inputs.shape[0]
    blocks = in_weight.shape[1]
    width = inputs.shape[1]
    normed = low(layer_norm(inputs, norm_gain[0], norm_bias[0]))
    streams = low_back(jnp.einsum('rnb,snbo->srno', normed.reshape(seq_length, blocks, -1), in_weight, precision=HIGH).reshape(3, seq_length, -1))
    masked = streams * keep_mask[None, :, None]
    padded = jnp.pad(masked, ((0, 0), (1, 1), (0, 0)))
    short_out = conv_taps[0][:, None, :] * padded[:, :-2] + conv_taps[1][:, None, :] * padded[:, 1:-1] + conv_taps[2][:, None, :] * padded[:, 2:]
    values = short_out[2] * short_out[0] * keep_mask[:, None]
    size_fft = 2 * seq_length
    feats, distance = lag_features(seq_length, size_fft)
    rates = decay_rates(jnp.arange(width, dtype=jnp.int32), width)
    long_filter = filter_values(feats, distance, rates, filter_in, filter_mid, filter_bias, filter_out)
    spec_values = jnp.fft.rfft(values, n=size_fft, axis=0)
    spec_kernel = jnp.fft.rfft(long_filter, axis=1).T
    conv_out = jnp.fft.irfft(spec_values * spec_kernel, n=size_fft, axis=0)[:seq_length]
    gated_in = low(conv_out * short_out[1])
    middle = inputs + low_back(block_product(gated_in, out_weight))
    normed_two = low(layer_norm(middle, norm_gain[1], norm_bias[1]))
    gate_up = low_back(jnp.einsum('rnb,snbo->srno', normed_two.reshape(seq_length, blocks, -1), up_weight, precision=HIGH).reshape(2, seq_length, -1))
    hidden = low(jax.nn.gelu(gate_up[0], approximate=False) * gate_up[1])
    return middle + low_back(block_product(hidden, down_weight))

def reference(tokens, lengths, cotangent, norm_gain, norm_bias, in_weight, conv_taps, filter_in, filter_mid, filter_bias, filter_out, out_weight, up_weight, down_weight):
    params = (norm_gain.astype(jnp.float32), norm_bias.astype(jnp.float32), in_weight.astype(jnp.float32), conv_taps.astype(jnp.float32), filter_in.astype(jnp.float32), filter_mid.astype(jnp.float32), filter_bias.astype(jnp.float32), filter_out.astype(jnp.float32), out_weight.astype(jnp.float32), up_weight.astype(jnp.float32), down_weight.astype(jnp.float32))
    positions = jnp.arange(SEQ, dtype=jnp.int32)

    def one_sequence(running, sequence):
        inputs, length_now, incoming = sequence
        keep_mask = (positions < length_now).astype(jnp.float32)

        def forward(values, *weights):
            return layer(values, keep_mask, *weights)
        result, pullback = jax.vjp(forward, inputs.astype(jnp.float32), *params)
        gradients = pullback(incoming.astype(jnp.float32))
        updated = tuple((total + piece for total, piece in zip(running, gradients[1:])))
        return (updated, (result.astype(jnp.bfloat16), gradients[0]))
    initial = tuple((jnp.zeros(param.shape, jnp.float32) for param in params))
    totals, (outputs, grad_tokens) = lax.scan(one_sequence, initial, (tokens, lengths, cotangent))
    return (outputs, grad_tokens, totals[0], totals[1], totals[2], totals[3], totals[4], totals[5], totals[6], totals[7], totals[8], totals[9], totals[10])
```

```python
import functools
import math

import jax
import jax.numpy as jnp
import numpy as np
from jax import lax
from jax.experimental import pallas as pl
from jax.experimental.pallas import tpu as pltpu
from jax.sharding import PartitionSpec as P

F32 = jnp.float32
BF16 = jnp.bfloat16
EPS = 1e-05
SINE_FREQ = 10.0
GROUP = 3
COLS = 128
HALF_ROWS = 16
FULL_ROWS = 32
FREQ_ROWS = 17
STAT_ROWS = 16
VMEM = pltpu.CompilerParams(vmem_limit_bytes=56 * 1024 * 1024)


def stage_tables():
    k1 = np.arange(FREQ_ROWS)[:, None, None]
    t1 = np.arange(FULL_ROWS)[None, :, None]
    t2 = np.arange(COLS)[None, None, :]
    phase = 2.0 * np.pi * ((k1 * (t1 * COLS + t2)) % 4096) / 4096.0
    both = np.stack([np.cos(phase), -np.sin(phase)], axis=1)
    out = np.zeros((8, FREQ_ROWS, 2, 16, FULL_ROWS, 16), np.float32)
    for a in range(16):
        out[:, :, :, a, :, a] = np.moveaxis(both[..., a::16], -1, 0)
    first = out.reshape(8, FREQ_ROWS * 32, FULL_ROWS * 16)
    theta = 2.0 * np.pi * (np.outer(np.arange(COLS), np.arange(COLS)) % COLS) / COLS
    second = np.block([[np.cos(theta), np.sin(theta)], [-np.sin(theta), np.cos(theta)]])
    return first, second


def lag_table(seq_total):
    lags = np.arange(2 * seq_total)
    scaled = np.where(lags < seq_total, lags, lags - 2 * seq_total) / float(seq_total)
    feats = np.stack(
        [
            scaled,
            np.cos(np.pi * scaled),
            np.sin(np.pi * scaled),
            np.cos(2.0 * np.pi * scaled),
            np.sin(2.0 * np.pi * scaled),
        ],
        axis=1,
    ).astype(np.float32)
    parts, rest = [], feats
    for _ in range(3):
        piece = rest.astype(jnp.bfloat16)
        parts.append(piece.astype(np.float32))
        rest = rest - piece.astype(np.float32)
    table = np.zeros((2 * seq_total, 16), np.float32)
    table[:, :15] = np.concatenate(parts, axis=1)
    return table


def dot(a, b):
    return jnp.dot(a, b, preferred_element_type=F32)


def low_lanes(rows):
    return lax.broadcasted_iota(jnp.int32, (rows, 128), 1) < 64


def tiles(value):
    return [value[:, 128 * i : 128 * (i + 1)] for i in range(value.shape[1] // 128)]


def half_turn(value):
    return pltpu.roll(value, 64, axis=1)


def stacked(value):
    first, second, last = tiles(value)
    low = low_lanes(value.shape[0])
    zero = jnp.zeros_like(last)
    return jnp.concatenate(
        [
            jnp.concatenate([first, jnp.where(low, last, zero)], axis=1),
            jnp.concatenate([second, jnp.where(low, zero, last)], axis=1),
        ],
        axis=0,
    )


def packed(value):
    rows = value.shape[0] // 2
    low = low_lanes(rows)
    last = jnp.where(low, value[:rows, 128:], value[rows:, 128:])
    return jnp.concatenate([value[:rows, :128], value[rows:, :128], last], axis=1)


def pair_sum(value):
    first, second, last = tiles(value)
    low = low_lanes(value.shape[0])
    zero = jnp.zeros_like(last)
    return (
        jnp.sum(first + jnp.where(low, last, zero), axis=1, keepdims=True),
        jnp.sum(second + jnp.where(low, zero, last), axis=1, keepdims=True),
    )


def spread(col_a, col_b, rows):
    wide_a = jnp.broadcast_to(col_a, (rows, 128))
    wide_b = jnp.broadcast_to(col_b, (rows, 128))
    return jnp.concatenate([wide_a, wide_b, jnp.where(low_lanes(rows), wide_a, wide_b)], axis=1)


def to_rows(columns, rows):
    lane = lax.broadcasted_iota(jnp.int32, (rows, 128), 1)
    out = jnp.zeros((rows, 128), F32)
    for at, column in enumerate(columns):
        out = jnp.where(lane == at, jnp.broadcast_to(column, (rows, 128)), out)
    if rows % 128:
        out = jnp.concatenate([out, jnp.zeros((128 - rows, 128), F32)], axis=0)
    return out.T[:8, :rows]


def to_columns(values):
    rows = values.shape[1]
    if rows % 128:
        values = jnp.concatenate([values, jnp.zeros((8, 128 - rows), F32)], axis=1)
    tall = jnp.concatenate([values, jnp.zeros((120, values.shape[1]), F32)], axis=0)
    return tall.T[:rows]


def split_rows(values):
    high = values.astype(BF16).astype(F32)
    return jnp.concatenate([high, values - high], axis=0).astype(BF16)


def join_rows(values):
    wide = values.astype(F32)
    return wide[:8] + wide[8:]


def position_mask(start, rows, count_a, count_b):
    place = start + lax.broadcasted_iota(jnp.int32, (rows, 128), 0)
    keep_a = (place < count_a).astype(F32)
    keep_b = (place < count_b).astype(F32)
    return jnp.concatenate([keep_a, keep_b, jnp.where(low_lanes(rows), keep_a, keep_b)], axis=1)


def sine_pair(angle):
    turns = jnp.floor(angle * (1.0 / math.pi) + 0.5)
    rest = angle - turns * 3.140625
    rest = rest - turns * 9.675025939941406e-4
    rest = rest - turns * 1.5099579909783764e-7
    half = turns * 0.5
    sign = 1.0 - 4.0 * (half - jnp.floor(half))
    square = rest * rest
    sine = square * (-1.0 / 39916800.0) + 1.0 / 362880.0
    sine = sine * square - 1.0 / 5040.0
    sine = sine * square + 1.0 / 120.0
    sine = sine * square - 1.0 / 6.0
    sine = rest + rest * square * sine
    cosine = square * (1.0 / 479001600.0) - 1.0 / 3628800.0
    cosine = cosine * square + 1.0 / 40320.0
    cosine = cosine * square - 1.0 / 720.0
    cosine = cosine * square + 1.0 / 24.0
    cosine = cosine * square - 0.5
    cosine = 1.0 + square * cosine
    return sine * sign, cosine * sign


MILLS = (
    0.11962639,
    0.12079834,
    0.0996376,
    0.12946887,
    -0.05539326,
    0.20820602,
    -0.15827569,
    0.03593167,
)


def normal_parts(value):
    bell = jnp.exp(value * value * -0.5)
    base = 1.0 + 0.3 * jnp.abs(value)
    inv = pl.reciprocal(base, approx=True)
    inv = inv * (2.0 - base * inv)
    tail = inv * MILLS[7] + MILLS[6]
    for coefficient in MILLS[5::-1]:
        tail = tail * inv + coefficient
    tail = tail * inv * bell
    return jnp.where(value >= 0.0, 1.0 - tail, tail), bell * (1.0 / math.sqrt(2.0 * math.pi))


def pack_pair(a, b, block):
    rows = a.shape[0]
    low = low_lanes(rows)
    base = 3 * (block // 2)
    ta = [a[:, 128 * (base + i) : 128 * (base + i + 1)] for i in range(3)]
    tb = [b[:, 128 * (base + i) : 128 * (base + i + 1)] for i in range(3)]
    if block % 2 == 0:
        parts = [ta[0], tb[0], jnp.where(low, ta[1], half_turn(tb[1]))]
    else:
        parts = [
            jnp.where(low, half_turn(ta[1]), half_turn(ta[2])),
            jnp.where(low, half_turn(tb[1]), half_turn(tb[2])),
            jnp.where(low, half_turn(ta[2]), tb[2]),
        ]
    return jnp.concatenate(parts, axis=1)


def unpack_pairs(even, odd):
    low = low_lanes(even.shape[0])
    ea, eb, el = tiles(even)
    oa, ob, ol = tiles(odd)
    a = [ea, jnp.where(low, el, half_turn(oa)), jnp.where(low, half_turn(oa), half_turn(ol))]
    b = [eb, jnp.where(low, half_turn(el), half_turn(ob)), jnp.where(low, half_turn(ob), ol)]
    return jnp.concatenate(a, axis=1), jnp.concatenate(b, axis=1)


def row_stats(value):
    mean = jnp.mean(value, axis=1, keepdims=True)
    centred = value - mean
    variance = jnp.mean(centred * centred, axis=1, keepdims=True)
    return mean, lax.rsqrt(variance + EPS)


def pack_tokens_kernel(x_ref, out_ref):
    rows = x_ref.shape[1]
    a = x_ref[0].astype(F32)
    b = x_ref[1].astype(F32)
    stats = split_rows(to_rows(row_stats(a) + row_stats(b), rows))
    for block in range(4):
        out_ref[block, :rows, :] = pack_pair(a, b, block).astype(BF16)
        out_ref[block, rows:, :rows] = stats


def pack_tokens(tokens):
    count, rows, width = tokens.shape
    return pl.pallas_call(
        pack_tokens_kernel,
        grid=(count // 2,),
        in_specs=[pl.BlockSpec((2, rows, width), lambda i: (i, 0, 0))],
        out_specs=pl.BlockSpec((4, rows + STAT_ROWS, 384), lambda i: (i, 0, 0)),
        out_shape=jax.ShapeDtypeStruct((2 * count, rows + STAT_ROWS, 384), BF16),
        compiler_params=VMEM,
        name="pack_tokens",
    )(tokens)


def pack_cotangent_kernel(x_ref, after_ref, out_ref):
    a = x_ref[0].astype(F32)
    b = x_ref[1].astype(F32)
    for block in range(4):
        out_ref[block] = pack_pair(a, b, block).astype(BF16)


def pack_cotangent(cotangent, after):
    count, rows, width = cotangent.shape
    return pl.pallas_call(
        pack_cotangent_kernel,
        grid=(count // 2,),
        in_specs=[
            pl.BlockSpec((2, rows, width), lambda i: (i, 0, 0)),
            pl.BlockSpec(memory_space=pl.ANY),
        ],
        out_specs=pl.BlockSpec((4, rows, 384), lambda i: (i, 0, 0)),
        out_shape=jax.ShapeDtypeStruct((2 * count, rows, 384), BF16),
        compiler_params=VMEM,
        name="pack_cotangent",
    )(cotangent, after)


def transform_first(table_ref, data_ref, spec_ref):
    count, _, lanes = data_ref.shape

    def one(j, carry):
        start = pl.ds(pl.multiple_of(16 * j, 16), 16)
        block = data_ref[:, start, :].reshape(count * 16, lanes)
        part = dot(table_ref[j], block).astype(BF16)
        spec_ref[:, start, :] = part.reshape(2 * FREQ_ROWS, 16, lanes)
        return carry

    lax.fori_loop(0, 8, one, 0)


def frequency_weight(k1):
    edge = jnp.logical_or(k1 == 0, k1 == FREQ_ROWS - 1)
    return jnp.where(edge, 1.0 / 4096.0, 2.0 / 4096.0).astype(F32)


def make_filter_kernel(
    feat_ref,
    fin_ref,
    bias_ref,
    mid_ref,
    fout_ref,
    rate_ref,
    table_ref,
    second_ref,
    s1_ref,
    c1_ref,
    s2_ref,
    c2_ref,
    spec_ref,
    taps_ref,
    work_ref,
):
    step_rows = 256
    total = feat_ref.shape[0]

    def one(i, carry):
        rows = pl.ds(pl.multiple_of(i * step_rows, step_rows), step_rows)
        inner = dot(feat_ref[rows, :], fin_ref[...]) + bias_ref[0:1, :]
        s1, c1 = sine_pair(SINE_FREQ * inner)
        s1_ref[rows, :] = s1.astype(BF16)
        c1_ref[rows, :] = c1.astype(BF16)
        p1 = s1.astype(BF16)
        r1 = s1 - p1.astype(F32)
        p2 = r1.astype(BF16)
        p3 = (r1 - p2.astype(F32)).astype(BF16)
        outer = dot(jnp.concatenate([p1, p2, p3], axis=1), mid_ref[...]) + bias_ref[1:2, :]
        s2, c2 = sine_pair(SINE_FREQ * outer)
        s2_ref[rows, :] = s2.astype(BF16)
        c2_ref[rows, :] = c2.astype(BF16)
        q1 = s2.astype(BF16)
        q2 = (s2 - q1.astype(F32)).astype(BF16)
        raw = dot(jnp.concatenate([q1, q2], axis=1), fout_ref[...])
        lag = i * step_rows + lax.broadcasted_iota(jnp.int32, (step_rows, 256), 0)
        signed = jnp.where(lag < total // 2, lag, total - lag)
        distance = signed.astype(F32) * (2.0 / total)
        kernel = raw * jnp.exp(-distance * rate_ref[...])
        taps_ref[pl.ds(2 * i, 2), :, :] = kernel.astype(BF16).reshape(2, COLS, 256)
        return carry

    lax.fori_loop(0, total // step_rows, one, 0)
    transform_first(table_ref, taps_ref, work_ref)

    def second(k1, carry):
        part = work_ref[pl.ds(2 * k1, 2), :, :].reshape(256, 256)
        spec_ref[k1] = dot(second_ref[...], part) * frequency_weight(k1)
        return carry

    lax.fori_loop(0, FREQ_ROWS, second, 0)


def make_filter(feats, fin, bias, mid, fout, rate, table, second):
    total = feats.shape[0]
    hidden = jax.ShapeDtypeStruct((total, 128), BF16)
    return pl.pallas_call(
        make_filter_kernel,
        out_shape=(hidden,) * 4 + (jax.ShapeDtypeStruct((FREQ_ROWS, 256, 256), F32),),
        scratch_shapes=[
            pltpu.VMEM((FULL_ROWS, COLS, 256), BF16),
            pltpu.VMEM((2 * FREQ_ROWS, COLS, 256), BF16),
        ],
        compiler_params=VMEM,
        name="make_filter",
    )(feats, fin, bias, mid, fout, rate, table, second)


def normed_pair(payload, rows, scales, offsets):
    value = payload[:rows].astype(F32)
    stats = to_columns(join_rows(payload[rows:, :rows]))
    mean = spread(stats[:, 0:1], stats[:, 2:3], rows)
    scale = spread(stats[:, 1:2], stats[:, 3:4], rows)
    unit = (value - mean) * scale
    return unit, scale, unit * scales + offsets


def mixer_in_kernel(
    counts_ref, x_ref, scales_ref, offsets_ref, w_ref, taps_ref, masked_ref, short_ref, values_ref, ring_ref, now_ref
):
    rows = values_ref.shape[0]
    step = pl.program_id(0)
    last = pl.num_programs(0) - 1
    count_a, count_b = counts_ref[0], counts_ref[1]

    @pl.when(step == 0)
    def _():
        ring_ref[...] = jnp.zeros_like(ring_ref)

    @pl.when(step < last)
    def _():
        _, _, normed = normed_pair(x_ref[0], rows, scales_ref[...], offsets_ref[...])
        out = dot(stacked(normed).astype(BF16), w_ref[...])
        keep = position_mask(step * rows, rows, count_a, count_b)
        for s in range(3):
            now_ref[s] = packed(out[:, 256 * s : 256 * (s + 1)]) * keep

    @pl.when(step == last)
    def _():
        now_ref[...] = jnp.zeros_like(now_ref)

    for s in range(3):
        ring_ref[s, rows + 8 :, :] = now_ref[s, :8, :]

    @pl.when(step > 0)
    def _():
        shorts = []
        for s in range(3):
            window = ring_ref[s]
            before = window[7 : 7 + rows]
            here = window[8 : 8 + rows]
            after = window[9 : 9 + rows]
            masked_ref[s] = here.astype(BF16)
            short = (
                taps_ref[s : s + 1, :] * before
                + taps_ref[3 + s : 4 + s, :] * here
                + taps_ref[6 + s : 7 + s, :] * after
            )
            short_ref[s] = short.astype(BF16)
            shorts.append(short)
        keep = position_mask((step - 1) * rows, rows, count_a, count_b)
        values_ref[...] = (shorts[2] * shorts[0] * keep).astype(BF16)

    ring_ref[:, 0:8, :] = ring_ref[:, rows : rows + 8, :]
    ring_ref[:, 8 : 8 + rows, :] = now_ref[...]


def lagged(step):
    return jnp.maximum(step - 1, 0)


def mixer_in(counts, payload, scales, offsets, weight, taps, total):
    chunks, tall, _ = payload.shape
    rows = tall - STAT_ROWS
    whole = lambda shape: pl.BlockSpec(shape, lambda i: (0,) * len(shape))
    return pl.pallas_call(
        mixer_in_kernel,
        grid=(chunks + 1,),
        in_specs=[
            pl.BlockSpec(memory_space=pltpu.SMEM),
            pl.BlockSpec((1, tall, 384), lambda i: (jnp.minimum(i, chunks - 1), 0, 0)),
            whole((1, 384)),
            whole((1, 384)),
            whole((256, 768)),
            whole((9, 384)),
        ],
        out_specs=[
            pl.BlockSpec((3, rows, 384), lambda i: (0, lagged(i), 0)),
            pl.BlockSpec((3, rows, 384), lambda i: (0, lagged(i), 0)),
            pl.BlockSpec((rows, 384), lambda i: (lagged(i), 0)),
        ],
        out_shape=[
            jax.ShapeDtypeStruct((3, total, 384), BF16),
            jax.ShapeDtypeStruct((3, total, 384), BF16),
            jax.ShapeDtypeStruct((total, 384), BF16),
        ],
        scratch_shapes=[
            pltpu.VMEM((3, rows + 16, 384), F32),
            pltpu.VMEM((3, rows, 384), F32),
        ],
        compiler_params=VMEM,
        name="mixer_in",
    )(counts, payload, scales, offsets, weight, taps)


def filter_lanes(block):
    return jnp.concatenate([block[:, :128], block], axis=1)


def long_conv_kernel(
    values_ref, gate_ref, filter_ref, first_ref, second_ref, third_ref, fourth_ref, spec_ref, conv_ref, gated_ref, work_ref
):
    transform_first(first_ref, values_ref, work_ref)

    def middle(k1, carry):
        part = work_ref[pl.ds(2 * k1, 2), :, :].reshape(256, 384)
        spec = dot(second_ref[...], part)
        spec_ref[k1] = spec.astype(BF16)
        re, im = spec[:128], spec[128:]
        block = filter_ref[k1]
        fre, fim = filter_lanes(block[:128]), filter_lanes(block[128:])
        prod = jnp.concatenate([re * fre - im * fim, re * fim + im * fre], axis=0).astype(BF16)
        work_ref[pl.ds(2 * k1, 2), :, :] = dot(third_ref[...], prod).astype(BF16).reshape(2, COLS, 384)
        return carry

    lax.fori_loop(0, FREQ_ROWS, middle, 0)

    def last(j, carry):
        start = pl.ds(pl.multiple_of(16 * j, 16), 16)
        part = work_ref[:, start, :].reshape(FREQ_ROWS * 32, 384)
        conv = dot(fourth_ref[j], part)
        conv_ref[:, start, :] = conv.astype(BF16).reshape(HALF_ROWS, 16, 384)
        gate = gate_ref[:, start, :].reshape(256, 384).astype(F32)
        gated_ref[:, start, :] = (conv * gate).astype(BF16).reshape(HALF_ROWS, 16, 384)
        return carry

    lax.fori_loop(0, 8, last, 0)


def full_spec(shape):
    return pl.BlockSpec(shape, lambda i: (0,) * len(shape))


def long_conv(values, short, spectrum, tables):
    first, second, third, fourth = tables
    seq = jax.ShapeDtypeStruct((HALF_ROWS, COLS, 384), BF16)
    cube = (HALF_ROWS, COLS, 384)
    return pl.pallas_call(
        long_conv_kernel,
        grid=(1,),
        in_specs=[
            full_spec(cube),
            pl.BlockSpec((None,) + cube, lambda i: (1, 0, 0, 0)),
            full_spec((FREQ_ROWS, 256, 256)),
            full_spec((8, FREQ_ROWS * 32, 256)),
            full_spec((256, 256)),
            full_spec((256, 256)),
            full_spec((8, 256, FREQ_ROWS * 32)),
        ],
        out_specs=[full_spec((FREQ_ROWS, 256, 384)), full_spec(cube), full_spec(cube)],
        out_shape=[jax.ShapeDtypeStruct((FREQ_ROWS, 256, 384), BF16), seq, seq],
        scratch_shapes=[pltpu.VMEM((2 * FREQ_ROWS, COLS, 384), BF16)],
        compiler_params=VMEM,
        name="long_conv",
    )(
        values.reshape(cube),
        short.reshape((3,) + cube),
        spectrum,
        first,
        second,
        third,
        fourth,
    )


def mixer_out_kernel(x_ref, gated_ref, w_ref, middle_ref, stats_ref):
    rows = gated_ref.shape[0]
    out = packed(dot(stacked(gated_ref[...]), w_ref[...]))
    middle = x_ref[0, :rows, :].astype(F32) + out
    middle_ref[...] = middle
    sum_a, sum_b = pair_sum(middle)
    mean_a, mean_b = sum_a * (1.0 / 192.0), sum_b * (1.0 / 192.0)
    centred = middle - spread(mean_a, mean_b, rows)
    square_a, square_b = pair_sum(centred * centred)
    stats_ref[0] = to_rows((mean_a, square_a, mean_b, square_b), rows)


def mixer_out(payload, gated, weight):
    chunks, tall, _ = payload.shape
    rows = tall - STAT_ROWS
    return pl.pallas_call(
        mixer_out_kernel,
        grid=(chunks,),
        in_specs=[
            pl.BlockSpec((1, tall, 384), lambda i: (i, 0, 0)),
            pl.BlockSpec((rows, 384), lambda i: (i, 0)),
            full_spec((256, 256)),
        ],
        out_specs=[
            pl.BlockSpec((rows, 384), lambda i: (i, 0)),
            pl.BlockSpec((1, 8, rows), lambda i: (i, 0, 0)),
        ],
        out_shape=[
            jax.ShapeDtypeStruct((chunks * rows, 384), F32),
            jax.ShapeDtypeStruct((chunks, 8, rows), F32),
        ],
        compiler_params=VMEM,
        name="mixer_out",
    )(payload, gated, weight)


def column_sums(value):
    return jnp.sum(value.reshape(value.shape[0] // 8, 8, value.shape[1]), axis=0)


def fold_rows(value):
    return jnp.concatenate([value[:128], value[128:192] + value[192:256]], axis=0)


def fold_lanes(value):
    last = value[:, 128:]
    summed = jnp.where(low_lanes(value.shape[0]), last + half_turn(last), jnp.zeros_like(last))
    return jnp.concatenate([value[:, :128], summed], axis=1)


def feed_forward_kernel(
    middle_ref,
    cot_ref,
    s0_ref,
    s1_ref,
    s2_ref,
    s3_ref,
    scales_ref,
    offsets_ref,
    up_ref,
    upt_ref,
    down_ref,
    downt_ref,
    out_ref,
    q_ref,
    sums_ref,
    norm_ref,
    gup_ref,
    gdown_ref,
    small_ref,
    up_acc,
    down_acc,
):
    rows = middle_ref.shape[0]
    step = pl.program_id(0)

    @pl.when(step == 0)
    def _():
        up_acc[...] = jnp.zeros_like(up_acc)
        down_acc[...] = jnp.zeros_like(down_acc)
        small_ref[...] = jnp.zeros_like(small_ref)

    parts = [ref[0] for ref in (s0_ref, s1_ref, s2_ref, s3_ref)]
    mean = (parts[0] + parts[1] + parts[2] + parts[3]) * 0.25
    spread_sum = jnp.zeros_like(mean)
    for part in parts:
        gap = part - mean
        spread_sum += 192.0 * gap * gap
    squares = parts[0] + parts[1] + parts[2] + parts[3]
    scale_a = lax.rsqrt((squares[1:2] + spread_sum[0:1]) * (1.0 / 768.0) + EPS)
    scale_b = lax.rsqrt((squares[3:4] + spread_sum[2:3]) * (1.0 / 768.0) + EPS)
    norm = jnp.concatenate([mean[0:1], scale_a, mean[2:3], scale_b, jnp.zeros((4, rows), F32)], axis=0)
    norm_ref[0] = norm
    columns = to_columns(norm)
    middle = middle_ref[...]
    unit = (middle - spread(columns[:, 0:1], columns[:, 2:3], rows)) * spread(columns[:, 1:2], columns[:, 3:4], rows)
    normed = stacked(unit * scales_ref[...] + offsets_ref[...]).astype(BF16)
    cot = stacked(cot_ref[0])
    normed_t = normed.T
    cot_t = cot.T
    down = jnp.zeros((2 * rows, 256), F32)
    back = jnp.zeros((2 * rows, 256), F32)
    width = 256
    for f in range(768 // width):
        at = slice(width * f, width * (f + 1))
        at_up = slice(768 + width * f, 768 + width * (f + 1))
        gate = dot(normed, up_ref[:, at])
        upper = dot(normed, up_ref[:, at_up])
        grad_hidden = dot(cot, downt_ref[:, at])
        cdf, density = normal_parts(gate)
        active = gate * cdf
        hidden = (active * upper).astype(BF16)
        grad_gate = (grad_hidden * upper * (cdf + gate * density)).astype(BF16)
        grad_upper = (grad_hidden * active).astype(BF16)
        down += dot(hidden, down_ref[at, :])
        back += dot(grad_gate, upt_ref[at, :]) + dot(grad_upper, upt_ref[at_up, :])
        up_acc[:, at] += fold_rows(dot(normed_t, grad_gate))
        up_acc[:, at_up] += fold_rows(dot(normed_t, grad_upper))
        down_acc[:, at] += dot(cot_t, hidden)
    out_ref[0] = (middle + packed(down)).astype(BF16)
    grad = packed(back)
    q = grad * scales_ref[...]
    q_ref[...] = q
    sums_ref[0] = to_rows(pair_sum(q) + pair_sum(q * unit), rows)
    small_ref[0:8, :] += column_sums(grad * unit)
    small_ref[8:16, :] += column_sums(grad)

    @pl.when(step == pl.num_programs(0) - 1)
    def _():
        gup_ref[...] = up_acc[...].astype(BF16)
        gdown_ref[...] = fold_lanes(down_acc[...].T).astype(BF16)


def feed_forward(middle, cot, stats, scales, offsets, up, upt, down, downt):
    chunks, rows, _ = cot.shape
    total = chunks * rows
    stat_spec = pl.BlockSpec((1, 8, rows), lambda i: (i, 0, 0))
    rows_spec = pl.BlockSpec((rows, 384), lambda i: (i, 0))
    chunk_spec = pl.BlockSpec((1, rows, 384), lambda i: (i, 0, 0))
    stat_shape = jax.ShapeDtypeStruct((chunks, 8, rows), F32)
    return pl.pallas_call(
        feed_forward_kernel,
        grid=(chunks,),
        in_specs=[rows_spec, chunk_spec]
        + [stat_spec] * 4
        + [full_spec(a.shape) for a in (scales, offsets, up, upt, down, downt)],
        out_specs=[
            chunk_spec,
            rows_spec,
            stat_spec,
            stat_spec,
            full_spec((192, 1536)),
            full_spec((768, 256)),
            full_spec((16, 384)),
        ],
        out_shape=[
            jax.ShapeDtypeStruct((chunks, rows, 384), BF16),
            jax.ShapeDtypeStruct((total, 384), F32),
            stat_shape,
            stat_shape,
            jax.ShapeDtypeStruct((192, 1536), BF16),
            jax.ShapeDtypeStruct((768, 256), BF16),
            jax.ShapeDtypeStruct((16, 384), F32),
        ],
        scratch_shapes=[pltpu.VMEM((192, 1536), F32), pltpu.VMEM((256, 768), F32)],
        compiler_params=VMEM,
        name="feed_forward",
    )(middle, cot, *stats, scales, offsets, up, upt, down, downt)


def gate_back_kernel(
    q_ref,
    middle_ref,
    cot_ref,
    norm_ref,
    s0_ref,
    s1_ref,
    s2_ref,
    s3_ref,
    gated_ref,
    conv_ref,
    short_ref,
    wt_ref,
    grad_ref,
    grad_conv_ref,
    grad_short_ref,
    gout_ref,
    out_acc,
):
    rows = q_ref.shape[0]
    step = pl.program_id(0)

    @pl.when(step == 0)
    def _():
        out_acc[...] = jnp.zeros_like(out_acc)

    sums = (s0_ref[0] + s1_ref[0] + s2_ref[0] + s3_ref[0]) * (1.0 / 768.0)
    columns = to_columns(sums)
    norm = to_columns(norm_ref[0])
    scale = spread(norm[:, 1:2], norm[:, 3:4], rows)
    unit = (middle_ref[...] - spread(norm[:, 0:1], norm[:, 2:3], rows)) * scale
    mean_q = spread(columns[:, 0:1], columns[:, 1:2], rows)
    mean_qh = spread(columns[:, 2:3], columns[:, 3:4], rows)
    grad = cot_ref[0].astype(F32) + scale * (q_ref[...] - mean_q - unit * mean_qh)
    grad_ref[...] = grad
    branch = stacked(grad).astype(BF16)
    out_acc[...] += fold_rows(dot(stacked(gated_ref[...]).T, branch))
    grad_gated = packed(dot(branch, wt_ref[...]))
    grad_conv_ref[...] = (grad_gated * short_ref[0].astype(F32)).astype(BF16)
    grad_short_ref[...] = (grad_gated * conv_ref[...].astype(F32)).astype(BF16)

    @pl.when(step == pl.num_programs(0) - 1)
    def _():
        gout_ref[...] = fold_lanes(out_acc[...]).astype(BF16)


def gate_back(q, middle, cot, norm, sums, gated, conv, short, wt):
    chunks, rows, _ = cot.shape
    total = chunks * rows
    stat_spec = pl.BlockSpec((1, 8, rows), lambda i: (i, 0, 0))
    rows_spec = pl.BlockSpec((rows, 384), lambda i: (i, 0))
    return pl.pallas_call(
        gate_back_kernel,
        grid=(chunks,),
        in_specs=[
            rows_spec,
            rows_spec,
            pl.BlockSpec((1, rows, 384), lambda i: (i, 0, 0)),
            stat_spec,
            stat_spec,
            stat_spec,
            stat_spec,
            stat_spec,
            rows_spec,
            rows_spec,
            pl.BlockSpec((1, rows, 384), lambda i: (1, i, 0)),
            full_spec((256, 256)),
        ],
        out_specs=[rows_spec, rows_spec, rows_spec, full_spec((192, 256))],
        out_shape=[
            jax.ShapeDtypeStruct((total, 384), F32),
            jax.ShapeDtypeStruct((total, 384), BF16),
            jax.ShapeDtypeStruct((total, 384), BF16),
            jax.ShapeDtypeStruct((192, 256), BF16),
        ],
        scratch_shapes=[pltpu.VMEM((192, 256), F32)],
        compiler_params=VMEM,
        name="gate_back",
    )(q, middle, cot, norm, *sums, gated, conv, short, wt)


def conv_back_kernel(
    grad_ref, spec_ref, filter_ref, first_ref, second_ref, third_ref, fourth_ref, after_ref, out_ref, cross_ref, work_ref
):
    transform_first(first_ref, grad_ref, work_ref)

    def middle(k1, carry):
        part = work_ref[pl.ds(2 * k1, 2), :, :].reshape(256, 384)
        grad = dot(second_ref[...], part)
        re, im = grad[:128], grad[128:]
        spec = spec_ref[k1].astype(F32)
        vre, vim = spec[:128], spec[128:]
        cre = re * vre + im * vim
        cim = im * vre - re * vim
        weight = frequency_weight(k1)
        fold = lambda v: jnp.concatenate([v[:, :128] + v[:, 128:256], v[:, 256:]], axis=1)
        cross_ref[k1] = (jnp.concatenate([fold(cre), fold(cim)], axis=0) * weight).astype(BF16)
        block = filter_ref[k1]
        fre, fim = filter_lanes(block[:128]), filter_lanes(block[128:])
        prod = jnp.concatenate([re * fre + im * fim, im * fre - re * fim], axis=0).astype(BF16)
        work_ref[pl.ds(2 * k1, 2), :, :] = dot(third_ref[...], prod).astype(BF16).reshape(2, COLS, 384)
        return carry

    lax.fori_loop(0, FREQ_ROWS, middle, 0)

    def last(j, carry):
        start = pl.ds(pl.multiple_of(16 * j, 16), 16)
        part = work_ref[:, start, :].reshape(FREQ_ROWS * 32, 384)
        out_ref[:, start, :] = dot(fourth_ref[j], part).reshape(HALF_ROWS, 16, 384)
        return carry

    lax.fori_loop(0, 8, last, 0)


def conv_back(grad, spec, spectrum, tables, after):
    first, second, third, fourth = tables
    cube = (HALF_ROWS, COLS, 384)
    return pl.pallas_call(
        conv_back_kernel,
        grid=(1,),
        in_specs=[
            full_spec(cube),
            full_spec((FREQ_ROWS, 256, 384)),
            full_spec((FREQ_ROWS, 256, 256)),
            full_spec((8, FREQ_ROWS * 32, 256)),
            full_spec((256, 256)),
            full_spec((256, 256)),
            full_spec((8, 256, FREQ_ROWS * 32)),
            pl.BlockSpec(memory_space=pl.ANY),
        ],
        out_specs=[full_spec(cube), full_spec((FREQ_ROWS, 256, 256))],
        out_shape=[
            jax.ShapeDtypeStruct(cube, F32),
            jax.ShapeDtypeStruct((FREQ_ROWS, 256, 256), BF16),
        ],
        scratch_shapes=[pltpu.VMEM((2 * FREQ_ROWS, COLS, 384), BF16)],
        compiler_params=VMEM,
        name="conv_back",
    )(grad.reshape(cube), spec, spectrum, first, second, third, fourth, after)


def mixer_back_kernel(
    counts_ref,
    grad_values_ref,
    grad_one_ref,
    short_a_ref,
    short_b_ref,
    masked_ref,
    x_ref,
    grad_ref,
    scales_ref,
    offsets_ref,
    taps_ref,
    wt_ref,
    after_ref,
    out_ref,
    gin_ref,
    small_ref,
    in_acc,
    ring_ref,
    now_ref,
):
    rows = grad_ref.shape[0]
    step = pl.program_id(0)
    last = pl.num_programs(0) - 1
    count_a, count_b = counts_ref[0], counts_ref[1]

    @pl.when(step == 0)
    def _():
        ring_ref[...] = jnp.zeros_like(ring_ref)
        in_acc[...] = jnp.zeros_like(in_acc)
        small_ref[...] = jnp.zeros_like(small_ref)

    @pl.when(step < last)
    def _():
        keep = position_mask(step * rows, rows, count_a, count_b)
        grad_values = grad_values_ref[...] * keep
        now_ref[0] = grad_values * short_b_ref[0].astype(F32)
        now_ref[1] = grad_one_ref[...].astype(F32)
        now_ref[2] = grad_values * short_a_ref[0].astype(F32)

    @pl.when(step == last)
    def _():
        now_ref[...] = jnp.zeros_like(now_ref)

    for s in range(3):
        ring_ref[s, rows + 8 :, :] = now_ref[s, :8, :]

    @pl.when(step > 0)
    def _():
        keep = position_mask((step - 1) * rows, rows, count_a, count_b)
        grads = []
        for s in range(3):
            window = ring_ref[s]
            shifted = (window[9 : 9 + rows], window[8 : 8 + rows], window[7 : 7 + rows])
            masked = masked_ref[s].astype(F32)
            total = jnp.zeros((rows, 384), F32)
            for j in range(3):
                total += taps_ref[3 * j + s : 3 * j + s + 1, :] * shifted[j]
                at = 16 + 8 * (3 * j + s)
                small_ref[at : at + 8, :] += column_sums(shifted[j] * masked)
            grads.append(stacked(total * keep).astype(BF16))
        flat = jnp.concatenate(grads, axis=1)
        unit, scale, normed = normed_pair(x_ref[0], rows, scales_ref[...], offsets_ref[...])
        in_acc[...] += fold_rows(dot(stacked(normed).astype(BF16).T, flat))
        grad_normed = packed(dot(flat, wt_ref[...]))
        small_ref[0:8, :] += column_sums(grad_normed * unit)
        small_ref[8:16, :] += column_sums(grad_normed)
        q = grad_normed * scales_ref[...]
        out_ref[0, :rows, :] = (grad_ref[...] + scale * q).astype(BF16)
        out_ref[0, rows:, :rows] = split_rows(to_rows(pair_sum(q) + pair_sum(q * unit), rows))

    ring_ref[:, 0:8, :] = ring_ref[:, rows : rows + 8, :]
    ring_ref[:, 8 : 8 + rows, :] = now_ref[...]

    @pl.when(step == last)
    def _():
        grads = in_acc[...]
        for s in range(3):
            gin_ref[:, 256 * s : 256 * (s + 1)] = fold_lanes(grads[:, 256 * s : 256 * (s + 1)]).astype(BF16)


def mixer_back(counts, grad_values, grad_one, short, masked, payload, grad, scales, offsets, taps, wt, after):
    chunks, tall, _ = payload.shape
    rows = tall - STAT_ROWS
    ahead = lambda i: jnp.minimum(i, chunks - 1)
    return pl.pallas_call(
        mixer_back_kernel,
        grid=(chunks + 1,),
        in_specs=[
            pl.BlockSpec(memory_space=pltpu.SMEM),
            pl.BlockSpec((rows, 384), lambda i: (ahead(i), 0)),
            pl.BlockSpec((rows, 384), lambda i: (ahead(i), 0)),
            pl.BlockSpec((1, rows, 384), lambda i: (0, ahead(i), 0)),
            pl.BlockSpec((1, rows, 384), lambda i: (2, ahead(i), 0)),
            pl.BlockSpec((3, rows, 384), lambda i: (0, lagged(i), 0)),
            pl.BlockSpec((1, tall, 384), lambda i: (lagged(i), 0, 0)),
            pl.BlockSpec((rows, 384), lambda i: (lagged(i), 0)),
            full_spec((1, 384)),
            full_spec((1, 384)),
            full_spec((9, 384)),
            full_spec((768, 256)),
            pl.BlockSpec(memory_space=pl.ANY),
        ],
        out_specs=[
            pl.BlockSpec((1, tall, 384), lambda i: (lagged(i), 0, 0)),
            full_spec((192, 768)),
            full_spec((88, 384)),
        ],
        out_shape=[
            jax.ShapeDtypeStruct((chunks, tall, 384), BF16),
            jax.ShapeDtypeStruct((192, 768), BF16),
            jax.ShapeDtypeStruct((88, 384), F32),
        ],
        scratch_shapes=[
            pltpu.VMEM((192, 768), F32),
            pltpu.VMEM((3, rows + 16, 384), F32),
            pltpu.VMEM((3, rows, 384), F32),
        ],
        compiler_params=VMEM,
        name="mixer_back",
    )(counts, grad_values, grad_one, short, short, masked, payload, grad, scales, offsets, taps, wt, after)


def filter_back_kernel(
    cross_ref,
    s1_ref,
    c1_ref,
    s2_ref,
    c2_ref,
    feat_ref,
    midt_ref,
    foutt_ref,
    rate_ref,
    third_ref,
    fourth_ref,
    after_ref,
    gfin_ref,
    gmid_ref,
    gfout_ref,
    gbias_ref,
    work_ref,
    taps_ref,
):
    total = feat_ref.shape[0]
    step_rows = 256

    def second(k1, carry):
        work_ref[pl.ds(2 * k1, 2), :, :] = dot(third_ref[...], cross_ref[k1]).astype(BF16).reshape(2, COLS, 256)
        return carry

    lax.fori_loop(0, FREQ_ROWS, second, 0)

    def last(j, carry):
        start = pl.ds(pl.multiple_of(16 * j, 16), 16)
        part = work_ref[:, start, :].reshape(FREQ_ROWS * 32, 256)
        taps_ref[:, start, :] = dot(fourth_ref[j], part).reshape(FULL_ROWS, 16, 256)
        return carry

    lax.fori_loop(0, 8, last, 0)
    gfin_ref[...] = jnp.zeros_like(gfin_ref)
    gmid_ref[...] = jnp.zeros_like(gmid_ref)
    gfout_ref[...] = jnp.zeros_like(gfout_ref)
    gbias_ref[...] = jnp.zeros_like(gbias_ref)

    def one(i, carry):
        rows = pl.ds(pl.multiple_of(i * step_rows, step_rows), step_rows)
        lag = i * step_rows + lax.broadcasted_iota(jnp.int32, (step_rows, 256), 0)
        signed = jnp.where(lag < total // 2, lag, total - lag)
        distance = signed.astype(F32) * (2.0 / total)
        grad = taps_ref[pl.ds(2 * i, 2), :, :].reshape(step_rows, 256) * jnp.exp(-distance * rate_ref[...])
        grad = grad.astype(BF16)
        gfout_ref[...] += dot(s2_ref[rows, :].T, grad)
        grad_second = dot(grad, foutt_ref[...]) * (SINE_FREQ * c2_ref[rows, :].astype(F32))
        gbias_ref[8:16, :] += column_sums(grad_second)
        grad_second = grad_second.astype(BF16)
        gmid_ref[...] += dot(s1_ref[rows, :].T, grad_second)
        grad_first = dot(grad_second, midt_ref[...]) * (SINE_FREQ * c1_ref[rows, :].astype(F32))
        gbias_ref[0:8, :] += column_sums(grad_first)
        gfin_ref[...] += dot(feat_ref[rows, :].T, grad_first.astype(BF16))
        return carry

    lax.fori_loop(0, total // step_rows, one, 0)


def filter_back(cross, hidden, feats, midt, foutt, rate, third, fourth, after):
    vmem = pl.BlockSpec(memory_space=pltpu.VMEM)
    return pl.pallas_call(
        filter_back_kernel,
        in_specs=[vmem] * 11 + [pl.BlockSpec(memory_space=pl.ANY)],
        out_shape=[
            jax.ShapeDtypeStruct((16, 128), F32),
            jax.ShapeDtypeStruct((128, 128), F32),
            jax.ShapeDtypeStruct((128, 256), F32),
            jax.ShapeDtypeStruct((16, 128), F32),
        ],
        scratch_shapes=[
            pltpu.VMEM((2 * FREQ_ROWS, COLS, 256), BF16),
            pltpu.VMEM((FULL_ROWS, COLS, 256), F32),
        ],
        compiler_params=VMEM,
        name="filter_back",
    )(cross, *hidden, feats, midt, foutt, rate, third, fourth, after)


def unpack_out_kernel(x_ref, out_ref):
    for even in (0, 2):
        a, b = unpack_pairs(x_ref[even].astype(F32), x_ref[even + 1].astype(F32))
        out_ref[0, :, 192 * even : 192 * even + 384] = a.astype(BF16)
        out_ref[1, :, 192 * even : 192 * even + 384] = b.astype(BF16)


def unpack_out(value):
    chunks, rows, _ = value.shape
    return pl.pallas_call(
        unpack_out_kernel,
        grid=(chunks // 4,),
        in_specs=[pl.BlockSpec((4, rows, 384), lambda i: (i, 0, 0))],
        out_specs=pl.BlockSpec((2, rows, 768), lambda i: (i, 0, 0)),
        out_shape=jax.ShapeDtypeStruct((chunks // 2, rows, 768), BF16),
        compiler_params=VMEM,
        name="unpack_out",
    )(value)


def unpack_grad_kernel(x_ref, tokens_ref, out_ref):
    rows = tokens_ref.shape[1]
    sums = jnp.zeros((8, rows), F32)
    for block in range(4):
        sums += join_rows(x_ref[block, rows:, :rows])
    columns = to_columns(sums) * (1.0 / 768.0)
    wide = ([], [])
    for even in (0, 2):
        a, b = unpack_pairs(x_ref[even, :rows].astype(F32), x_ref[even + 1, :rows].astype(F32))
        wide[0].append(a)
        wide[1].append(b)
    for which in range(2):
        token = tokens_ref[which].astype(F32)
        mean, scale = row_stats(token)
        unit = (token - mean) * scale
        grad = jnp.concatenate(wide[which], axis=1)
        mean_q = columns[:, which : which + 1]
        mean_qh = columns[:, 2 + which : 3 + which]
        out_ref[which] = grad - scale * (mean_q + unit * mean_qh)


def unpack_grad(value, tokens):
    chunks, tall, _ = value.shape
    rows = tall - STAT_ROWS
    return pl.pallas_call(
        unpack_grad_kernel,
        grid=(chunks // 4,),
        in_specs=[
            pl.BlockSpec((4, tall, 384), lambda i: (i, 0, 0)),
            pl.BlockSpec((2, rows, 768), lambda i: (i, 0, 0)),
        ],
        out_specs=pl.BlockSpec((2, rows, 768), lambda i: (i, 0, 0)),
        out_shape=jax.ShapeDtypeStruct((chunks // 2, rows, 768), F32),
        compiler_params=VMEM,
        name="unpack_grad",
    )(value, tokens)


def doubled(value, axis):
    return jnp.concatenate([value, lax.slice_in_dim(value, 128, 192, axis=axis)], axis=axis)


def pair_lanes(value):
    head, tail = value[:, :128], value[:, 128:]
    return jnp.concatenate([head, head, tail, tail], axis=1)


def unpair_lanes(value):
    return jnp.concatenate([value[:, :128] + value[:, 128:256], value[:, 256:320] + value[:, 320:]], axis=1)


def at_block(value, block, axis):
    return lax.dynamic_index_in_dim(value, block, axis=axis, keepdims=False)


def per_device(
    tokens,
    lengths,
    cotangent,
    norm_gain,
    norm_bias,
    in_weight,
    conv_taps,
    filter_in,
    filter_mid,
    filter_bias,
    filter_out,
    out_weight,
    up_weight,
    down_weight,
):
    count, rows, features = tokens.shape
    blocks = in_weight.shape[1]
    data_size = lax.axis_size("dp")
    seq_size = lax.axis_size("seq")
    total = rows * seq_size
    groups = seq_size // blocks
    place = lax.axis_index("seq")
    block = place % blocks
    group = place // blocks
    width = features // blocks
    data_at = lax.axis_index("dp")

    def exchange(value):
        return lax.all_to_all(value, "seq", 0, 0, tiled=True)

    def shared(value):
        out = [value]
        for r in range(1, blocks):
            out.append(lax.ppermute(value, "seq", [(i, i ^ r) for i in range(seq_size)]))
        return out

    def gathered(value):
        out = [value]
        for r in range(1, data_size):
            out.append(lax.ppermute(value, "dp", [(i, i ^ r) for i in range(data_size)]))
        every = jnp.stack(out)
        return jnp.concatenate([lax.dynamic_slice_in_dim(every, data_at ^ i, 1, axis=0) for i in range(data_size)])

    def from_blocks(value):
        every = jnp.stack(shared(value))
        return jnp.concatenate([lax.dynamic_slice_in_dim(every, block ^ i, 1, axis=0) for i in range(blocks)])

    fout_parts = []
    for q in range(groups):
        pairs = [(groups * (i % blocks) + (i // blocks + q) % groups, i) for i in range(seq_size)]
        fout_parts.append(lax.ppermute(filter_out, "seq", pairs))
    fout_every = jnp.stack(fout_parts)
    fout_block = jnp.concatenate(
        [at_block(fout_every, (i - group) % groups, 0) for i in range(groups)], axis=1
    )

    payload = exchange(pack_tokens(tokens))
    counts = lax.dynamic_slice_in_dim(lengths, 2 * group, 2, axis=0)

    small = jnp.concatenate(
        [
            norm_gain.reshape(-1),
            norm_bias.reshape(-1),
            conv_taps.reshape(-1),
            filter_in.reshape(-1),
            filter_bias.reshape(-1),
            filter_mid.reshape(-1),
            fout_block.reshape(-1),
        ]
    )
    small_size = -(-small.shape[0] // 2048) * 2048
    small = jnp.pad(small, (0, small_size - small.shape[0])).reshape(-1, 128)
    small_all = gathered(small).reshape(data_size, small_size)
    shard = features // data_size
    hidden_shard = filter_in.shape[1]
    cuts = np.cumsum(
        [0, 2 * shard, 2 * shard, 9 * shard, 5 * hidden_shard, 2 * hidden_shard, 128 * hidden_shard, width * hidden_shard]
    )
    pieces = [small_all[:, cuts[i] : cuts[i + 1]] for i in range(7)]

    def channels(piece, lead):
        whole = jnp.moveaxis(piece.reshape(data_size, lead, shard), 0, 1).reshape(lead, features)
        return lax.dynamic_slice_in_dim(whole, block * width, width, axis=1).astype(F32)

    gains = pair_lanes(channels(pieces[0], 2))
    offsets = pair_lanes(channels(pieces[1], 2))
    taps = pair_lanes(channels(pieces[2], 9))
    fin = jnp.moveaxis(pieces[3].reshape(data_size, 5, hidden_shard), 0, 1).reshape(5, 128)
    fbias = jnp.moveaxis(pieces[4].reshape(data_size, 2, hidden_shard), 0, 1).reshape(2, 128)
    fmid = pieces[5].reshape(128, 128)
    fout = doubled(pieces[6].reshape(128, width), 1)
    fin_stack = jnp.concatenate([fin, fin, fin, jnp.zeros((1, 128), BF16)], axis=0)
    channel_ids = block * width + jnp.arange(width, dtype=jnp.int32)
    fast, slow = math.log(100.0) / 0.3, math.log(100.0) / 1.5
    rates = slow + (fast - slow) * channel_ids.astype(F32) / float(features - 1)
    rates = doubled(rates[None, :], 1)

    large = jnp.concatenate(
        [
            at_block(in_weight, block, 1).reshape(-1, width),
            at_block(out_weight, block, 0).reshape(-1, width),
            at_block(up_weight, block, 1).reshape(-1, width),
            at_block(down_weight, block, 0).reshape(-1, width),
        ],
        axis=0,
    )
    large_all = lax.all_gather(large, "dp", axis=0, tiled=False)
    part = width // data_size
    row_cuts = np.cumsum([0, 3 * part, part, 8 * part, 4 * part])
    lw = [large_all[:, row_cuts[i] : row_cuts[i + 1]] for i in range(4)]
    w_in = jnp.moveaxis(lw[0].reshape(data_size, 3, part, width), 0, 1).reshape(3, width, width)
    w_in = doubled(doubled(w_in, 2), 1)
    w_in_flat = jnp.moveaxis(w_in, 0, 1).reshape(256, 768)
    w_in_t = jnp.swapaxes(w_in, 1, 2).reshape(768, 256)
    w_out = doubled(doubled(lw[1].reshape(width, width), 1), 0)
    w_up = jnp.moveaxis(lw[2].reshape(data_size, 2, part, 4 * width), 0, 1).reshape(2, width, 4 * width)
    w_up = doubled(w_up, 1)
    w_up_flat = jnp.concatenate([w_up[0], w_up[1]], axis=1)
    w_up_t = jnp.swapaxes(w_up, 1, 2).reshape(8 * width, 256)
    w_down = doubled(lw[3].reshape(4 * width, width), 1)

    first_np, second_np = stage_tables()
    full_first = jnp.asarray(first_np, BF16)
    full_last = jnp.asarray(np.swapaxes(first_np, 1, 2), BF16)
    second = jnp.asarray(second_np, BF16)
    third = jnp.asarray(second_np.T, BF16)
    tables = (full_first[:, :, :256], second, third, full_last[:, :256])
    feats = jnp.asarray(lag_table(total), BF16)

    hidden = make_filter(
        feats,
        fin_stack,
        fbias.astype(F32),
        jnp.concatenate([fmid, fmid, fmid], axis=0),
        jnp.concatenate([fout, fout], axis=0),
        rates,
        full_first,
        second,
    )
    spectrum = hidden[4]
    hidden = hidden[:4]

    cot = exchange(pack_cotangent(cotangent, payload))
    masked, short, values = mixer_in(counts, payload, gains[0:1], offsets[0:1], w_in_flat, taps, total)
    spec, conv, gated = long_conv(values, short, spectrum, tables)
    conv = conv.reshape(total, 384)
    gated = gated.reshape(total, 384)
    middle, stats = mixer_out(payload, gated, w_out)

    out, q, sums, norm, g_up, g_down, small_two = feed_forward(
        middle, cot, shared(stats), gains[1:2], offsets[1:2], w_up_flat, w_up_t, w_down, w_down.T
    )
    ffn = jnp.concatenate(
        [
            g_up.reshape(data_size, part * 8 * width // 256, 256),
            g_down.reshape(data_size, 4 * width // data_size, 256),
        ],
        axis=1,
    )
    ffn = lax.all_to_all(ffn, "dp", 0, 0, tiled=True)
    out = exchange(out)

    grad, grad_conv, grad_one, g_out = gate_back(q, middle, cot, norm, shared(sums), gated, conv, short, w_out.T)
    grad_values, cross = conv_back(grad_conv, spec, spectrum, tables, ffn)
    back, g_in, small_one = mixer_back(
        counts,
        grad_values.reshape(total, 384),
        grad_one,
        short,
        masked,
        payload,
        grad,
        gains[0:1],
        offsets[0:1],
        taps,
        w_in_t,
        out,
    )
    back = exchange(back)
    out_tokens = unpack_out(out)
    grad_tokens = unpack_grad(back, tokens)
    g_fin, g_mid, g_fout, g_fbias = filter_back(cross, hidden, feats, fmid.T, fout.T, rates, third, full_last, out)

    def reduced(value):
        value = value.astype(F32).sum(axis=0)
        step = 1
        while step < groups:
            pairs = [(i, i ^ (step * blocks)) for i in range(seq_size)]
            sent = value.astype(BF16)
            value = sent.astype(F32) + lax.ppermute(sent, "seq", pairs).astype(F32)
            step *= 2
        return from_blocks(value.astype(BF16)).astype(F32)

    ffn = reduced(ffn)
    cut = part * 8 * width // 256
    grad_up = jnp.moveaxis(ffn[:, :cut].reshape(blocks, part, 2, 4 * width), 2, 0)
    grad_down = ffn[:, cut:, :width]

    sums_one = unpair_lanes(small_one.reshape(11, 8, 384).sum(axis=1))
    sums_two = unpair_lanes(small_two.reshape(2, 8, 384).sum(axis=1))
    per_block = jnp.concatenate([sums_one[0:1], sums_two[0:1], sums_one[1:2], sums_two[1:2], sums_one[2:]], axis=0)
    g_fin = g_fin[0:5] + g_fin[5:10] + g_fin[10:15]
    g_fbias = g_fbias.reshape(2, 8, 128).sum(axis=1)
    g_fout = g_fout[:, :192] + jnp.pad(g_fout[:, 192:], ((0, 0), (128, 0)))
    same = jnp.concatenate([per_block.reshape(-1), g_fin.reshape(-1), g_fbias.reshape(-1)])
    own = jnp.concatenate(
        [
            g_in.reshape(data_size, -1),
            g_out.reshape(data_size, -1),
            g_mid.reshape(data_size, -1).astype(BF16),
            g_fout.reshape(data_size, -1).astype(BF16),
            jnp.broadcast_to(same.astype(BF16)[None], (data_size, same.shape[0])),
        ],
        axis=1,
    )
    filled = -(-own.shape[1] // 2048) * 2048
    own = jnp.pad(own, ((0, 0), (0, filled - own.shape[1]))).reshape(data_size, filled // 128, 128)
    rest = reduced(lax.all_to_all(own, "dp", 0, 0, tiled=True)).reshape(blocks, filled)
    ends = np.cumsum(
        [0, part * 768, part * 256, hidden_shard * 128, hidden_shard * width, 13 * width, 5 * 128, 2 * 128]
    )
    got = [rest[:, ends[i] : ends[i + 1]] for i in range(7)]
    grad_in = jnp.moveaxis(got[0].reshape(blocks, part, 3, 256)[..., :width], 2, 0)
    grad_outw = got[1].reshape(blocks, part, 256)[..., :width]
    grad_mid = got[2].reshape(blocks, hidden_shard, 128).sum(axis=0)
    grad_fout = jnp.moveaxis(got[3].reshape(blocks, hidden_shard, width), 0, 1).reshape(hidden_shard, features)
    grad_fout = lax.dynamic_slice_in_dim(grad_fout, place * (features // seq_size), features // seq_size, axis=1)
    norms = jnp.moveaxis(got[4].reshape(blocks, 13, width), 0, 1).reshape(13, features)
    norms = lax.dynamic_slice_in_dim(norms, data_at * shard, shard, axis=1)
    grad_fin = got[5].reshape(blocks, 5, 128).sum(axis=0)
    grad_fin = lax.dynamic_slice_in_dim(grad_fin, data_at * hidden_shard, hidden_shard, axis=1)
    grad_fbias = got[6].reshape(blocks, 2, 128).sum(axis=0)
    grad_fbias = lax.dynamic_slice_in_dim(grad_fbias, data_at * hidden_shard, hidden_shard, axis=1)
    return (
        out_tokens,
        grad_tokens,
        norms[0:2],
        norms[2:4],
        grad_in,
        norms[4:13].reshape(3, 3, shard),
        grad_fin,
        grad_mid,
        grad_fbias,
        grad_fout,
        grad_outw,
        grad_up,
        grad_down,
    )


def solution(mesh):
    placed = (
        P("dp", "seq", None),
        P("dp"),
        P("dp", "seq", None),
        P(None, "dp"),
        P(None, "dp"),
        P(None, None, "dp", None),
        P(None, None, "dp"),
        P(None, "dp"),
        P("dp", None),
        P(None, "dp"),
        P("dp", "seq"),
        P(None, "dp", None),
        P(None, None, "dp", None),
        P(None, "dp", None),
    )
    return jax.shard_map(
        per_device,
        mesh=mesh,
        in_specs=placed,
        out_specs=(
            P("dp", "seq", None),
            P("dp", "seq", None),
            P(None, "dp"),
            P(None, "dp"),
            P(None, None, "dp", None),
            P(None, None, "dp"),
            P(None, "dp"),
            P("dp", None),
            P(None, "dp"),
            P("dp", "seq"),
            P(None, "dp", None),
            P(None, None, "dp", None),
            P(None, "dp", None),
        ),
        check_vma=False,
    )
```

```python
import functools
import math

import jax
import jax.numpy as jnp
import numpy as np
from jax import lax
from jax.experimental import pallas as pl
from jax.experimental.pallas import tpu as pltpu
from jax.sharding import PartitionSpec as P

F32 = jnp.float32
BF16 = jnp.bfloat16
EPS = 1e-05
SINE_FREQ = 10.0
GROUP = 3
COLS = 128
HALF_ROWS = 16
FULL_ROWS = 32
FREQ_ROWS = 17
STAT_ROWS = 16
GROUPED = 2
VMEM = pltpu.CompilerParams(vmem_limit_bytes=56 * 1024 * 1024)
WIDE_VMEM = pltpu.CompilerParams(vmem_limit_bytes=60 * 1024 * 1024)


def stage_tables():
    k1 = np.arange(FREQ_ROWS)[:, None, None]
    t1 = np.arange(FULL_ROWS)[None, :, None]
    t2 = np.arange(COLS)[None, None, :]
    phase = 2.0 * np.pi * ((k1 * (t1 * COLS + t2)) % 4096) / 4096.0
    both = np.stack([np.cos(phase), -np.sin(phase)], axis=1)
    out = np.zeros((8, FREQ_ROWS, 2, 16, FULL_ROWS, 16), np.float32)
    for a in range(16):
        out[:, :, :, a, :, a] = np.moveaxis(both[..., a::16], -1, 0)
    first = out.reshape(8, FREQ_ROWS * 32, FULL_ROWS * 16)
    theta = 2.0 * np.pi * (np.outer(np.arange(COLS), np.arange(COLS)) % COLS) / COLS
    second = np.block([[np.cos(theta), np.sin(theta)], [-np.sin(theta), np.cos(theta)]])
    return first, second


def lag_table(seq_total):
    lags = np.arange(2 * seq_total)
    scaled = np.where(lags < seq_total, lags, lags - 2 * seq_total) / float(seq_total)
    feats = np.stack(
        [
            scaled,
            np.cos(np.pi * scaled),
            np.sin(np.pi * scaled),
            np.cos(2.0 * np.pi * scaled),
            np.sin(2.0 * np.pi * scaled),
        ],
        axis=1,
    ).astype(np.float32)
    parts, rest = [], feats
    for _ in range(3):
        piece = rest.astype(jnp.bfloat16)
        parts.append(piece.astype(np.float32))
        rest = rest - piece.astype(np.float32)
    table = np.zeros((2 * seq_total, 16), np.float32)
    table[:, :15] = np.concatenate(parts, axis=1)
    return table


def dot(a, b):
    return jnp.dot(a, b, preferred_element_type=F32)


def low_lanes(rows):
    return lax.broadcasted_iota(jnp.int32, (rows, 128), 1) < 64


def tiles(value):
    return [value[:, 128 * i : 128 * (i + 1)] for i in range(value.shape[1] // 128)]


def half_turn(value):
    return pltpu.roll(value, 64, axis=1)


def stacked(value):
    first, second, last = tiles(value)
    low = low_lanes(value.shape[0])
    zero = jnp.zeros_like(last)
    return jnp.concatenate(
        [
            jnp.concatenate([first, jnp.where(low, last, zero)], axis=1),
            jnp.concatenate([second, jnp.where(low, zero, last)], axis=1),
        ],
        axis=0,
    )


def packed(value):
    rows = value.shape[0] // 2
    low = low_lanes(rows)
    last = jnp.where(low, value[:rows, 128:], value[rows:, 128:])
    return jnp.concatenate([value[:rows, :128], value[rows:, :128], last], axis=1)


def pair_sum(value):
    first, second, last = tiles(value)
    low = low_lanes(value.shape[0])
    zero = jnp.zeros_like(last)
    return (
        jnp.sum(first + jnp.where(low, last, zero), axis=1, keepdims=True),
        jnp.sum(second + jnp.where(low, zero, last), axis=1, keepdims=True),
    )


def spread(col_a, col_b, rows):
    wide_a = jnp.broadcast_to(col_a, (rows, 128))
    wide_b = jnp.broadcast_to(col_b, (rows, 128))
    return jnp.concatenate([wide_a, wide_b, jnp.where(low_lanes(rows), wide_a, wide_b)], axis=1)


def to_rows(columns, rows):
    lane = lax.broadcasted_iota(jnp.int32, (rows, 128), 1)
    out = jnp.zeros((rows, 128), F32)
    for at, column in enumerate(columns):
        out = jnp.where(lane == at, jnp.broadcast_to(column, (rows, 128)), out)
    if rows % 128:
        out = jnp.concatenate([out, jnp.zeros((128 - rows, 128), F32)], axis=0)
    return out.T[:8, :rows]


def to_columns(values):
    rows = values.shape[1]
    if rows % 128:
        values = jnp.concatenate([values, jnp.zeros((8, 128 - rows), F32)], axis=1)
    tall = jnp.concatenate([values, jnp.zeros((120, values.shape[1]), F32)], axis=0)
    return tall.T[:rows]


def split_rows(values):
    high = values.astype(BF16).astype(F32)
    return jnp.concatenate([high, values - high], axis=0).astype(BF16)


def join_rows(values):
    wide = values.astype(F32)
    return wide[:8] + wide[8:]


def position_mask(start, rows, count_a, count_b):
    place = start + lax.broadcasted_iota(jnp.int32, (rows, 128), 0)
    keep_a = (place < count_a).astype(F32)
    keep_b = (place < count_b).astype(F32)
    return jnp.concatenate([keep_a, keep_b, jnp.where(low_lanes(rows), keep_a, keep_b)], axis=1)


def sine_pair(angle):
    turns = jnp.floor(angle * (1.0 / math.pi) + 0.5)
    rest = angle - turns * 3.140625
    rest = rest - turns * 9.675025939941406e-4
    rest = rest - turns * 1.5099579909783764e-7
    half = turns * 0.5
    sign = 1.0 - 4.0 * (half - jnp.floor(half))
    square = rest * rest
    sine = square * (-1.0 / 39916800.0) + 1.0 / 362880.0
    sine = sine * square - 1.0 / 5040.0
    sine = sine * square + 1.0 / 120.0
    sine = sine * square - 1.0 / 6.0
    sine = rest + rest * square * sine
    cosine = square * (1.0 / 479001600.0) - 1.0 / 3628800.0
    cosine = cosine * square + 1.0 / 40320.0
    cosine = cosine * square - 1.0 / 720.0
    cosine = cosine * square + 1.0 / 24.0
    cosine = cosine * square - 0.5
    cosine = 1.0 + square * cosine
    return sine * sign, cosine * sign


def normal_cdf(value):
    return 0.5 + 0.5 * lax.erf(value * math.sqrt(0.5))


def normal_density(value):
    return jnp.exp(value * value * -0.5) * (1.0 / math.sqrt(2.0 * math.pi))


def work(micros):
    return pl.CostEstimate(flops=int(micros * 1.15e9), bytes_accessed=0, transcendentals=0)


def pass_kernel(*refs):
    pass


def after(value, *others):
    anywhere = pl.BlockSpec(memory_space=pl.ANY)
    return pl.pallas_call(
        pass_kernel,
        in_specs=[anywhere] * (1 + len(others)),
        out_specs=anywhere,
        out_shape=jax.ShapeDtypeStruct(value.shape, value.dtype),
        input_output_aliases={0: 0},
        name="after",
    )(value, *others)


def pack_pair(a, b, block):
    rows = a.shape[0]
    low = low_lanes(rows)
    base = 3 * (block // 2)
    ta = [a[:, 128 * (base + i) : 128 * (base + i + 1)] for i in range(3)]
    tb = [b[:, 128 * (base + i) : 128 * (base + i + 1)] for i in range(3)]
    if block % 2 == 0:
        parts = [ta[0], tb[0], jnp.where(low, ta[1], half_turn(tb[1]))]
    else:
        parts = [
            jnp.where(low, half_turn(ta[1]), half_turn(ta[2])),
            jnp.where(low, half_turn(tb[1]), half_turn(tb[2])),
            jnp.where(low, half_turn(ta[2]), tb[2]),
        ]
    return jnp.concatenate(parts, axis=1)


def unpack_pairs(even, odd):
    low = low_lanes(even.shape[0])
    ea, eb, el = tiles(even)
    oa, ob, ol = tiles(odd)
    a = [ea, jnp.where(low, el, half_turn(oa)), jnp.where(low, half_turn(oa), half_turn(ol))]
    b = [eb, jnp.where(low, half_turn(el), half_turn(ob)), jnp.where(low, half_turn(ob), ol)]
    return jnp.concatenate(a, axis=1), jnp.concatenate(b, axis=1)


def row_stats(value):
    mean = jnp.mean(value, axis=1, keepdims=True)
    centred = value - mean
    variance = jnp.mean(centred * centred, axis=1, keepdims=True)
    return mean, lax.rsqrt(variance + EPS)


def pack_tokens_kernel(x_ref, out_ref):
    rows = x_ref.shape[1]
    a = x_ref[0].astype(F32)
    b = x_ref[1].astype(F32)
    stats = split_rows(to_rows(row_stats(a) + row_stats(b), rows))
    for block in range(4):
        out_ref[block, :rows, :] = pack_pair(a, b, block).astype(BF16)
        out_ref[block, rows:, :rows] = stats


def pack_tokens(tokens):
    count, rows, width = tokens.shape
    return pl.pallas_call(
        pack_tokens_kernel,
        grid=(count // 2,),
        in_specs=[pl.BlockSpec((2, rows, width), lambda i: (i, 0, 0))],
        out_specs=pl.BlockSpec((4, rows + STAT_ROWS, 384), lambda i: (i, 0, 0)),
        out_shape=jax.ShapeDtypeStruct((2 * count, rows + STAT_ROWS, 384), BF16),
        compiler_params=VMEM,
        cost_estimate=work(3.3),
        name="pack_tokens",
    )(tokens)


def pack_cotangent_kernel(x_ref, after_ref, out_ref):
    a = x_ref[0].astype(F32)
    b = x_ref[1].astype(F32)
    for block in range(4):
        out_ref[block] = pack_pair(a, b, block).astype(BF16)


def pack_cotangent(cotangent, after):
    count, rows, width = cotangent.shape
    return pl.pallas_call(
        pack_cotangent_kernel,
        grid=(count // 2,),
        in_specs=[
            pl.BlockSpec((2, rows, width), lambda i: (i, 0, 0)),
            pl.BlockSpec(memory_space=pl.ANY),
        ],
        out_specs=pl.BlockSpec((4, rows, 384), lambda i: (i, 0, 0)),
        out_shape=jax.ShapeDtypeStruct((2 * count, rows, 384), BF16),
        compiler_params=VMEM,
        cost_estimate=work(0.5),
        name="pack_cotangent",
    )(cotangent, after)


def transform_first(table_ref, data_ref, spec_ref):
    count, _, lanes = data_ref.shape

    def one(j, carry):
        start = pl.ds(pl.multiple_of(16 * j, 16), 16)
        block = data_ref[:, start, :].reshape(count * 16, lanes)
        part = dot(table_ref[j], block).astype(BF16)
        spec_ref[:, start, :] = part.reshape(2 * FREQ_ROWS, 16, lanes)
        return carry

    lax.fori_loop(0, 8, one, 0, unroll=True)


def frequency_weight(k1):
    edge = jnp.logical_or(k1 == 0, k1 == FREQ_ROWS - 1)
    return jnp.where(edge, 1.0 / 4096.0, 2.0 / 4096.0).astype(F32)


def make_filter_kernel(
    feat_ref,
    fin_ref,
    bias_ref,
    mid_ref,
    fout_ref,
    rate_ref,
    table_ref,
    second_ref,
    s1_ref,
    c1_ref,
    s2_ref,
    c2_ref,
    spec_ref,
    taps_ref,
    work_ref,
):
    step_rows = 256
    total = feat_ref.shape[0]

    def one(i, carry):
        rows = pl.ds(pl.multiple_of(i * step_rows, step_rows), step_rows)
        inner = dot(feat_ref[rows, :], fin_ref[...]) + bias_ref[0:1, :]
        s1, c1 = sine_pair(SINE_FREQ * inner)
        s1_ref[rows, :] = s1.astype(BF16)
        c1_ref[rows, :] = c1.astype(BF16)
        p1 = s1.astype(BF16)
        r1 = s1 - p1.astype(F32)
        p2 = r1.astype(BF16)
        p3 = (r1 - p2.astype(F32)).astype(BF16)
        outer = dot(jnp.concatenate([p1, p2, p3], axis=1), mid_ref[...]) + bias_ref[1:2, :]
        s2, c2 = sine_pair(SINE_FREQ * outer)
        s2_ref[rows, :] = s2.astype(BF16)
        c2_ref[rows, :] = c2.astype(BF16)
        q1 = s2.astype(BF16)
        q2 = (s2 - q1.astype(F32)).astype(BF16)
        raw = dot(jnp.concatenate([q1, q2], axis=1), fout_ref[...])
        lag = i * step_rows + lax.broadcasted_iota(jnp.int32, (step_rows, 256), 0)
        signed = jnp.where(lag < total // 2, lag, total - lag)
        distance = signed.astype(F32) * (2.0 / total)
        kernel = raw * jnp.exp(-distance * rate_ref[...])
        taps_ref[pl.ds(2 * i, 2), :, :] = kernel.astype(BF16).reshape(2, COLS, 256)
        return carry

    lax.fori_loop(0, total // step_rows, one, 0, unroll=4)
    transform_first(table_ref, taps_ref, work_ref)

    def second(k1, carry):
        part = work_ref[pl.ds(2 * k1, 2), :, :].reshape(256, 256)
        spec_ref[k1] = dot(second_ref[...], part) * frequency_weight(k1)
        return carry

    lax.fori_loop(0, FREQ_ROWS, second, 0, unroll=True)


def make_filter(feats, fin, bias, mid, fout, rate, table, second):
    total = feats.shape[0]
    hidden = jax.ShapeDtypeStruct((total, 128), BF16)
    return pl.pallas_call(
        make_filter_kernel,
        out_shape=(hidden,) * 4 + (jax.ShapeDtypeStruct((FREQ_ROWS, 256, 256), F32),),
        scratch_shapes=[
            pltpu.VMEM((FULL_ROWS, COLS, 256), BF16),
            pltpu.VMEM((2 * FREQ_ROWS, COLS, 256), BF16),
        ],
        compiler_params=VMEM,
        cost_estimate=work(2),
        name="make_filter",
    )(feats, fin, bias, mid, fout, rate, table, second)


def normed_pair(payload, rows, scales, offsets):
    value = payload[:rows].astype(F32)
    stats = to_columns(join_rows(payload[rows:, :rows]))
    mean = spread(stats[:, 0:1], stats[:, 2:3], rows)
    scale = spread(stats[:, 1:2], stats[:, 3:4], rows)
    unit = (value - mean) * scale
    return unit, scale, unit * scales + offsets


def filter_lanes(block):
    return jnp.concatenate([block[:, :128], block], axis=1)


def full_spec(shape):
    return pl.BlockSpec(shape, lambda i: (0,) * len(shape))


ANYWHERE = pl.BlockSpec(memory_space=pl.ANY)


def three_shifts(window, rows):
    return window[7 : 7 + rows], window[8 : 8 + rows], window[9 : 9 + rows]


def mixer_forward_kernel(
    counts_ref,
    x_ref,
    scales_ref,
    offsets_ref,
    w_ref,
    wout_ref,
    second_ref,
    third_ref,
    first_hbm,
    fourth_hbm,
    filter_hbm,
    short_hbm,
    spec_hbm,
    conv_hbm,
    middle_hbm,
    stats_ref,
    first_ref,
    fourth_ref,
    filter_ref,
    normed_ref,
    short_ref,
    values_ref,
    work_ref,
    spec_ref,
    conv_ref,
    gated_ref,
    middle_ref,
    in_sems,
    out_sems,
):
    chunks, tall, _ = x_ref.shape
    rows = tall - STAT_ROWS
    total = chunks * rows
    size = 256
    count_a, count_b = counts_ref[0], counts_ref[1]
    loads = [
        pltpu.make_async_copy(src, dst, in_sems.at[i])
        for i, (src, dst) in enumerate(
            (
                (first_hbm.at[:, :, pl.ds(0, HALF_ROWS * 16)], first_ref),
                (filter_hbm, filter_ref),
                (fourth_hbm.at[:, pl.ds(0, HALF_ROWS * 16), :], fourth_ref),
            )
        )
    ]
    stores = [
        pltpu.make_async_copy(src, dst, out_sems.at[i])
        for i, (src, dst) in enumerate(
            (
                (short_ref, short_hbm),
                (spec_ref, spec_hbm),
                (conv_ref, conv_hbm),
                (middle_ref, middle_hbm),
            )
        )
    ]
    for load in loads:
        load.start()

    edge = jnp.zeros((8, 384), F32)
    normed_ref[0:8, :] = edge
    normed_ref[8 + total :, :] = edge
    for c in range(chunks):
        _, _, normed = normed_pair(x_ref[c], rows, scales_ref[...], offsets_ref[...])
        keep = position_mask(c * rows, rows, count_a, count_b)
        normed_ref[8 + c * rows : 8 + (c + 1) * rows, :] = normed * keep
    for b in range(total // size):
        at = slice(size * b, size * (b + 1))
        window = normed_ref[size * b : size * (b + 1) + 16, :]
        wide = jnp.concatenate([stacked(v).astype(BF16) for v in three_shifts(window, size)], axis=1)
        out = dot(wide, w_ref[...])
        shorts = [packed(out[:, 256 * s : 256 * (s + 1)]) for s in range(3)]
        for s in range(3):
            short_ref[s, at, :] = shorts[s].astype(BF16)
        keep = position_mask(size * b, size, count_a, count_b)
        values = (shorts[2] * shorts[0] * keep).astype(BF16)
        values_ref[2 * b : 2 * b + 2, :, :] = values.reshape(2, COLS, 384)
    stores[0].start()

    loads[0].wait()
    transform_first(first_ref, values_ref, work_ref)
    loads[1].wait()

    def middle(k1, carry):
        part = work_ref[pl.ds(2 * k1, 2), :, :].reshape(256, 384)
        spec = dot(second_ref[...], part)
        spec_ref[k1] = spec.astype(BF16)
        re, im = spec[:128], spec[128:]
        block = filter_ref[k1]
        fre, fim = filter_lanes(block[:128]), filter_lanes(block[128:])
        prod = jnp.concatenate([re * fre - im * fim, re * fim + im * fre], axis=0).astype(BF16)
        work_ref[pl.ds(2 * k1, 2), :, :] = dot(third_ref[...], prod).astype(BF16).reshape(2, COLS, 384)
        return carry

    lax.fori_loop(0, FREQ_ROWS, middle, 0, unroll=True)
    stores[1].start()
    loads[2].wait()
    for j in range(8):
        part = work_ref[:, 16 * j : 16 * (j + 1), :].reshape(FREQ_ROWS * 32, 384)
        conv = dot(fourth_ref[j], part)
        for i in range(HALF_ROWS):
            at = slice(COLS * i + 16 * j, COLS * i + 16 * (j + 1))
            piece = conv[16 * i : 16 * (i + 1)]
            conv_ref[at, :] = piece.astype(BF16)
            gated_ref[at, :] = (piece * short_ref[1, at, :].astype(F32)).astype(BF16)
    stores[2].start()
    for c in range(chunks):
        at = slice(rows * c, rows * (c + 1))
        out = packed(dot(stacked(gated_ref[at, :]), wout_ref[...]))
        value = x_ref[c, :rows, :].astype(F32) + out
        middle_ref[at, :] = value
        sum_a, sum_b = pair_sum(value)
        mean_a, mean_b = sum_a * (1.0 / 192.0), sum_b * (1.0 / 192.0)
        centred = value - spread(mean_a, mean_b, rows)
        square_a, square_b = pair_sum(centred * centred)
        stats_ref[c] = to_rows((mean_a, square_a, mean_b, square_b), rows)
    stores[3].start()
    for store in stores:
        store.wait()


def mixer_forward(counts, payload, scales, offsets, weight, wout, spectrum, tables):
    chunks, tall, _ = payload.shape
    rows = tall - STAT_ROWS
    total = chunks * rows
    first, second, third, fourth = tables
    seq = (total, 384)
    wide = (FREQ_ROWS, 256, 384)
    return pl.pallas_call(
        mixer_forward_kernel,
        grid=(1,),
        in_specs=[pl.BlockSpec(memory_space=pltpu.SMEM)]
        + [full_spec(a.shape) for a in (payload, scales, offsets, weight, wout, second, third)]
        + [ANYWHERE] * 3,
        out_specs=[ANYWHERE] * 4 + [full_spec((chunks, 8, rows))],
        out_shape=[
            jax.ShapeDtypeStruct((3,) + seq, BF16),
            jax.ShapeDtypeStruct(wide, BF16),
            jax.ShapeDtypeStruct(seq, BF16),
            jax.ShapeDtypeStruct(seq, F32),
            jax.ShapeDtypeStruct((chunks, 8, rows), F32),
        ],
        scratch_shapes=[
            pltpu.VMEM(first.shape[:2] + (HALF_ROWS * 16,), BF16),
            pltpu.VMEM((8, HALF_ROWS * 16, fourth.shape[2]), BF16),
            pltpu.VMEM(spectrum.shape, F32),
            pltpu.VMEM((total + 16, 384), F32),
            pltpu.VMEM((3,) + seq, BF16),
            pltpu.VMEM((HALF_ROWS, COLS, 384), BF16),
            pltpu.VMEM((2 * FREQ_ROWS, COLS, 384), BF16),
            pltpu.VMEM(wide, BF16),
            pltpu.VMEM(seq, BF16),
            pltpu.VMEM(seq, BF16),
            pltpu.VMEM(seq, F32),
            pltpu.SemaphoreType.DMA((3,)),
            pltpu.SemaphoreType.DMA((4,)),
        ],
        compiler_params=VMEM,
        cost_estimate=work(25),
        name="mixer_forward",
    )(counts, payload, scales, offsets, weight, wout, second, third, first, fourth, spectrum)


def column_sums(value):
    return jnp.sum(value.reshape(value.shape[0] // 8, 8, value.shape[1]), axis=0)


def fold_rows(value):
    return jnp.concatenate([value[:128], value[128:192] + value[192:256]], axis=0)


def fold_lanes(value):
    last = value[:, 128:]
    summed = jnp.where(low_lanes(value.shape[0]), last + half_turn(last), jnp.zeros_like(last))
    return jnp.concatenate([value[:, :128], summed], axis=1)


def feed_forward_kernel(
    middle_ref,
    s0_ref,
    s1_ref,
    s2_ref,
    s3_ref,
    scales_ref,
    offsets_ref,
    up_ref,
    down_ref,
    out_ref,
    pair_ref,
    normed_ref,
    unit_ref,
    norm_ref,
):
    chunks, rows, _ = out_ref.shape
    for c in range(chunks):
        at_rows = slice(rows * c, rows * (c + 1))
        parts = [ref[c] for ref in (s0_ref, s1_ref, s2_ref, s3_ref)]
        mean = (parts[0] + parts[1] + parts[2] + parts[3]) * 0.25
        spread_sum = jnp.zeros_like(mean)
        for part in parts:
            gap = part - mean
            spread_sum += 192.0 * gap * gap
        squares = parts[0] + parts[1] + parts[2] + parts[3]
        scale_a = lax.rsqrt((squares[1:2] + spread_sum[0:1]) * (1.0 / 768.0) + EPS)
        scale_b = lax.rsqrt((squares[3:4] + spread_sum[2:3]) * (1.0 / 768.0) + EPS)
        norm = jnp.concatenate([mean[0:1], scale_a, mean[2:3], scale_b, jnp.zeros((4, rows), F32)], axis=0)
        norm_ref[c] = norm
        columns = to_columns(norm)
        middle = middle_ref[at_rows, :]
        unit = (middle - spread(columns[:, 0:1], columns[:, 2:3], rows)) * spread(columns[:, 1:2], columns[:, 3:4], rows)
        unit_ref[at_rows, :] = unit.astype(BF16)
        normed = stacked(unit * scales_ref[...] + offsets_ref[...]).astype(BF16)
        normed_ref[c] = normed
        hiddens = []
        width = 256
        for f in range(768 // width):
            at = slice(width * f, width * (f + 1))
            at_up = slice(768 + width * f, 768 + width * (f + 1))
            gate = dot(normed, up_ref[:, at])
            upper = dot(normed, up_ref[:, at_up])
            pair_ref[c, :, at] = gate.astype(BF16)
            pair_ref[c, :, at_up] = upper.astype(BF16)
            hiddens.append((gate * normal_cdf(gate) * upper).astype(BF16))
        down = dot(jnp.concatenate(hiddens, axis=1), down_ref[...])
        out_ref[c] = (middle + packed(down)).astype(BF16)


def feed_forward(middle, stats, scales, offsets, up, down):
    chunks, _, rows = stats[0].shape
    total = chunks * rows
    many = min(chunks, GROUPED)
    stat_spec = pl.BlockSpec((many, 8, rows), lambda i: (i, 0, 0))
    rows_spec = pl.BlockSpec((many * rows, 384), lambda i: (i, 0))
    return pl.pallas_call(
        feed_forward_kernel,
        grid=(chunks // many,),
        in_specs=[rows_spec] + [stat_spec] * 4 + [full_spec(a.shape) for a in (scales, offsets, up, down)],
        out_specs=[
            pl.BlockSpec((many, rows, 384), lambda i: (i, 0, 0)),
            pl.BlockSpec((many, 2 * rows, 1536), lambda i: (i, 0, 0)),
            pl.BlockSpec((many, 2 * rows, 256), lambda i: (i, 0, 0)),
            rows_spec,
            stat_spec,
        ],
        out_shape=[
            jax.ShapeDtypeStruct((chunks, rows, 384), BF16),
            jax.ShapeDtypeStruct((chunks, 2 * rows, 1536), BF16),
            jax.ShapeDtypeStruct((chunks, 2 * rows, 256), BF16),
            jax.ShapeDtypeStruct((total, 384), BF16),
            jax.ShapeDtypeStruct((chunks, 8, rows), F32),
        ],
        compiler_params=VMEM,
        cost_estimate=work(11),
        name="feed_forward",
    )(middle, *stats, scales, offsets, up, down)


def feed_back_kernel(
    cot_ref,
    pair_ref,
    normed_ref,
    unit_ref,
    scales_ref,
    upt_ref,
    downt_ref,
    q_ref,
    sums_ref,
    gffn_ref,
    small_ref,
    up_acc,
    down_acc,
):
    chunks, rows, _ = cot_ref.shape
    step = pl.program_id(0)

    @pl.when(step == 0)
    def _():
        small_ref[...] = jnp.zeros_like(small_ref)
        up_acc[...] = jnp.zeros_like(up_acc)
        down_acc[...] = jnp.zeros_like(down_acc)

    join = lambda parts: jnp.concatenate(parts, axis=0)
    cot = join([stacked(cot_ref[c]) for c in range(chunks)])
    size = 2 * rows * chunks
    grad_hidden = dot(cot, downt_ref[...])
    hidden, gates, uppers = [], [], []
    width = 256
    for f in range(768 // width):
        at = slice(width * f, width * (f + 1))
        at_up = slice(768 + width * f, 768 + width * (f + 1))
        gate = pair_ref[:, :, at].reshape(size, width).astype(F32)
        upper = pair_ref[:, :, at_up].reshape(size, width).astype(F32)
        cdf = normal_cdf(gate)
        active = gate * cdf
        hidden.append((active * upper).astype(BF16))
        gates.append((grad_hidden[:, at] * upper * (cdf + gate * normal_density(gate))).astype(BF16))
        uppers.append((grad_hidden[:, at] * active).astype(BF16))
    hidden = jnp.concatenate(hidden, axis=1)
    grads = jnp.concatenate(gates + uppers, axis=1)
    back = dot(grads, upt_ref[...])
    up_acc[...] += fold_rows(dot(normed_ref[...].reshape(size, 256).T, grads))
    down_acc[...] += dot(cot.T, hidden)
    for c in range(chunks):
        at_rows = slice(rows * c, rows * (c + 1))
        grad = packed(back[2 * rows * c : 2 * rows * (c + 1)])
        unit = unit_ref[at_rows, :].astype(F32)
        q = grad * scales_ref[...]
        q_ref[at_rows, :] = q.astype(BF16)
        sums_ref[c] = to_rows(pair_sum(q) + pair_sum(q * unit), rows)
        small_ref[0:8, :] += column_sums(grad * unit)
        small_ref[8:16, :] += column_sums(grad)

    @pl.when(step == pl.num_programs(0) - 1)
    def _():
        parts = gffn_ref.shape[0]
        share = 192 // parts
        down = fold_lanes(down_acc[...].T).astype(BF16)
        for d in range(parts):
            for t in range(6):
                value = up_acc[share * d : share * (d + 1), 256 * t : 256 * (t + 1)]
                gffn_ref[d, share * t : share * (t + 1), :] = value.astype(BF16)
            gffn_ref[d, 6 * share :, :] = down[4 * share * d : 4 * share * (d + 1)]


def feed_back(cot, pair, normed, unit, scales, upt, downt, parts):
    chunks, rows, _ = cot.shape
    total = chunks * rows
    many = min(chunks, GROUPED)
    rows_spec = pl.BlockSpec((many * rows, 384), lambda i: (i, 0))
    spec = lambda shape: pl.BlockSpec((many,) + shape[1:], lambda i: (i, 0, 0))
    stats = (chunks, 8, rows)
    return pl.pallas_call(
        feed_back_kernel,
        grid=(chunks // many,),
        in_specs=[spec(cot.shape), spec(pair.shape), spec(normed.shape), rows_spec]
        + [full_spec(a.shape) for a in (scales, upt, downt)],
        out_specs=[rows_spec, spec(stats), full_spec((parts, 1920 // parts, 256)), full_spec((16, 384))],
        out_shape=[
            jax.ShapeDtypeStruct((total, 384), BF16),
            jax.ShapeDtypeStruct(stats, F32),
            jax.ShapeDtypeStruct((parts, 1920 // parts, 256), BF16),
            jax.ShapeDtypeStruct((16, 384), F32),
        ],
        scratch_shapes=[pltpu.VMEM((192, 1536), F32), pltpu.VMEM((256, 768), F32)],
        compiler_params=VMEM,
        cost_estimate=work(2),
        name="feed_back",
    )(cot, pair, normed, unit, scales, upt, downt)


def mixer_backward_kernel(
    counts_ref,
    norm_ref,
    s0_ref,
    s1_ref,
    s2_ref,
    s3_ref,
    woutt_ref,
    second_ref,
    third_ref,
    cot_hbm,
    q_hbm,
    unit_hbm,
    conv_hbm,
    short_hbm,
    first_hbm,
    spec_hbm,
    filter_hbm,
    fourth_hbm,
    grad_hbm,
    cross_hbm,
    grads_hbm,
    cot_ref,
    q_ref,
    unit_ref,
    conv_ref,
    short_ref,
    first_ref,
    spec_ref,
    filter_ref,
    fourth_ref,
    work_ref,
    cross_ref,
    grads_ref,
    in_sems,
    out_sems,
):
    chunks, _, rows = norm_ref.shape
    total = chunks * rows
    count_a, count_b = counts_ref[0], counts_ref[1]
    half = total // 2
    early, late = pl.ds(0, half), pl.ds(half, half)
    lanes = first_ref.shape[2]
    loads = [
        pltpu.make_async_copy(src, dst, in_sems.at[i])
        for i, (src, dst) in enumerate(
            [
                (src.at[part], dst.at[part])
                for part in (early, late)
                for src, dst in (
                    (cot_hbm, cot_ref),
                    (q_hbm, q_ref),
                    (unit_hbm, unit_ref),
                    (short_hbm.at[1], short_ref.at[1]),
                    (conv_hbm, conv_ref),
                )
            ]
            + [
                (first_hbm.at[:, :, pl.ds(0, lanes)], first_ref),
                (spec_hbm, spec_ref),
                (filter_hbm, filter_ref),
                (fourth_hbm.at[:, pl.ds(0, lanes), :], fourth_ref),
                (short_hbm.at[0], short_ref.at[0]),
                (short_hbm.at[2], short_ref.at[2]),
            ]
        )
    ]
    for load in loads:
        load.start()

    for c in range(chunks):
        if c == 0:
            for load in loads[0:5]:
                load.wait()
        if c == chunks // 2:
            for load in loads[5:10]:
                load.wait()
        at = slice(rows * c, rows * (c + 1))
        sums = (s0_ref[c] + s1_ref[c] + s2_ref[c] + s3_ref[c]) * (1.0 / 768.0)
        columns = to_columns(jnp.concatenate([sums[0:4], norm_ref[c][0:4]], axis=0))
        scale = spread(columns[:, 5:6], columns[:, 7:8], rows)
        mean_q = spread(columns[:, 0:1], columns[:, 1:2], rows)
        mean_qh = spread(columns[:, 2:3], columns[:, 3:4], rows)
        back = q_ref[at, :].astype(F32) - mean_q - unit_ref[at, :].astype(F32) * mean_qh
        grad = cot_ref[at, :].astype(F32) + scale * back
        cot_ref[at, :] = grad.astype(BF16)
        grad_gated = packed(dot(stacked(grad).astype(BF16), woutt_ref[...]))
        unit_ref[at, :] = (grad_gated * short_ref[1, at, :].astype(F32)).astype(BF16)
        grads_ref[1, at, :] = (grad_gated * conv_ref[at, :].astype(F32)).astype(BF16)
    stores = [
        pltpu.make_async_copy(src, dst, out_sems.at[i])
        for i, (src, dst) in enumerate(((cot_ref, grad_hbm), (cross_ref, cross_hbm), (grads_ref, grads_hbm)))
    ]
    stores[0].start()

    loads[10].wait()
    for j in range(8):
        block = jnp.concatenate(
            [unit_ref[COLS * i + 16 * j : COLS * i + 16 * (j + 1), :] for i in range(HALF_ROWS)], axis=0
        )
        part = dot(first_ref[j], block).astype(BF16)
        work_ref[:, 16 * j : 16 * (j + 1), :] = part.reshape(2 * FREQ_ROWS, 16, 384)
    for load in loads[11:13]:
        load.wait()

    def middle(k1, carry):
        part = work_ref[pl.ds(2 * k1, 2), :, :].reshape(256, 384)
        grad = dot(second_ref[...], part)
        re, im = grad[:128], grad[128:]
        spec = spec_ref[k1].astype(F32)
        vre, vim = spec[:128], spec[128:]
        cre = re * vre + im * vim
        cim = im * vre - re * vim
        weight = frequency_weight(k1)
        fold = lambda v: jnp.concatenate([v[:, :128] + v[:, 128:256], v[:, 256:]], axis=1)
        cross_ref[k1] = (jnp.concatenate([fold(cre), fold(cim)], axis=0) * weight).astype(BF16)
        block = filter_ref[k1]
        fre, fim = filter_lanes(block[:128]), filter_lanes(block[128:])
        prod = jnp.concatenate([re * fre + im * fim, im * fre - re * fim], axis=0).astype(BF16)
        work_ref[pl.ds(2 * k1, 2), :, :] = dot(third_ref[...], prod).astype(BF16).reshape(2, COLS, 384)
        return carry

    lax.fori_loop(0, FREQ_ROWS, middle, 0, unroll=True)
    stores[1].start()
    for load in loads[13:]:
        load.wait()
    for j in range(8):
        part = work_ref[:, 16 * j : 16 * (j + 1), :].reshape(FREQ_ROWS * 32, 384)
        grad_values = dot(fourth_ref[j], part)
        for i in range(HALF_ROWS):
            start = COLS * i + 16 * j
            at = slice(start, start + 16)
            piece = grad_values[16 * i : 16 * (i + 1)] * position_mask(start, 16, count_a, count_b)
            grads_ref[0, at, :] = (piece * short_ref[2, at, :].astype(F32)).astype(BF16)
            grads_ref[2, at, :] = (piece * short_ref[0, at, :].astype(F32)).astype(BF16)
    stores[2].start()
    for store in stores:
        store.wait()


def mixer_backward(counts, norm, sums, woutt, cot, q, unit, conv, short, spec, spectrum, tables):
    chunks, _, rows = norm.shape
    total = chunks * rows
    first, second, third, fourth = tables
    lanes = HALF_ROWS * 16
    seq = (total, 384)
    cross = (FREQ_ROWS, 256, 256)
    blocked = [norm, *sums, woutt, second, third]
    return pl.pallas_call(
        mixer_backward_kernel,
        grid=(1,),
        in_specs=[pl.BlockSpec(memory_space=pltpu.SMEM)]
        + [full_spec(a.shape) for a in blocked]
        + [ANYWHERE] * 9,
        out_specs=[ANYWHERE] * 3,
        out_shape=[
            jax.ShapeDtypeStruct(seq, BF16),
            jax.ShapeDtypeStruct(cross, BF16),
            jax.ShapeDtypeStruct((3,) + seq, BF16),
        ],
        scratch_shapes=[pltpu.VMEM(seq, BF16)] * 4
        + [
            pltpu.VMEM((3,) + seq, BF16),
            pltpu.VMEM(first.shape[:2] + (lanes,), BF16),
            pltpu.VMEM(spec.shape, BF16),
            pltpu.VMEM(spectrum.shape, F32),
            pltpu.VMEM((8, lanes, fourth.shape[2]), BF16),
            pltpu.VMEM((2 * FREQ_ROWS, COLS, 384), BF16),
            pltpu.VMEM(cross, BF16),
            pltpu.VMEM((3,) + seq, BF16),
            pltpu.SemaphoreType.DMA((16,)),
            pltpu.SemaphoreType.DMA((3,)),
        ],
        compiler_params=VMEM,
        cost_estimate=work(4),
        name="mixer_backward",
    )(counts, *blocked, cot, q, unit, conv, short, first, spec, spectrum, fourth)


def input_back_kernel(
    counts_ref, x_ref, scales_ref, offsets_ref, wt_ref, grads_ref, grad_ref, out_ref, small_ref, parts_ref
):
    chunks, tall, _ = x_ref.shape
    rows = tall - STAT_ROWS
    total = chunks * rows
    size = 512
    count_a, count_b = counts_ref[0], counts_ref[1]
    edge = jnp.zeros((8, 384), F32)
    for j in range(3):
        parts_ref[j, 0:8, :] = edge
        parts_ref[j, 8 + total :, :] = edge
    for b in range(total // size):
        at = slice(size * b, size * (b + 1))
        wide = jnp.concatenate([stacked(grads_ref[s, at, :]) for s in range(3)], axis=1)
        out = dot(wide, wt_ref[...])
        for j in range(3):
            parts_ref[j, 8 + size * b : 8 + size * (b + 1), :] = packed(out[:, 256 * j : 256 * (j + 1)])
    gain = jnp.zeros((8, 384), F32)
    bias = jnp.zeros((8, 384), F32)
    for c in range(chunks):
        at = slice(rows * c, rows * (c + 1))
        ahead = parts_ref[0, rows * c : rows * (c + 1) + 16, :][9 : 9 + rows]
        here = parts_ref[1, 8 + rows * c : 8 + rows * (c + 1), :]
        behind = parts_ref[2, rows * c : rows * (c + 1) + 16, :][7 : 7 + rows]
        keep = position_mask(c * rows, rows, count_a, count_b)
        grad_normed = (ahead + here + behind) * keep
        unit, scale, _ = normed_pair(x_ref[c], rows, scales_ref[...], offsets_ref[...])
        gain += column_sums(grad_normed * unit)
        bias += column_sums(grad_normed)
        q = grad_normed * scales_ref[...]
        out_ref[c, :rows, :] = (grad_ref[at, :].astype(F32) + scale * q).astype(BF16)
        out_ref[c, rows:, :rows] = split_rows(to_rows(pair_sum(q) + pair_sum(q * unit), rows))
    small_ref[0:8, :] = gain
    small_ref[8:16, :] = bias


def input_back(counts, payload, scales, offsets, wt, grads, grad):
    chunks, tall, _ = payload.shape
    total = chunks * (tall - STAT_ROWS)
    return pl.pallas_call(
        input_back_kernel,
        grid=(1,),
        in_specs=[pl.BlockSpec(memory_space=pltpu.SMEM)]
        + [full_spec(a.shape) for a in (payload, scales, offsets, wt, grads, grad)],
        out_specs=[full_spec(payload.shape), full_spec((16, 384))],
        out_shape=[
            jax.ShapeDtypeStruct(payload.shape, BF16),
            jax.ShapeDtypeStruct((16, 384), F32),
        ],
        scratch_shapes=[pltpu.VMEM((3, total + 16, 384), F32)],
        compiler_params=VMEM,
        cost_estimate=work(3),
        name="input_back",
    )(counts, payload, scales, offsets, wt, grads, grad)


def mixer_grads_kernel(
    counts_ref,
    x_ref,
    scales_ref,
    offsets_ref,
    taps_ref,
    win_ref,
    grads_ref,
    grad_ref,
    conv_ref,
    short_ref,
    gin_ref,
    gtaps_ref,
    normed_ref,
    in_acc,
):
    chunks, tall, _ = x_ref.shape
    rows = tall - STAT_ROWS
    total = chunks * rows
    size = 512
    parts = gin_ref.shape[0]
    share = 192 // parts
    count_a, count_b = counts_ref[0], counts_ref[1]
    edge = jnp.zeros((8, 384), F32)
    normed_ref[0:8, :] = edge
    normed_ref[8 + total :, :] = edge
    for c in range(chunks):
        _, _, normed = normed_pair(x_ref[c], rows, scales_ref[...], offsets_ref[...])
        keep = position_mask(c * rows, rows, count_a, count_b)
        normed_ref[8 + c * rows : 8 + (c + 1) * rows, :] = normed * keep
    gout = jnp.zeros((192, 256), F32)
    for b in range(total // size):
        at = slice(size * b, size * (b + 1))
        wide_grads = jnp.concatenate([stacked(grads_ref[s, at, :]) for s in range(3)], axis=1)
        window = normed_ref[size * b : size * (b + 1) + 16, :]
        wide = jnp.concatenate([stacked(v).astype(BF16) for v in three_shifts(window, size)], axis=1)
        product = dot(wide.T, wide_grads)
        if b == 0:
            in_acc[...] = product
        else:
            in_acc[...] += product
        gated = (conv_ref[at, :].astype(F32) * short_ref[at, :].astype(F32)).astype(BF16)
        gout += fold_rows(dot(stacked(gated).T, stacked(grad_ref[at, :])))
    gout = fold_lanes(gout).astype(BF16)
    for d in range(parts):
        gin_ref[d, 3 * share :, :] = gout[share * d : share * (d + 1)]
    for s in range(3):
        lanes = slice(256 * s, 256 * (s + 1))
        total_in = jnp.zeros((192, 256), F32)
        for j in range(3):
            block = fold_lanes(fold_rows(in_acc[256 * j : 256 * (j + 1), lanes]))
            at = 3 * j + s
            total_in += block * taps_ref[at : at + 1, :]
            gtaps_ref[8 * at : 8 * (at + 1), :] = column_sums(block * win_ref[:, lanes].astype(F32))
        total_in = total_in.astype(BF16)
        for d in range(parts):
            gin_ref[d, share * s : share * (s + 1), :] = total_in[share * d : share * (d + 1)]


def mixer_grads(counts, payload, scales, offsets, taps, win, grads, grad, conv, short, parts):
    chunks, tall, _ = payload.shape
    total = chunks * (tall - STAT_ROWS)
    return pl.pallas_call(
        mixer_grads_kernel,
        grid=(1,),
        in_specs=[pl.BlockSpec(memory_space=pltpu.SMEM)]
        + [full_spec(a.shape) for a in (payload, scales, offsets, taps, win, grads, grad, conv)]
        + [pl.BlockSpec((None, total, 384), lambda i: (1, 0, 0))],
        out_specs=[full_spec((parts, 768 // parts, 256)), full_spec((72, 256))],
        out_shape=[
            jax.ShapeDtypeStruct((parts, 768 // parts, 256), BF16),
            jax.ShapeDtypeStruct((72, 256), F32),
        ],
        scratch_shapes=[pltpu.VMEM((total + 16, 384), F32), pltpu.VMEM((768, 768), F32)],
        compiler_params=VMEM,
        cost_estimate=work(1),
        name="mixer_grads",
    )(counts, payload, scales, offsets, taps, win, grads, grad, conv, short)


def filter_back_kernel(
    cross_ref,
    s1_ref,
    c1_ref,
    s2_ref,
    c2_ref,
    feat_ref,
    midt_ref,
    foutt_ref,
    rate_ref,
    third_ref,
    fourth_ref,
    gfin_ref,
    gmid_ref,
    gfout_ref,
    gbias_ref,
    work_ref,
    taps_ref,
):
    total = feat_ref.shape[0]
    step_rows = 256

    def second(k1, carry):
        work_ref[pl.ds(2 * k1, 2), :, :] = dot(third_ref[...], cross_ref[k1]).astype(BF16).reshape(2, COLS, 256)
        return carry

    lax.fori_loop(0, FREQ_ROWS, second, 0, unroll=True)

    def last(j, carry):
        start = pl.ds(pl.multiple_of(16 * j, 16), 16)
        part = work_ref[:, start, :].reshape(FREQ_ROWS * 32, 256)
        taps_ref[:, start, :] = dot(fourth_ref[j], part).reshape(FULL_ROWS, 16, 256)
        return carry

    lax.fori_loop(0, 8, last, 0, unroll=True)
    gfin_ref[...] = jnp.zeros_like(gfin_ref)
    gmid_ref[...] = jnp.zeros_like(gmid_ref)
    gfout_ref[...] = jnp.zeros_like(gfout_ref)
    gbias_ref[...] = jnp.zeros_like(gbias_ref)

    def one(i, carry):
        rows = pl.ds(pl.multiple_of(i * step_rows, step_rows), step_rows)
        lag = i * step_rows + lax.broadcasted_iota(jnp.int32, (step_rows, 256), 0)
        signed = jnp.where(lag < total // 2, lag, total - lag)
        distance = signed.astype(F32) * (2.0 / total)
        grad = taps_ref[pl.ds(2 * i, 2), :, :].reshape(step_rows, 256) * jnp.exp(-distance * rate_ref[...])
        grad = grad.astype(BF16)
        gfout_ref[...] += dot(s2_ref[rows, :].T, grad)
        grad_second = dot(grad, foutt_ref[...]) * (SINE_FREQ * c2_ref[rows, :].astype(F32))
        gbias_ref[8:16, :] += column_sums(grad_second)
        grad_second = grad_second.astype(BF16)
        gmid_ref[...] += dot(s1_ref[rows, :].T, grad_second)
        grad_first = dot(grad_second, midt_ref[...]) * (SINE_FREQ * c1_ref[rows, :].astype(F32))
        gbias_ref[0:8, :] += column_sums(grad_first)
        gfin_ref[...] += dot(feat_ref[rows, :].T, grad_first.astype(BF16))
        return carry

    lax.fori_loop(0, total // step_rows, one, 0, unroll=4)


def filter_back(cross, hidden, feats, midt, foutt, rate, third, fourth):
    return pl.pallas_call(
        filter_back_kernel,
        out_shape=[
            jax.ShapeDtypeStruct((16, 128), F32),
            jax.ShapeDtypeStruct((128, 128), F32),
            jax.ShapeDtypeStruct((128, 256), F32),
            jax.ShapeDtypeStruct((16, 128), F32),
        ],
        scratch_shapes=[
            pltpu.VMEM((2 * FREQ_ROWS, COLS, 256), BF16),
            pltpu.VMEM((FULL_ROWS, COLS, 256), F32),
        ],
        compiler_params=VMEM,
        cost_estimate=work(1),
        name="filter_back",
    )(cross, *hidden, feats, midt, foutt, rate, third, fourth)


def unpack_out_kernel(x_ref, out_ref):
    for even in (0, 2):
        a, b = unpack_pairs(x_ref[even].astype(F32), x_ref[even + 1].astype(F32))
        out_ref[0, :, 192 * even : 192 * even + 384] = a.astype(BF16)
        out_ref[1, :, 192 * even : 192 * even + 384] = b.astype(BF16)


def unpack_out(value):
    chunks, rows, _ = value.shape
    return pl.pallas_call(
        unpack_out_kernel,
        grid=(chunks // 4,),
        in_specs=[pl.BlockSpec((4, rows, 384), lambda i: (i, 0, 0))],
        out_specs=pl.BlockSpec((2, rows, 768), lambda i: (i, 0, 0)),
        out_shape=jax.ShapeDtypeStruct((chunks // 2, rows, 768), BF16),
        compiler_params=VMEM,
        cost_estimate=work(0.3),
        name="unpack_out",
    )(value)


def unpack_grad_kernel(x_ref, tokens_ref, out_ref):
    rows = tokens_ref.shape[1]
    sums = jnp.zeros((8, rows), F32)
    for block in range(4):
        sums += join_rows(x_ref[block, rows:, :rows])
    columns = to_columns(sums) * (1.0 / 768.0)
    wide = ([], [])
    for even in (0, 2):
        a, b = unpack_pairs(x_ref[even, :rows].astype(F32), x_ref[even + 1, :rows].astype(F32))
        wide[0].append(a)
        wide[1].append(b)
    for which in range(2):
        token = tokens_ref[which].astype(F32)
        mean, scale = row_stats(token)
        unit = (token - mean) * scale
        grad = jnp.concatenate(wide[which], axis=1)
        mean_q = columns[:, which : which + 1]
        mean_qh = columns[:, 2 + which : 3 + which]
        out_ref[which] = grad - scale * (mean_q + unit * mean_qh)


def unpack_grad(value, tokens):
    chunks, tall, _ = value.shape
    rows = tall - STAT_ROWS
    return pl.pallas_call(
        unpack_grad_kernel,
        grid=(chunks // 4,),
        in_specs=[
            pl.BlockSpec((4, tall, 384), lambda i: (i, 0, 0)),
            pl.BlockSpec((2, rows, 768), lambda i: (i, 0, 0)),
        ],
        out_specs=pl.BlockSpec((2, rows, 768), lambda i: (i, 0, 0)),
        out_shape=jax.ShapeDtypeStruct((chunks // 2, rows, 768), F32),
        compiler_params=VMEM,
        cost_estimate=work(4.7),
        name="unpack_grad",
    )(value, tokens)


def finish_ffn_kernel(block_ref, *refs):
    pieces, (up_ref, down_ref) = refs[:4], refs[4:]
    share = up_ref.shape[2]
    for r in range(4):
        at = lax.bitwise_xor(block_ref[0], r)
        for t in range(6):
            value = pieces[r][share * t : share * (t + 1), :].astype(F32)
            up_ref[t // 3, at, :, 256 * (t % 3) : 256 * (t % 3 + 1)] = value
        down_ref[at] = pieces[r][6 * share :, :192].astype(F32)


def finish_ffn(block, pieces):
    share = pieces[0].shape[0] // 10
    vmem = pl.BlockSpec(memory_space=pltpu.VMEM)
    return pl.pallas_call(
        finish_ffn_kernel,
        in_specs=[pl.BlockSpec(memory_space=pltpu.SMEM)] + [vmem] * 4,
        out_shape=[
            jax.ShapeDtypeStruct((2, 4, share, 768), F32),
            jax.ShapeDtypeStruct((4, 4 * share, 192), F32),
        ],
        cost_estimate=work(0.3),
        name="finish_ffn",
    )(block, *pieces)


def finish_mixer_kernel(block_ref, *refs):
    pieces, (in_ref, out_ref, mid_ref, fout_ref, rows_ref) = refs[:4], refs[4:]
    share = in_ref.shape[2]
    hidden = mid_ref.shape[0]
    start = 4 * share
    for r in range(4):
        at = lax.bitwise_xor(block_ref[0], r)
        for s in range(3):
            in_ref[s, at] = pieces[r][share * s : share * (s + 1), :192].astype(F32)
        out_ref[at] = pieces[r][3 * share : 4 * share, :192].astype(F32)
        fout_ref[at] = pieces[r][start + hidden : start + 2 * hidden, :192].astype(F32)
        rows_ref[at] = pieces[r][start + 2 * hidden :, :].astype(F32)
    mids = [piece[start : start + hidden, :128].astype(F32) for piece in pieces]
    mid_ref[...] = mids[0] + mids[1] + mids[2] + mids[3]


def finish_mixer(block, pieces, share, hidden):
    vmem = pl.BlockSpec(memory_space=pltpu.VMEM)
    rest = pieces[0].shape[0] - 4 * share - 2 * hidden
    return pl.pallas_call(
        finish_mixer_kernel,
        in_specs=[pl.BlockSpec(memory_space=pltpu.SMEM)] + [vmem] * 4,
        out_shape=[
            jax.ShapeDtypeStruct((3, 4, share, 192), F32),
            jax.ShapeDtypeStruct((4, share, 192), F32),
            jax.ShapeDtypeStruct((hidden, 128), F32),
            jax.ShapeDtypeStruct((4, hidden, 192), F32),
            jax.ShapeDtypeStruct((4, rest, 256), F32),
        ],
        cost_estimate=work(0.3),
        name="finish_mixer",
    )(block, *pieces)


def own_block_kernel(block_ref, in_ref, out_ref, up_ref, down_ref, order_ref, all_ref):
    share = out_ref.shape[1]
    pieces = [in_ref[i, 0] for i in range(3)] + [out_ref[0]]
    wide = [up_ref[g, 0, :, 256 * t : 256 * (t + 1)] for g in range(2) for t in range(3)]
    fill = lambda v: jnp.concatenate([v.astype(F32), jnp.zeros((v.shape[0], 64), F32)], axis=1)
    rows = [fill(v) for v in pieces] + [v.astype(F32) for v in wide] + [fill(down_ref[0])]
    all_ref[...] = jnp.concatenate(rows, axis=0).astype(BF16)


def own_block(block, in_weight, out_weight, up_weight, down_weight, order):
    share = out_weight.shape[1]
    width = out_weight.shape[2]
    return pl.pallas_call(
        own_block_kernel,
        grid_spec=pltpu.PrefetchScalarGridSpec(
            num_scalar_prefetch=1,
            grid=(1,),
            in_specs=[
                pl.BlockSpec((3, 1, share, width), lambda i, at: (0, at[0], 0, 0)),
                pl.BlockSpec((1, share, width), lambda i, at: (at[0], 0, 0)),
                pl.BlockSpec((2, 1, share, 4 * width), lambda i, at: (0, at[0], 0, 0)),
                pl.BlockSpec((1, 4 * share, width), lambda i, at: (at[0], 0, 0)),
                ANYWHERE,
            ],
            out_specs=pl.BlockSpec((14 * share, 256), lambda i, at: (0, 0)),
        ),
        out_shape=jax.ShapeDtypeStruct((14 * share, 256), BF16),
        compiler_params=VMEM,
        cost_estimate=work(0.5),
        name="own_block",
    )(block, in_weight, out_weight, up_weight, down_weight, order)


def lanes_twice(value):
    last = value[:, 128:]
    return jnp.concatenate(
        [value[:, :128], jnp.where(low_lanes(value.shape[0]), last, half_turn(last))], axis=1
    )


def rows_twice(value):
    return jnp.concatenate([value, value[128:192]], axis=0)


def whole_weights_kernel(
    all_ref, taps_ref, win_ref, wtaps_ref, wtapst_ref, wout_ref, woutt_ref, up_ref, upt_ref, down_ref, downt_ref
):
    count, tall, _ = all_ref.shape
    share = tall // 14
    parts = [all_ref[d].astype(F32) for d in range(count)]

    def assembled(start, size):
        return jnp.concatenate([part[start : start + size] for part in parts], axis=0)

    plain = jnp.concatenate([lanes_twice(assembled(share * s, share)) for s in range(3)], axis=1)
    win_ref[...] = plain.astype(BF16)
    for j in range(3):
        rows = slice(256 * j, 256 * (j + 1))
        scaled = rows_twice(plain * taps_ref[j : j + 1, :])
        wtaps_ref[rows, :] = scaled.astype(BF16)
        wtapst_ref[:, rows] = scaled.T.astype(BF16)
    out = rows_twice(lanes_twice(assembled(3 * share, share)))
    wout_ref[...] = out.astype(BF16)
    woutt_ref[...] = out.T.astype(BF16)
    for t in range(6):
        cols = slice(256 * t, 256 * (t + 1))
        up = rows_twice(assembled((4 + t) * share, share))
        up_ref[:, cols] = up.astype(BF16)
        upt_ref[cols, :] = up.T.astype(BF16)
    down = lanes_twice(assembled(10 * share, 4 * share))
    down_ref[...] = down.astype(BF16)
    downt_ref[...] = down.T.astype(BF16)


def whole_weights(gathered, taps):
    vmem = pl.BlockSpec(memory_space=pltpu.VMEM)
    shapes = ((192, 768), (768, 768), (768, 768), (256, 256), (256, 256))
    shapes += ((256, 1536), (1536, 256), (768, 256), (256, 768))
    return pl.pallas_call(
        whole_weights_kernel,
        in_specs=[vmem, vmem],
        out_shape=[jax.ShapeDtypeStruct(shape, BF16) for shape in shapes],
        compiler_params=VMEM,
        cost_estimate=work(1),
        name="whole_weights",
    )(gathered, taps)


def doubled(value, axis):
    return jnp.concatenate([value, lax.slice_in_dim(value, 128, 192, axis=axis)], axis=axis)


def pair_lanes(value):
    head, tail = value[:, :128], value[:, 128:]
    return jnp.concatenate([head, head, tail, tail], axis=1)


def unpair_lanes(value):
    return jnp.concatenate([value[:, :128] + value[:, 128:256], value[:, 256:320] + value[:, 320:]], axis=1)


def at_block(value, block, axis):
    return lax.dynamic_index_in_dim(value, block, axis=axis, keepdims=False)


def per_device(
    tokens,
    lengths,
    cotangent,
    norm_gain,
    norm_bias,
    in_weight,
    conv_taps,
    filter_in,
    filter_mid,
    filter_bias,
    filter_out,
    out_weight,
    up_weight,
    down_weight,
):
    count, rows, features = tokens.shape
    blocks = in_weight.shape[1]
    data_size = lax.axis_size("dp")
    seq_size = lax.axis_size("seq")
    total = rows * seq_size
    groups = seq_size // blocks
    place = lax.axis_index("seq")
    block = place % blocks
    group = place // blocks
    width = features // blocks
    data_at = lax.axis_index("dp")
    block_at = block.astype(jnp.int32).reshape(1)

    def exchange(value):
        return lax.all_to_all(value, "seq", 0, 0, tiled=True)

    def shared(value):
        out = [value]
        for r in range(1, blocks):
            out.append(lax.ppermute(value, "seq", [(i, i ^ r) for i in range(seq_size)]))
        return out

    def gathered(value):
        out = [value]
        for r in range(1, data_size):
            out.append(lax.ppermute(value, "dp", [(i, i ^ r) for i in range(data_size)]))
        every = jnp.stack(out)
        return jnp.concatenate([lax.dynamic_slice_in_dim(every, data_at ^ i, 1, axis=0) for i in range(data_size)])

    def scattered(value):
        total = at_block(value, data_at, 0).astype(F32)
        for r in range(1, data_size):
            sent = at_block(value, data_at ^ r, 0)
            total += lax.ppermute(sent, "dp", [(i, i ^ r) for i in range(data_size)]).astype(F32)
        return total

    def over_groups(value, *others):
        step = 1
        while step < groups:
            pairs = [(i, i ^ (step * blocks)) for i in range(seq_size)]
            sent = value.astype(BF16)
            if others:
                sent = after(sent, *others)
            value = sent.astype(F32) + lax.ppermute(sent, "seq", pairs).astype(F32)
            step *= 2
        return value.astype(BF16)

    fout_parts = []
    for q in range(groups):
        pairs = [(groups * (i % blocks) + (i // blocks + q) % groups, i) for i in range(seq_size)]
        fout_parts.append(lax.ppermute(filter_out, "seq", pairs))
    fout_every = jnp.stack(fout_parts)
    fout_block = jnp.concatenate(
        [at_block(fout_every, (i - group) % groups, 0) for i in range(groups)], axis=1
    )

    packed_tokens = after(pack_tokens(tokens), *fout_parts)
    payload = exchange(packed_tokens)
    counts = lax.dynamic_slice_in_dim(lengths, 2 * group, 2, axis=0)

    small = jnp.concatenate(
        [
            norm_gain.reshape(-1),
            norm_bias.reshape(-1),
            conv_taps.reshape(-1),
            filter_in.reshape(-1),
            filter_bias.reshape(-1),
            filter_mid.reshape(-1),
            fout_block.reshape(-1),
        ]
    )
    small_size = -(-small.shape[0] // 2048) * 2048
    small = jnp.pad(small, (0, small_size - small.shape[0])).reshape(-1, 128)
    small_all = gathered(small).reshape(data_size, small_size)
    shard = features // data_size
    hidden_shard = filter_in.shape[1]
    cuts = np.cumsum(
        [0, 2 * shard, 2 * shard, 9 * shard, 5 * hidden_shard, 2 * hidden_shard, 128 * hidden_shard, width * hidden_shard]
    )
    pieces = [small_all[:, cuts[i] : cuts[i + 1]] for i in range(7)]

    def channels(piece, lead):
        whole = jnp.moveaxis(piece.reshape(data_size, lead, shard), 0, 1).reshape(lead, features)
        return lax.dynamic_slice_in_dim(whole, block * width, width, axis=1).astype(F32)

    gains = pair_lanes(channels(pieces[0], 2))
    offsets = pair_lanes(channels(pieces[1], 2))
    taps = channels(pieces[2], 9)
    fin = jnp.moveaxis(pieces[3].reshape(data_size, 5, hidden_shard), 0, 1).reshape(5, 128)
    fbias = jnp.moveaxis(pieces[4].reshape(data_size, 2, hidden_shard), 0, 1).reshape(2, 128)
    fmid = pieces[5].reshape(128, 128)
    fout = doubled(pieces[6].reshape(128, width), 1)
    fin_stack = jnp.concatenate([fin, fin, fin, jnp.zeros((1, 128), BF16)], axis=0)
    channel_ids = block * width + jnp.arange(width, dtype=jnp.int32)
    fast, slow = math.log(100.0) / 0.3, math.log(100.0) / 1.5
    rates = slow + (fast - slow) * channel_ids.astype(F32) / float(features - 1)
    rates = doubled(rates[None, :], 1)

    part = width // data_size
    large = own_block(block_at, in_weight, out_weight, up_weight, down_weight, packed_tokens)
    large_all = lax.all_gather(large, "dp", axis=0, tiled=False)
    taps_wide = doubled(taps, 1).reshape(3, 768)
    w_in_flat, w_taps, w_taps_t, w_out, w_out_t, w_up, w_up_t, w_down, w_down_t = whole_weights(large_all, taps_wide)

    first_np, second_np = stage_tables()
    full_first = jnp.asarray(first_np, BF16)
    full_last = jnp.asarray(np.swapaxes(first_np, 1, 2), BF16)
    second = jnp.asarray(second_np, BF16)
    third = jnp.asarray(second_np.T, BF16)
    tables = (full_first, second, third, full_last)
    feats = jnp.asarray(lag_table(total), BF16)

    hidden = make_filter(
        feats,
        fin_stack,
        fbias.astype(F32),
        jnp.concatenate([fmid, fmid, fmid], axis=0),
        jnp.concatenate([fout, fout], axis=0),
        rates,
        full_first,
        second,
    )
    spectrum = hidden[4]
    hidden = hidden[:4]

    cot = exchange(after(pack_cotangent(cotangent, spectrum), payload))
    short, spec, conv, middle, stats = mixer_forward(
        counts, payload, gains[0:1], offsets[0:1], w_taps, w_out, spectrum, tables
    )

    out, pair_low, normed_low, unit, norm = feed_forward(
        middle, shared(stats), gains[1:2], offsets[1:2], w_up, w_down
    )
    out = exchange(after(out, cot))
    q, sums, ffn, small_two = feed_back(
        cot, pair_low, normed_low, unit, gains[1:2], w_up_t, w_down_t, data_size
    )
    sums = shared(sums)
    ffn = scattered(ffn).astype(BF16)

    grad, cross, grads = mixer_backward(
        counts, norm, sums, w_out_t, cot.reshape(total, 384), q, unit, conv, short, spec, spectrum, tables
    )
    ffn = over_groups(ffn)
    back, small_one = input_back(counts, payload, gains[0:1], offsets[0:1], w_taps_t, grads, grad)
    back = exchange(after(back, out, ffn))
    g_mixer, g_taps = mixer_grads(
        counts,
        payload,
        gains[0:1],
        offsets[0:1],
        jnp.pad(taps, ((0, 0), (0, 256 - width))),
        w_in_flat,
        grads,
        grad,
        conv,
        short,
        data_size,
    )
    out_tokens = unpack_out(out)
    grad_tokens = unpack_grad(back, tokens)
    grad_up, grad_down = finish_ffn(block_at, shared(ffn))
    g_fin, g_mid, g_fout, g_fbias = filter_back(
        after(cross, out_tokens), hidden, feats, fmid.T, fout.T, rates, third, full_last
    )

    def rows_of(value):
        return jnp.pad(value, ((0, 0), (0, 256 - value.shape[1])))

    sums_one = unpair_lanes(small_one.reshape(2, 8, 384).sum(axis=1))
    sums_two = unpair_lanes(small_two.reshape(2, 8, 384).sum(axis=1))
    sums_taps = g_taps.reshape(9, 8, 256).sum(axis=1)
    g_fin = g_fin[0:5] + g_fin[5:10] + g_fin[10:15]
    g_fbias = g_fbias.reshape(2, 8, 128).sum(axis=1)
    g_fout = g_fout[:, :192] + jnp.pad(g_fout[:, 192:], ((0, 0), (128, 0)))
    same = jnp.concatenate(
        [
            rows_of(sums_one[0:1]),
            rows_of(sums_two[0:1]),
            rows_of(sums_one[1:2]),
            rows_of(sums_two[1:2]),
            sums_taps,
            rows_of(g_fin),
            rows_of(g_fbias),
            jnp.zeros((12, 256), F32),
        ],
        axis=0,
    ).astype(BF16)
    own = jnp.concatenate(
        [
            g_mixer,
            rows_of(g_mid).astype(BF16).reshape(data_size, hidden_shard, 256),
            rows_of(g_fout).astype(BF16).reshape(data_size, hidden_shard, 256),
            jnp.broadcast_to(same[None], (data_size,) + same.shape),
        ],
        axis=1,
    )
    grad_in, grad_outw, grad_mid, grad_fout, rows = finish_mixer(
        block_at, shared(over_groups(scattered(own), back)), part, hidden_shard
    )
    grad_fout = jnp.moveaxis(grad_fout, 0, 1).reshape(hidden_shard, features)
    grad_fout = lax.dynamic_slice_in_dim(grad_fout, place * (features // seq_size), features // seq_size, axis=1)
    norms = jnp.moveaxis(rows[:, :13, :width], 0, 1).reshape(13, features)
    norms = lax.dynamic_slice_in_dim(norms, data_at * shard, shard, axis=1)
    filters = rows[:, 13:20, :128].sum(axis=0)
    filters = lax.dynamic_slice_in_dim(filters, data_at * hidden_shard, hidden_shard, axis=1)
    grad_fin, grad_fbias = filters[0:5], filters[5:7]
    return (
        out_tokens,
        grad_tokens,
        norms[0:2],
        norms[2:4],
        grad_in,
        norms[4:13].reshape(3, 3, shard),
        grad_fin,
        grad_mid,
        grad_fbias,
        grad_fout,
        grad_outw,
        grad_up,
        grad_down,
    )


def solution(mesh):
    placed = (
        P("dp", "seq", None),
        P("dp"),
        P("dp", "seq", None),
        P(None, "dp"),
        P(None, "dp"),
        P(None, None, "dp", None),
        P(None, None, "dp"),
        P(None, "dp"),
        P("dp", None),
        P(None, "dp"),
        P("dp", "seq"),
        P(None, "dp", None),
        P(None, None, "dp", None),
        P(None, "dp", None),
    )
    return jax.shard_map(
        per_device,
        mesh=mesh,
        in_specs=placed,
        out_specs=(
            P("dp", "seq", None),
            P("dp", "seq", None),
            P(None, "dp"),
            P(None, "dp"),
            P(None, None, "dp", None),
            P(None, None, "dp"),
            P(None, "dp"),
            P("dp", None),
            P(None, "dp"),
            P("dp", "seq"),
            P(None, "dp", None),
            P(None, None, "dp", None),
            P(None, "dp", None),
        ),
        check_vma=False,
    )
```

```python
import functools
import math

import jax
import jax.numpy as jnp
import numpy as np
from jax import lax
from jax.experimental import pallas as pl
from jax.experimental.pallas import tpu as pltpu
from jax.sharding import PartitionSpec as P

F32 = jnp.float32
BF16 = jnp.bfloat16
EPS = 1e-05
SINE_FREQ = 10.0
GROUP = 3
COLS = 128
HALF_ROWS = 16
FULL_ROWS = 32
FREQ_ROWS = 17
STAT_ROWS = 16
GROUPED = 2
VMEM = pltpu.CompilerParams(vmem_limit_bytes=56 * 1024 * 1024)
WIDE_VMEM = pltpu.CompilerParams(vmem_limit_bytes=60 * 1024 * 1024)


def stage_tables():
    k1 = np.arange(FREQ_ROWS)[:, None, None]
    t1 = np.arange(FULL_ROWS)[None, :, None]
    t2 = np.arange(COLS)[None, None, :]
    phase = 2.0 * np.pi * ((k1 * (t1 * COLS + t2)) % 4096) / 4096.0
    both = np.stack([np.cos(phase), -np.sin(phase)], axis=1)
    out = np.zeros((8, FREQ_ROWS, 2, 16, FULL_ROWS, 16), np.float32)
    for a in range(16):
        out[:, :, :, a, :, a] = np.moveaxis(both[..., a::16], -1, 0)
    first = out.reshape(8, FREQ_ROWS * 32, FULL_ROWS * 16)
    theta = 2.0 * np.pi * (np.outer(np.arange(COLS), np.arange(COLS)) % COLS) / COLS
    second = np.block([[np.cos(theta), np.sin(theta)], [-np.sin(theta), np.cos(theta)]])
    return first, second


def lag_table(seq_total):
    lags = np.arange(2 * seq_total)
    scaled = np.where(lags < seq_total, lags, lags - 2 * seq_total) / float(seq_total)
    feats = np.stack(
        [
            scaled,
            np.cos(np.pi * scaled),
            np.sin(np.pi * scaled),
            np.cos(2.0 * np.pi * scaled),
            np.sin(2.0 * np.pi * scaled),
        ],
        axis=1,
    ).astype(np.float32)
    parts, rest = [], feats
    for _ in range(3):
        piece = rest.astype(jnp.bfloat16)
        parts.append(piece.astype(np.float32))
        rest = rest - piece.astype(np.float32)
    table = np.zeros((2 * seq_total, 16), np.float32)
    table[:, :15] = np.concatenate(parts, axis=1)
    return table


def dot(a, b):
    return jnp.dot(a, b, preferred_element_type=F32)


def low_lanes(rows):
    return lax.broadcasted_iota(jnp.int32, (rows, 128), 1) < 64


def tiles(value):
    return [value[:, 128 * i : 128 * (i + 1)] for i in range(value.shape[1] // 128)]


def half_turn(value):
    return pltpu.roll(value, 64, axis=1)


def stacked(value):
    first, second, last = tiles(value)
    low = low_lanes(value.shape[0])
    zero = jnp.zeros_like(last)
    return jnp.concatenate(
        [
            jnp.concatenate([first, jnp.where(low, last, zero)], axis=1),
            jnp.concatenate([second, jnp.where(low, zero, last)], axis=1),
        ],
        axis=0,
    )


def packed(value):
    rows = value.shape[0] // 2
    low = low_lanes(rows)
    last = jnp.where(low, value[:rows, 128:], value[rows:, 128:])
    return jnp.concatenate([value[:rows, :128], value[rows:, :128], last], axis=1)


def pair_sum(value):
    first, second, last = tiles(value)
    low = low_lanes(value.shape[0])
    zero = jnp.zeros_like(last)
    return (
        jnp.sum(first + jnp.where(low, last, zero), axis=1, keepdims=True),
        jnp.sum(second + jnp.where(low, zero, last), axis=1, keepdims=True),
    )


def spread(col_a, col_b, rows):
    wide_a = jnp.broadcast_to(col_a, (rows, 128))
    wide_b = jnp.broadcast_to(col_b, (rows, 128))
    return jnp.concatenate([wide_a, wide_b, jnp.where(low_lanes(rows), wide_a, wide_b)], axis=1)


def to_rows(columns, rows):
    lane = lax.broadcasted_iota(jnp.int32, (rows, 128), 1)
    out = jnp.zeros((rows, 128), F32)
    for at, column in enumerate(columns):
        out = jnp.where(lane == at, jnp.broadcast_to(column, (rows, 128)), out)
    if rows % 128:
        out = jnp.concatenate([out, jnp.zeros((128 - rows, 128), F32)], axis=0)
    return out.T[:8, :rows]


def to_columns(values):
    rows = values.shape[1]
    if rows % 128:
        values = jnp.concatenate([values, jnp.zeros((8, 128 - rows), F32)], axis=1)
    tall = jnp.concatenate([values, jnp.zeros((120, values.shape[1]), F32)], axis=0)
    return tall.T[:rows]


def split_rows(values):
    high = values.astype(BF16).astype(F32)
    return jnp.concatenate([high, values - high], axis=0).astype(BF16)


def join_rows(values):
    wide = values.astype(F32)
    return wide[:8] + wide[8:]


def position_mask(start, rows, count_a, count_b):
    place = start + lax.broadcasted_iota(jnp.int32, (rows, 128), 0)
    keep_a = (place < count_a).astype(F32)
    keep_b = (place < count_b).astype(F32)
    return jnp.concatenate([keep_a, keep_b, jnp.where(low_lanes(rows), keep_a, keep_b)], axis=1)


def sine_pair(angle):
    turns = jnp.floor(angle * (1.0 / math.pi) + 0.5)
    rest = angle - turns * 3.140625
    rest = rest - turns * 9.675025939941406e-4
    rest = rest - turns * 1.5099579909783764e-7
    half = turns * 0.5
    sign = 1.0 - 4.0 * (half - jnp.floor(half))
    square = rest * rest
    sine = square * (-1.0 / 39916800.0) + 1.0 / 362880.0
    sine = sine * square - 1.0 / 5040.0
    sine = sine * square + 1.0 / 120.0
    sine = sine * square - 1.0 / 6.0
    sine = rest + rest * square * sine
    cosine = square * (1.0 / 479001600.0) - 1.0 / 3628800.0
    cosine = cosine * square + 1.0 / 40320.0
    cosine = cosine * square - 1.0 / 720.0
    cosine = cosine * square + 1.0 / 24.0
    cosine = cosine * square - 0.5
    cosine = 1.0 + square * cosine
    return sine * sign, cosine * sign


def normal_cdf(value):
    return 0.5 + 0.5 * lax.erf(value * math.sqrt(0.5))


def normal_density(value):
    return jnp.exp(value * value * -0.5) * (1.0 / math.sqrt(2.0 * math.pi))


def work(micros):
    return pl.CostEstimate(flops=int(micros * 1.15e9), bytes_accessed=0, transcendentals=0)


def pass_kernel(*refs):
    pass


def after(value, *others):
    anywhere = pl.BlockSpec(memory_space=pl.ANY)
    return pl.pallas_call(
        pass_kernel,
        in_specs=[anywhere] * (1 + len(others)),
        out_specs=anywhere,
        out_shape=jax.ShapeDtypeStruct(value.shape, value.dtype),
        input_output_aliases={0: 0},
        name="after",
    )(value, *others)


def pack_pair(a, b, block):
    rows = a.shape[0]
    low = low_lanes(rows)
    base = 3 * (block // 2)
    ta = [a[:, 128 * (base + i) : 128 * (base + i + 1)] for i in range(3)]
    tb = [b[:, 128 * (base + i) : 128 * (base + i + 1)] for i in range(3)]
    if block % 2 == 0:
        parts = [ta[0], tb[0], jnp.where(low, ta[1], half_turn(tb[1]))]
    else:
        parts = [
            jnp.where(low, half_turn(ta[1]), half_turn(ta[2])),
            jnp.where(low, half_turn(tb[1]), half_turn(tb[2])),
            jnp.where(low, half_turn(ta[2]), tb[2]),
        ]
    return jnp.concatenate(parts, axis=1)


def unpack_pairs(even, odd):
    low = low_lanes(even.shape[0])
    ea, eb, el = tiles(even)
    oa, ob, ol = tiles(odd)
    a = [ea, jnp.where(low, el, half_turn(oa)), jnp.where(low, half_turn(oa), half_turn(ol))]
    b = [eb, jnp.where(low, half_turn(el), half_turn(ob)), jnp.where(low, half_turn(ob), ol)]
    return jnp.concatenate(a, axis=1), jnp.concatenate(b, axis=1)


def row_stats(value):
    mean = jnp.mean(value, axis=1, keepdims=True)
    centred = value - mean
    variance = jnp.mean(centred * centred, axis=1, keepdims=True)
    return mean, lax.rsqrt(variance + EPS)


def pack_tokens_kernel(x_ref, out_ref):
    rows = x_ref.shape[1]
    a = x_ref[0].astype(F32)
    b = x_ref[1].astype(F32)
    stats = split_rows(to_rows(row_stats(a) + row_stats(b), rows))
    for block in range(4):
        out_ref[block, :rows, :] = pack_pair(a, b, block).astype(BF16)
        out_ref[block, rows:, :rows] = stats


def pack_tokens(tokens):
    count, rows, width = tokens.shape
    return pl.pallas_call(
        pack_tokens_kernel,
        grid=(count // 2,),
        in_specs=[pl.BlockSpec((2, rows, width), lambda i: (i, 0, 0))],
        out_specs=pl.BlockSpec((4, rows + STAT_ROWS, 384), lambda i: (i, 0, 0)),
        out_shape=jax.ShapeDtypeStruct((2 * count, rows + STAT_ROWS, 384), BF16),
        compiler_params=VMEM,
        cost_estimate=work(3.3),
        name="pack_tokens",
    )(tokens)


def pack_cotangent_kernel(x_ref, after_ref, out_ref):
    a = x_ref[0].astype(F32)
    b = x_ref[1].astype(F32)
    for block in range(4):
        out_ref[block] = pack_pair(a, b, block).astype(BF16)


def pack_cotangent(cotangent, after):
    count, rows, width = cotangent.shape
    return pl.pallas_call(
        pack_cotangent_kernel,
        grid=(count // 2,),
        in_specs=[
            pl.BlockSpec((2, rows, width), lambda i: (i, 0, 0)),
            pl.BlockSpec(memory_space=pl.ANY),
        ],
        out_specs=pl.BlockSpec((4, rows, 384), lambda i: (i, 0, 0)),
        out_shape=jax.ShapeDtypeStruct((2 * count, rows, 384), BF16),
        compiler_params=VMEM,
        cost_estimate=work(0.5),
        name="pack_cotangent",
    )(cotangent, after)


def transform_first(table_ref, data_ref, spec_ref):
    count, _, lanes = data_ref.shape

    def one(j, carry):
        start = pl.ds(pl.multiple_of(16 * j, 16), 16)
        block = data_ref[:, start, :].reshape(count * 16, lanes)
        part = dot(table_ref[j], block).astype(BF16)
        spec_ref[:, start, :] = part.reshape(2 * FREQ_ROWS, 16, lanes)
        return carry

    lax.fori_loop(0, 8, one, 0, unroll=True)


def frequency_weight(k1):
    edge = jnp.logical_or(k1 == 0, k1 == FREQ_ROWS - 1)
    return jnp.where(edge, 1.0 / 4096.0, 2.0 / 4096.0).astype(F32)


def make_filter_kernel(
    feat_ref,
    fin_ref,
    bias_ref,
    mid_ref,
    fout_ref,
    rate_ref,
    table_ref,
    second_ref,
    s1_ref,
    c1_ref,
    s2_ref,
    c2_ref,
    spec_ref,
    taps_ref,
    work_ref,
):
    step_rows = 256
    total = feat_ref.shape[0]

    def one(i, carry):
        rows = pl.ds(pl.multiple_of(i * step_rows, step_rows), step_rows)
        inner = dot(feat_ref[rows, :], fin_ref[...]) + bias_ref[0:1, :]
        s1, c1 = sine_pair(SINE_FREQ * inner)
        s1_ref[rows, :] = s1.astype(BF16)
        c1_ref[rows, :] = c1.astype(BF16)
        p1 = s1.astype(BF16)
        r1 = s1 - p1.astype(F32)
        p2 = r1.astype(BF16)
        p3 = (r1 - p2.astype(F32)).astype(BF16)
        outer = dot(jnp.concatenate([p1, p2, p3], axis=1), mid_ref[...]) + bias_ref[1:2, :]
        s2, c2 = sine_pair(SINE_FREQ * outer)
        s2_ref[rows, :] = s2.astype(BF16)
        c2_ref[rows, :] = c2.astype(BF16)
        q1 = s2.astype(BF16)
        q2 = (s2 - q1.astype(F32)).astype(BF16)
        raw = dot(jnp.concatenate([q1, q2], axis=1), fout_ref[...])
        lag = i * step_rows + lax.broadcasted_iota(jnp.int32, (step_rows, 256), 0)
        signed = jnp.where(lag < total // 2, lag, total - lag)
        distance = signed.astype(F32) * (2.0 / total)
        kernel = raw * jnp.exp(-distance * rate_ref[...])
        taps_ref[pl.ds(2 * i, 2), :, :] = kernel.astype(BF16).reshape(2, COLS, 256)
        return carry

    lax.fori_loop(0, total // step_rows, one, 0, unroll=True)
    transform_first(table_ref, taps_ref, work_ref)

    def second(k1, carry):
        part = work_ref[pl.ds(2 * k1, 2), :, :].reshape(256, 256)
        spec_ref[k1] = dot(second_ref[...], part) * frequency_weight(k1)
        return carry

    lax.fori_loop(0, FREQ_ROWS, second, 0, unroll=True)


def make_filter(feats, fin, bias, mid, fout, rate, table, second):
    total = feats.shape[0]
    hidden = jax.ShapeDtypeStruct((total, 128), BF16)
    return pl.pallas_call(
        make_filter_kernel,
        out_shape=(hidden,) * 4 + (jax.ShapeDtypeStruct((FREQ_ROWS, 256, 256), F32),),
        scratch_shapes=[
            pltpu.VMEM((FULL_ROWS, COLS, 256), BF16),
            pltpu.VMEM((2 * FREQ_ROWS, COLS, 256), BF16),
        ],
        compiler_params=VMEM,
        cost_estimate=work(2),
        name="make_filter",
    )(feats, fin, bias, mid, fout, rate, table, second)


def normed_pair(payload, rows, scales, offsets):
    value = payload[:rows].astype(F32)
    stats = to_columns(join_rows(payload[rows:, :rows]))
    mean = spread(stats[:, 0:1], stats[:, 2:3], rows)
    scale = spread(stats[:, 1:2], stats[:, 3:4], rows)
    unit = (value - mean) * scale
    return unit, scale, unit * scales + offsets


def filter_lanes(block):
    return jnp.concatenate([block[:, :128], block], axis=1)


def full_spec(shape):
    return pl.BlockSpec(shape, lambda i: (0,) * len(shape))


ANYWHERE = pl.BlockSpec(memory_space=pl.ANY)


def three_shifts(window, rows):
    return window[7 : 7 + rows], window[8 : 8 + rows], window[9 : 9 + rows]


def mixer_forward_kernel(
    counts_ref,
    x_ref,
    scales_ref,
    offsets_ref,
    w_ref,
    wout_ref,
    second_ref,
    third_ref,
    first_hbm,
    fourth_hbm,
    filter_hbm,
    short_hbm,
    spec_hbm,
    conv_hbm,
    middle_hbm,
    stats_ref,
    first_ref,
    fourth_ref,
    filter_ref,
    normed_ref,
    short_ref,
    values_ref,
    work_ref,
    spec_ref,
    conv_ref,
    gated_ref,
    middle_ref,
    in_sems,
    out_sems,
):
    chunks, tall, _ = x_ref.shape
    rows = tall - STAT_ROWS
    total = chunks * rows
    size = 256
    count_a, count_b = counts_ref[0], counts_ref[1]
    loads = [
        pltpu.make_async_copy(src, dst, in_sems.at[i])
        for i, (src, dst) in enumerate(
            (
                (first_hbm.at[:, :, pl.ds(0, HALF_ROWS * 16)], first_ref),
                (filter_hbm, filter_ref),
                (fourth_hbm.at[:, pl.ds(0, HALF_ROWS * 16), :], fourth_ref),
            )
        )
    ]
    stores = [
        pltpu.make_async_copy(src, dst, out_sems.at[i])
        for i, (src, dst) in enumerate(
            (
                (short_ref, short_hbm),
                (spec_ref, spec_hbm),
                (conv_ref, conv_hbm),
                (middle_ref, middle_hbm),
            )
        )
    ]
    for load in loads:
        load.start()

    edge = jnp.zeros((8, 384), F32)
    normed_ref[0:8, :] = edge
    normed_ref[8 + total :, :] = edge
    for c in range(chunks):
        _, _, normed = normed_pair(x_ref[c], rows, scales_ref[...], offsets_ref[...])
        keep = position_mask(c * rows, rows, count_a, count_b)
        normed_ref[8 + c * rows : 8 + (c + 1) * rows, :] = normed * keep
    for b in range(total // size):
        at = slice(size * b, size * (b + 1))
        window = normed_ref[size * b : size * (b + 1) + 16, :]
        wide = jnp.concatenate([stacked(v).astype(BF16) for v in three_shifts(window, size)], axis=1)
        out = dot(wide, w_ref[...])
        shorts = [packed(out[:, 256 * s : 256 * (s + 1)]) for s in range(3)]
        for s in range(3):
            short_ref[s, at, :] = shorts[s].astype(BF16)
        keep = position_mask(size * b, size, count_a, count_b)
        values = (shorts[2] * shorts[0] * keep).astype(BF16)
        values_ref[2 * b : 2 * b + 2, :, :] = values.reshape(2, COLS, 384)
    stores[0].start()

    loads[0].wait()
    transform_first(first_ref, values_ref, work_ref)
    loads[1].wait()

    def middle(k1, carry):
        part = work_ref[pl.ds(2 * k1, 2), :, :].reshape(256, 384)
        spec = dot(second_ref[...], part)
        spec_ref[k1] = spec.astype(BF16)
        re, im = spec[:128], spec[128:]
        block = filter_ref[k1]
        fre, fim = filter_lanes(block[:128]), filter_lanes(block[128:])
        prod = jnp.concatenate([re * fre - im * fim, re * fim + im * fre], axis=0).astype(BF16)
        work_ref[pl.ds(2 * k1, 2), :, :] = dot(third_ref[...], prod).astype(BF16).reshape(2, COLS, 384)
        return carry

    lax.fori_loop(0, FREQ_ROWS, middle, 0, unroll=True)
    stores[1].start()
    loads[2].wait()
    for j in range(8):
        part = work_ref[:, 16 * j : 16 * (j + 1), :].reshape(FREQ_ROWS * 32, 384)
        conv = dot(fourth_ref[j], part)
        for i in range(HALF_ROWS):
            at = slice(COLS * i + 16 * j, COLS * i + 16 * (j + 1))
            piece = conv[16 * i : 16 * (i + 1)]
            conv_ref[at, :] = piece.astype(BF16)
            gated_ref[at, :] = (piece * short_ref[1, at, :].astype(F32)).astype(BF16)
    stores[2].start()
    for c in range(chunks):
        at = slice(rows * c, rows * (c + 1))
        out = packed(dot(stacked(gated_ref[at, :]), wout_ref[...]))
        value = x_ref[c, :rows, :].astype(F32) + out
        middle_ref[at, :] = value
        sum_a, sum_b = pair_sum(value)
        mean_a, mean_b = sum_a * (1.0 / 192.0), sum_b * (1.0 / 192.0)
        centred = value - spread(mean_a, mean_b, rows)
        square_a, square_b = pair_sum(centred * centred)
        stats_ref[c] = to_rows((mean_a, square_a, mean_b, square_b), rows)
    stores[3].start()
    for store in stores:
        store.wait()


def mixer_forward(counts, payload, scales, offsets, weight, wout, spectrum, tables):
    chunks, tall, _ = payload.shape
    rows = tall - STAT_ROWS
    total = chunks * rows
    first, second, third, fourth = tables
    seq = (total, 384)
    wide = (FREQ_ROWS, 256, 384)
    return pl.pallas_call(
        mixer_forward_kernel,
        grid=(1,),
        in_specs=[pl.BlockSpec(memory_space=pltpu.SMEM)]
        + [full_spec(a.shape) for a in (payload, scales, offsets, weight, wout, second, third)]
        + [ANYWHERE] * 3,
        out_specs=[ANYWHERE] * 4 + [full_spec((chunks, 8, rows))],
        out_shape=[
            jax.ShapeDtypeStruct((3,) + seq, BF16),
            jax.ShapeDtypeStruct(wide, BF16),
            jax.ShapeDtypeStruct(seq, BF16),
            jax.ShapeDtypeStruct(seq, F32),
            jax.ShapeDtypeStruct((chunks, 8, rows), F32),
        ],
        scratch_shapes=[
            pltpu.VMEM(first.shape[:2] + (HALF_ROWS * 16,), BF16),
            pltpu.VMEM((8, HALF_ROWS * 16, fourth.shape[2]), BF16),
            pltpu.VMEM(spectrum.shape, F32),
            pltpu.VMEM((total + 16, 384), F32),
            pltpu.VMEM((3,) + seq, BF16),
            pltpu.VMEM((HALF_ROWS, COLS, 384), BF16),
            pltpu.VMEM((2 * FREQ_ROWS, COLS, 384), BF16),
            pltpu.VMEM(wide, BF16),
            pltpu.VMEM(seq, BF16),
            pltpu.VMEM(seq, BF16),
            pltpu.VMEM(seq, F32),
            pltpu.SemaphoreType.DMA((3,)),
            pltpu.SemaphoreType.DMA((4,)),
        ],
        compiler_params=VMEM,
        cost_estimate=work(25),
        name="mixer_forward",
    )(counts, payload, scales, offsets, weight, wout, second, third, first, fourth, spectrum)


def column_sums(value):
    return jnp.sum(value.reshape(value.shape[0] // 8, 8, value.shape[1]), axis=0)


def fold_rows(value):
    return jnp.concatenate([value[:128], value[128:192] + value[192:256]], axis=0)


def fold_lanes(value):
    last = value[:, 128:]
    summed = jnp.where(low_lanes(value.shape[0]), last + half_turn(last), jnp.zeros_like(last))
    return jnp.concatenate([value[:, :128], summed], axis=1)


def feed_forward_kernel(
    middle_ref,
    s0_ref,
    s1_ref,
    s2_ref,
    s3_ref,
    scales_ref,
    offsets_ref,
    up_ref,
    down_ref,
    out_ref,
    pair_ref,
    normed_ref,
    unit_ref,
    norm_ref,
):
    chunks, rows, _ = out_ref.shape
    for c in range(chunks):
        at_rows = slice(rows * c, rows * (c + 1))
        parts = [ref[c] for ref in (s0_ref, s1_ref, s2_ref, s3_ref)]
        mean = (parts[0] + parts[1] + parts[2] + parts[3]) * 0.25
        spread_sum = jnp.zeros_like(mean)
        for part in parts:
            gap = part - mean
            spread_sum += 192.0 * gap * gap
        squares = parts[0] + parts[1] + parts[2] + parts[3]
        scale_a = lax.rsqrt((squares[1:2] + spread_sum[0:1]) * (1.0 / 768.0) + EPS)
        scale_b = lax.rsqrt((squares[3:4] + spread_sum[2:3]) * (1.0 / 768.0) + EPS)
        norm = jnp.concatenate([mean[0:1], scale_a, mean[2:3], scale_b, jnp.zeros((4, rows), F32)], axis=0)
        norm_ref[c] = norm
        columns = to_columns(norm)
        middle = middle_ref[at_rows, :]
        unit = (middle - spread(columns[:, 0:1], columns[:, 2:3], rows)) * spread(columns[:, 1:2], columns[:, 3:4], rows)
        unit_ref[at_rows, :] = unit.astype(BF16)
        normed = stacked(unit * scales_ref[...] + offsets_ref[...]).astype(BF16)
        normed_ref[c] = normed
        hiddens = []
        width = 256
        for f in range(768 // width):
            at = slice(width * f, width * (f + 1))
            at_up = slice(768 + width * f, 768 + width * (f + 1))
            gate = dot(normed, up_ref[:, at])
            upper = dot(normed, up_ref[:, at_up])
            pair_ref[c, :, at] = gate.astype(BF16)
            pair_ref[c, :, at_up] = upper.astype(BF16)
            hiddens.append((gate * normal_cdf(gate) * upper).astype(BF16))
        down = dot(jnp.concatenate(hiddens, axis=1), down_ref[...])
        out_ref[c] = (middle + packed(down)).astype(BF16)


def feed_forward(middle, stats, scales, offsets, up, down):
    chunks, _, rows = stats[0].shape
    total = chunks * rows
    many = min(chunks, GROUPED)
    stat_spec = pl.BlockSpec((many, 8, rows), lambda i: (i, 0, 0))
    rows_spec = pl.BlockSpec((many * rows, 384), lambda i: (i, 0))
    return pl.pallas_call(
        feed_forward_kernel,
        grid=(chunks // many,),
        in_specs=[rows_spec] + [stat_spec] * 4 + [full_spec(a.shape) for a in (scales, offsets, up, down)],
        out_specs=[
            pl.BlockSpec((many, rows, 384), lambda i: (i, 0, 0)),
            pl.BlockSpec((many, 2 * rows, 1536), lambda i: (i, 0, 0)),
            pl.BlockSpec((many, 2 * rows, 256), lambda i: (i, 0, 0)),
            rows_spec,
            stat_spec,
        ],
        out_shape=[
            jax.ShapeDtypeStruct((chunks, rows, 384), BF16),
            jax.ShapeDtypeStruct((chunks, 2 * rows, 1536), BF16),
            jax.ShapeDtypeStruct((chunks, 2 * rows, 256), BF16),
            jax.ShapeDtypeStruct((total, 384), BF16),
            jax.ShapeDtypeStruct((chunks, 8, rows), F32),
        ],
        compiler_params=VMEM,
        cost_estimate=work(11),
        name="feed_forward",
    )(middle, *stats, scales, offsets, up, down)


def feed_back_kernel(
    cot_ref,
    pair_ref,
    normed_ref,
    unit_ref,
    scales_ref,
    upt_ref,
    downt_ref,
    q_ref,
    sums_ref,
    gffn_ref,
    small_ref,
    up_acc,
    down_acc,
):
    chunks, rows, _ = cot_ref.shape
    step = pl.program_id(0)

    @pl.when(step == 0)
    def _():
        small_ref[...] = jnp.zeros_like(small_ref)
        up_acc[...] = jnp.zeros_like(up_acc)
        down_acc[...] = jnp.zeros_like(down_acc)

    join = lambda parts: jnp.concatenate(parts, axis=0)
    cot = join([stacked(cot_ref[c]) for c in range(chunks)])
    size = 2 * rows * chunks
    grad_hidden = dot(cot, downt_ref[...])
    hidden, gates, uppers = [], [], []
    width = 256
    for f in range(768 // width):
        at = slice(width * f, width * (f + 1))
        at_up = slice(768 + width * f, 768 + width * (f + 1))
        gate = pair_ref[:, :, at].reshape(size, width).astype(F32)
        upper = pair_ref[:, :, at_up].reshape(size, width).astype(F32)
        cdf = normal_cdf(gate)
        active = gate * cdf
        hidden.append((active * upper).astype(BF16))
        gates.append((grad_hidden[:, at] * upper * (cdf + gate * normal_density(gate))).astype(BF16))
        uppers.append((grad_hidden[:, at] * active).astype(BF16))
    hidden = jnp.concatenate(hidden, axis=1)
    grads = jnp.concatenate(gates + uppers, axis=1)
    back = dot(grads, upt_ref[...])
    up_acc[...] += fold_rows(dot(normed_ref[...].reshape(size, 256).T, grads))
    down_acc[...] += dot(cot.T, hidden)
    for c in range(chunks):
        at_rows = slice(rows * c, rows * (c + 1))
        grad = packed(back[2 * rows * c : 2 * rows * (c + 1)])
        unit = unit_ref[at_rows, :].astype(F32)
        q = grad * scales_ref[...]
        q_ref[at_rows, :] = q.astype(BF16)
        sums_ref[c] = to_rows(pair_sum(q) + pair_sum(q * unit), rows)
        small_ref[0:8, :] += column_sums(grad * unit)
        small_ref[8:16, :] += column_sums(grad)

    @pl.when(step == pl.num_programs(0) - 1)
    def _():
        parts = gffn_ref.shape[0]
        share = 192 // parts
        down = fold_lanes(down_acc[...].T).astype(BF16)
        for d in range(parts):
            for t in range(6):
                value = up_acc[share * d : share * (d + 1), 256 * t : 256 * (t + 1)]
                gffn_ref[d, share * t : share * (t + 1), :] = value.astype(BF16)
            gffn_ref[d, 6 * share :, :] = down[4 * share * d : 4 * share * (d + 1)]


def feed_back(cot, pair, normed, unit, scales, upt, downt, parts):
    chunks, rows, _ = cot.shape
    total = chunks * rows
    many = min(chunks, GROUPED)
    rows_spec = pl.BlockSpec((many * rows, 384), lambda i: (i, 0))
    spec = lambda shape: pl.BlockSpec((many,) + shape[1:], lambda i: (i, 0, 0))
    stats = (chunks, 8, rows)
    return pl.pallas_call(
        feed_back_kernel,
        grid=(chunks // many,),
        in_specs=[spec(cot.shape), spec(pair.shape), spec(normed.shape), rows_spec]
        + [full_spec(a.shape) for a in (scales, upt, downt)],
        out_specs=[rows_spec, spec(stats), full_spec((parts, 1920 // parts, 256)), full_spec((16, 384))],
        out_shape=[
            jax.ShapeDtypeStruct((total, 384), BF16),
            jax.ShapeDtypeStruct(stats, F32),
            jax.ShapeDtypeStruct((parts, 1920 // parts, 256), BF16),
            jax.ShapeDtypeStruct((16, 384), F32),
        ],
        scratch_shapes=[pltpu.VMEM((192, 1536), F32), pltpu.VMEM((256, 768), F32)],
        compiler_params=VMEM,
        cost_estimate=work(2),
        name="feed_back",
    )(cot, pair, normed, unit, scales, upt, downt)


def mixer_backward_kernel(
    counts_ref,
    norm_ref,
    s0_ref,
    s1_ref,
    s2_ref,
    s3_ref,
    woutt_ref,
    second_ref,
    third_ref,
    scales_ref,
    offsets_ref,
    x_hbm,
    wt_hbm,
    cot_hbm,
    q_hbm,
    unit_hbm,
    conv_hbm,
    short_hbm,
    first_hbm,
    spec_hbm,
    filter_hbm,
    fourth_hbm,
    grad_hbm,
    cross_hbm,
    grads_hbm,
    out_ref,
    small_ref,
    x_ref,
    wt_ref,
    parts_ref,
    cot_ref,
    q_ref,
    unit_ref,
    conv_ref,
    short_ref,
    first_ref,
    spec_ref,
    filter_ref,
    fourth_ref,
    work_ref,
    cross_ref,
    grads_ref,
    in_sems,
    out_sems,
):
    chunks, _, rows = norm_ref.shape
    total = chunks * rows
    count_a, count_b = counts_ref[0], counts_ref[1]
    half = total // 2
    early, late = pl.ds(0, half), pl.ds(half, half)
    lanes = first_ref.shape[2]
    loads = [
        pltpu.make_async_copy(src, dst, in_sems.at[i])
        for i, (src, dst) in enumerate(
            [
                (src.at[part], dst.at[part])
                for part in (early, late)
                for src, dst in (
                    (cot_hbm, cot_ref),
                    (q_hbm, q_ref),
                    (unit_hbm, unit_ref),
                    (short_hbm.at[1], short_ref.at[1]),
                    (conv_hbm, conv_ref),
                )
            ]
            + [
                (first_hbm.at[:, :, pl.ds(0, lanes)], first_ref),
                (spec_hbm, spec_ref),
                (filter_hbm, filter_ref),
                (fourth_hbm.at[:, pl.ds(0, lanes), :], fourth_ref),
                (short_hbm.at[0], short_ref.at[0]),
                (short_hbm.at[2], short_ref.at[2]),
                (wt_hbm, wt_ref),
                (x_hbm, x_ref),
            ]
        )
    ]
    for load in loads:
        load.start()

    for c in range(chunks):
        if c == 0:
            for load in loads[0:5]:
                load.wait()
        if c == chunks // 2:
            for load in loads[5:10]:
                load.wait()
        at = slice(rows * c, rows * (c + 1))
        sums = (s0_ref[c] + s1_ref[c] + s2_ref[c] + s3_ref[c]) * (1.0 / 768.0)
        columns = to_columns(jnp.concatenate([sums[0:4], norm_ref[c][0:4]], axis=0))
        scale = spread(columns[:, 5:6], columns[:, 7:8], rows)
        mean_q = spread(columns[:, 0:1], columns[:, 1:2], rows)
        mean_qh = spread(columns[:, 2:3], columns[:, 3:4], rows)
        back = q_ref[at, :].astype(F32) - mean_q - unit_ref[at, :].astype(F32) * mean_qh
        grad = cot_ref[at, :].astype(F32) + scale * back
        cot_ref[at, :] = grad.astype(BF16)
        grad_gated = packed(dot(stacked(grad).astype(BF16), woutt_ref[...]))
        unit_ref[at, :] = (grad_gated * short_ref[1, at, :].astype(F32)).astype(BF16)
        grads_ref[1, at, :] = (grad_gated * conv_ref[at, :].astype(F32)).astype(BF16)
    stores = [
        pltpu.make_async_copy(src, dst, out_sems.at[i])
        for i, (src, dst) in enumerate(((cot_ref, grad_hbm), (cross_ref, cross_hbm), (grads_ref, grads_hbm)))
    ]
    stores[0].start()

    loads[10].wait()
    for j in range(8):
        block = jnp.concatenate(
            [unit_ref[COLS * i + 16 * j : COLS * i + 16 * (j + 1), :] for i in range(HALF_ROWS)], axis=0
        )
        part = dot(first_ref[j], block).astype(BF16)
        work_ref[:, 16 * j : 16 * (j + 1), :] = part.reshape(2 * FREQ_ROWS, 16, 384)
    for load in loads[11:13]:
        load.wait()

    def middle(k1, carry):
        part = work_ref[pl.ds(2 * k1, 2), :, :].reshape(256, 384)
        grad = dot(second_ref[...], part)
        re, im = grad[:128], grad[128:]
        spec = spec_ref[k1].astype(F32)
        vre, vim = spec[:128], spec[128:]
        cre = re * vre + im * vim
        cim = im * vre - re * vim
        weight = frequency_weight(k1)
        fold = lambda v: jnp.concatenate([v[:, :128] + v[:, 128:256], v[:, 256:]], axis=1)
        cross_ref[k1] = (jnp.concatenate([fold(cre), fold(cim)], axis=0) * weight).astype(BF16)
        block = filter_ref[k1]
        fre, fim = filter_lanes(block[:128]), filter_lanes(block[128:])
        prod = jnp.concatenate([re * fre + im * fim, im * fre - re * fim], axis=0).astype(BF16)
        work_ref[pl.ds(2 * k1, 2), :, :] = dot(third_ref[...], prod).astype(BF16).reshape(2, COLS, 384)
        return carry

    lax.fori_loop(0, FREQ_ROWS, middle, 0, unroll=True)
    stores[1].start()
    for load in loads[13:]:
        load.wait()
    for j in range(8):
        part = work_ref[:, 16 * j : 16 * (j + 1), :].reshape(FREQ_ROWS * 32, 384)
        grad_values = dot(fourth_ref[j], part)
        for i in range(HALF_ROWS):
            start = COLS * i + 16 * j
            at = slice(start, start + 16)
            piece = grad_values[16 * i : 16 * (i + 1)] * position_mask(start, 16, count_a, count_b)
            grads_ref[0, at, :] = (piece * short_ref[2, at, :].astype(F32)).astype(BF16)
            grads_ref[2, at, :] = (piece * short_ref[0, at, :].astype(F32)).astype(BF16)
    stores[2].start()

    size = 512
    edge = jnp.zeros((8, 384), F32)
    for j in range(3):
        parts_ref[j, 0:8, :] = edge
        parts_ref[j, 8 + total :, :] = edge
    for b in range(total // size):
        at = slice(size * b, size * (b + 1))
        wide = jnp.concatenate([stacked(grads_ref[s, at, :]) for s in range(3)], axis=1)
        out = dot(wide, wt_ref[...])
        for j in range(3):
            parts_ref[j, 8 + size * b : 8 + size * (b + 1), :] = packed(out[:, 256 * j : 256 * (j + 1)])
    gain = jnp.zeros((8, 384), F32)
    bias = jnp.zeros((8, 384), F32)
    for c in range(chunks):
        at = slice(rows * c, rows * (c + 1))
        ahead = parts_ref[0, rows * c : rows * (c + 1) + 16, :][9 : 9 + rows]
        here = parts_ref[1, 8 + rows * c : 8 + rows * (c + 1), :]
        behind = parts_ref[2, rows * c : rows * (c + 1) + 16, :][7 : 7 + rows]
        keep = position_mask(c * rows, rows, count_a, count_b)
        grad_normed = (ahead + here + behind) * keep
        unit, scale, _ = normed_pair(x_ref[c], rows, scales_ref[...], offsets_ref[...])
        gain += column_sums(grad_normed * unit)
        bias += column_sums(grad_normed)
        q = grad_normed * scales_ref[...]
        out_ref[c, :rows, :] = (cot_ref[at, :].astype(F32) + scale * q).astype(BF16)
        out_ref[c, rows:, :rows] = split_rows(to_rows(pair_sum(q) + pair_sum(q * unit), rows))
    small_ref[0:8, :] = gain
    small_ref[8:16, :] = bias
    for store in stores:
        store.wait()


def mixer_backward(
    counts, norm, sums, woutt, scales, offsets, payload, wt, cot, q, unit, conv, short, spec, spectrum, tables
):
    chunks, _, rows = norm.shape
    total = chunks * rows
    first, second, third, fourth = tables
    lanes = HALF_ROWS * 16
    seq = (total, 384)
    cross = (FREQ_ROWS, 256, 256)
    blocked = [norm, *sums, woutt, second, third, scales, offsets]
    return pl.pallas_call(
        mixer_backward_kernel,
        grid=(1,),
        in_specs=[pl.BlockSpec(memory_space=pltpu.SMEM)]
        + [full_spec(a.shape) for a in blocked]
        + [ANYWHERE] * 11,
        out_specs=[ANYWHERE] * 3 + [full_spec(payload.shape), full_spec((16, 384))],
        out_shape=[
            jax.ShapeDtypeStruct(seq, BF16),
            jax.ShapeDtypeStruct(cross, BF16),
            jax.ShapeDtypeStruct((3,) + seq, BF16),
            jax.ShapeDtypeStruct(payload.shape, BF16),
            jax.ShapeDtypeStruct((16, 384), F32),
        ],
        scratch_shapes=[
            pltpu.VMEM(payload.shape, BF16),
            pltpu.VMEM(wt.shape, BF16),
            pltpu.VMEM((3, total + 16, 384), F32),
        ]
        + [pltpu.VMEM(seq, BF16)] * 4
        + [
            pltpu.VMEM((3,) + seq, BF16),
            pltpu.VMEM(first.shape[:2] + (lanes,), BF16),
            pltpu.VMEM(spec.shape, BF16),
            pltpu.VMEM(spectrum.shape, F32),
            pltpu.VMEM((8, lanes, fourth.shape[2]), BF16),
            pltpu.VMEM((2 * FREQ_ROWS, COLS, 384), BF16),
            pltpu.VMEM(cross, BF16),
            pltpu.VMEM((3,) + seq, BF16),
            pltpu.SemaphoreType.DMA((18,)),
            pltpu.SemaphoreType.DMA((3,)),
        ],
        compiler_params=WIDE_VMEM,
        cost_estimate=work(4),
        name="mixer_backward",
    )(counts, *blocked, payload, wt, cot, q, unit, conv, short, first, spec, spectrum, fourth)


def mixer_grads_kernel(
    counts_ref,
    x_ref,
    scales_ref,
    offsets_ref,
    taps_ref,
    win_ref,
    grads_ref,
    grad_ref,
    conv_ref,
    short_ref,
    gin_ref,
    gtaps_ref,
    normed_ref,
    in_acc,
):
    chunks, tall, _ = x_ref.shape
    rows = tall - STAT_ROWS
    total = chunks * rows
    size = 512
    parts = gin_ref.shape[0]
    share = 192 // parts
    count_a, count_b = counts_ref[0], counts_ref[1]
    edge = jnp.zeros((8, 384), F32)
    normed_ref[0:8, :] = edge
    normed_ref[8 + total :, :] = edge
    for c in range(chunks):
        _, _, normed = normed_pair(x_ref[c], rows, scales_ref[...], offsets_ref[...])
        keep = position_mask(c * rows, rows, count_a, count_b)
        normed_ref[8 + c * rows : 8 + (c + 1) * rows, :] = normed * keep
    gout = jnp.zeros((192, 256), F32)
    for b in range(total // size):
        at = slice(size * b, size * (b + 1))
        wide_grads = jnp.concatenate([stacked(grads_ref[s, at, :]) for s in range(3)], axis=1)
        window = normed_ref[size * b : size * (b + 1) + 16, :]
        wide = jnp.concatenate([stacked(v).astype(BF16) for v in three_shifts(window, size)], axis=1)
        product = dot(wide.T, wide_grads)
        if b == 0:
            in_acc[...] = product
        else:
            in_acc[...] += product
        gated = (conv_ref[at, :].astype(F32) * short_ref[at, :].astype(F32)).astype(BF16)
        gout += fold_rows(dot(stacked(gated).T, stacked(grad_ref[at, :])))
    gout = fold_lanes(gout).astype(BF16)
    for d in range(parts):
        gin_ref[d, 3 * share :, :] = gout[share * d : share * (d + 1)]
    for s in range(3):
        lanes = slice(256 * s, 256 * (s + 1))
        total_in = jnp.zeros((192, 256), F32)
        for j in range(3):
            block = fold_lanes(fold_rows(in_acc[256 * j : 256 * (j + 1), lanes]))
            at = 3 * j + s
            total_in += block * taps_ref[at : at + 1, :]
            gtaps_ref[8 * at : 8 * (at + 1), :] = column_sums(block * win_ref[:, lanes].astype(F32))
        total_in = total_in.astype(BF16)
        for d in range(parts):
            gin_ref[d, share * s : share * (s + 1), :] = total_in[share * d : share * (d + 1)]


def mixer_grads(counts, payload, scales, offsets, taps, win, grads, grad, conv, short, parts):
    chunks, tall, _ = payload.shape
    total = chunks * (tall - STAT_ROWS)
    return pl.pallas_call(
        mixer_grads_kernel,
        grid=(1,),
        in_specs=[pl.BlockSpec(memory_space=pltpu.SMEM)]
        + [full_spec(a.shape) for a in (payload, scales, offsets, taps, win, grads, grad, conv)]
        + [pl.BlockSpec((None, total, 384), lambda i: (1, 0, 0))],
        out_specs=[full_spec((parts, 768 // parts, 256)), full_spec((72, 256))],
        out_shape=[
            jax.ShapeDtypeStruct((parts, 768 // parts, 256), BF16),
            jax.ShapeDtypeStruct((72, 256), F32),
        ],
        scratch_shapes=[pltpu.VMEM((total + 16, 384), F32), pltpu.VMEM((768, 768), F32)],
        compiler_params=VMEM,
        cost_estimate=work(0.01),
        name="mixer_grads",
    )(counts, payload, scales, offsets, taps, win, grads, grad, conv, short)


def filter_back_kernel(
    cross_ref,
    s1_ref,
    c1_ref,
    s2_ref,
    c2_ref,
    feat_ref,
    midt_ref,
    foutt_ref,
    rate_ref,
    third_ref,
    fourth_ref,
    mixer_ref,
    gtaps_ref,
    small_one_ref,
    small_two_ref,
    own_ref,
    gfin_ref,
    gmid_ref,
    gfout_ref,
    gbias_ref,
    work_ref,
    taps_ref,
):
    total = feat_ref.shape[0]
    step_rows = 256

    def second(k1, carry):
        work_ref[pl.ds(2 * k1, 2), :, :] = dot(third_ref[...], cross_ref[k1]).astype(BF16).reshape(2, COLS, 256)
        return carry

    lax.fori_loop(0, FREQ_ROWS, second, 0, unroll=True)

    def last(j, carry):
        start = pl.ds(pl.multiple_of(16 * j, 16), 16)
        part = work_ref[:, start, :].reshape(FREQ_ROWS * 32, 256)
        taps_ref[:, start, :] = dot(fourth_ref[j], part).reshape(FULL_ROWS, 16, 256)
        return carry

    lax.fori_loop(0, 8, last, 0, unroll=True)
    gfin_ref[...] = jnp.zeros_like(gfin_ref)
    gmid_ref[...] = jnp.zeros_like(gmid_ref)
    gfout_ref[...] = jnp.zeros_like(gfout_ref)
    gbias_ref[...] = jnp.zeros_like(gbias_ref)

    def one(i, carry):
        rows = pl.ds(pl.multiple_of(i * step_rows, step_rows), step_rows)
        lag = i * step_rows + lax.broadcasted_iota(jnp.int32, (step_rows, 256), 0)
        signed = jnp.where(lag < total // 2, lag, total - lag)
        distance = signed.astype(F32) * (2.0 / total)
        grad = taps_ref[pl.ds(2 * i, 2), :, :].reshape(step_rows, 256) * jnp.exp(-distance * rate_ref[...])
        grad = grad.astype(BF16)
        gfout_ref[...] += dot(s2_ref[rows, :].T, grad)
        grad_second = dot(grad, foutt_ref[...]) * (SINE_FREQ * c2_ref[rows, :].astype(F32))
        gbias_ref[8:16, :] += column_sums(grad_second)
        grad_second = grad_second.astype(BF16)
        gmid_ref[...] += dot(s1_ref[rows, :].T, grad_second)
        grad_first = dot(grad_second, midt_ref[...]) * (SINE_FREQ * c1_ref[rows, :].astype(F32))
        gbias_ref[0:8, :] += column_sums(grad_first)
        gfin_ref[...] += dot(feat_ref[rows, :].T, grad_first.astype(BF16))
        return carry

    lax.fori_loop(0, total // step_rows, one, 0, unroll=True)


    parts, tall, _ = mixer_ref.shape
    hidden = 128 // parts
    wide = lambda v: jnp.concatenate([v, jnp.zeros((v.shape[0], 128), F32)], axis=1)
    mid = wide(gmid_ref[...]).astype(BF16)
    fout = fold_lanes(gfout_ref[...]).astype(BF16)

    def channel_row(rows):
        row = jnp.sum(rows, axis=0, keepdims=True)
        joined = jnp.concatenate([row[:, :128] + row[:, 128:256], row[:, 256:]], axis=1)
        return fold_lanes(joined)

    same = [
        channel_row(small_one_ref[0:8, :]),
        channel_row(small_two_ref[0:8, :]),
        channel_row(small_one_ref[8:16, :]),
        channel_row(small_two_ref[8:16, :]),
    ]
    same += [jnp.sum(gtaps_ref[8 * i : 8 * (i + 1), :], axis=0, keepdims=True) for i in range(9)]
    same += [wide(gfin_ref[0:5, :] + gfin_ref[5:10, :] + gfin_ref[10:15, :])]
    same += [wide(jnp.sum(gbias_ref[8 * i : 8 * (i + 1), :], axis=0, keepdims=True)) for i in range(2)]
    same += [jnp.zeros((12, 256), F32)]
    same = jnp.concatenate(same, axis=0).astype(BF16)
    for d in range(parts):
        own_ref[d, :tall, :] = mixer_ref[d]
        own_ref[d, tall : tall + hidden, :] = mid[hidden * d : hidden * (d + 1)]
        own_ref[d, tall + hidden : tall + 2 * hidden, :] = fout[hidden * d : hidden * (d + 1)]
        own_ref[d, tall + 2 * hidden :, :] = same


def filter_back(cross, hidden, feats, midt, foutt, rate, third, fourth, mixer, gtaps, small_one, small_two):
    parts, tall, _ = mixer.shape
    return pl.pallas_call(
        filter_back_kernel,
        out_shape=jax.ShapeDtypeStruct((parts, tall + 256 // parts + 32, 256), BF16),
        scratch_shapes=[
            pltpu.VMEM((16, 128), F32),
            pltpu.VMEM((128, 128), F32),
            pltpu.VMEM((128, 256), F32),
            pltpu.VMEM((16, 128), F32),
            pltpu.VMEM((2 * FREQ_ROWS, COLS, 256), BF16),
            pltpu.VMEM((FULL_ROWS, COLS, 256), F32),
        ],
        compiler_params=VMEM,
        cost_estimate=work(0.01),
        name="filter_back",
    )(cross, *hidden, feats, midt, foutt, rate, third, fourth, mixer, gtaps, small_one, small_two)


def unpack_out_kernel(x_ref, out_ref):
    for even in (0, 2):
        a, b = unpack_pairs(x_ref[even].astype(F32), x_ref[even + 1].astype(F32))
        out_ref[0, :, 192 * even : 192 * even + 384] = a.astype(BF16)
        out_ref[1, :, 192 * even : 192 * even + 384] = b.astype(BF16)


def unpack_out(value):
    chunks, rows, _ = value.shape
    return pl.pallas_call(
        unpack_out_kernel,
        grid=(chunks // 4,),
        in_specs=[pl.BlockSpec((4, rows, 384), lambda i: (i, 0, 0))],
        out_specs=pl.BlockSpec((2, rows, 768), lambda i: (i, 0, 0)),
        out_shape=jax.ShapeDtypeStruct((chunks // 2, rows, 768), BF16),
        compiler_params=VMEM,
        cost_estimate=work(0.01),
        name="unpack_out",
    )(value)


def unpack_grad_kernel(x_ref, tokens_ref, out_ref):
    rows = tokens_ref.shape[1]
    sums = jnp.zeros((8, rows), F32)
    for block in range(4):
        sums += join_rows(x_ref[block, rows:, :rows])
    columns = to_columns(sums) * (1.0 / 768.0)
    wide = ([], [])
    for even in (0, 2):
        a, b = unpack_pairs(x_ref[even, :rows].astype(F32), x_ref[even + 1, :rows].astype(F32))
        wide[0].append(a)
        wide[1].append(b)
    for which in range(2):
        token = tokens_ref[which].astype(F32)
        mean, scale = row_stats(token)
        unit = (token - mean) * scale
        grad = jnp.concatenate(wide[which], axis=1)
        mean_q = columns[:, which : which + 1]
        mean_qh = columns[:, 2 + which : 3 + which]
        out_ref[which] = grad - scale * (mean_q + unit * mean_qh)


def unpack_grad(value, tokens):
    chunks, tall, _ = value.shape
    rows = tall - STAT_ROWS
    return pl.pallas_call(
        unpack_grad_kernel,
        grid=(chunks // 4,),
        in_specs=[
            pl.BlockSpec((4, tall, 384), lambda i: (i, 0, 0)),
            pl.BlockSpec((2, rows, 768), lambda i: (i, 0, 0)),
        ],
        out_specs=pl.BlockSpec((2, rows, 768), lambda i: (i, 0, 0)),
        out_shape=jax.ShapeDtypeStruct((chunks // 2, rows, 768), F32),
        compiler_params=VMEM,
        cost_estimate=work(8),
        name="unpack_grad",
    )(value, tokens)


def finish_ffn_kernel(block_ref, *refs):
    pieces, (up_ref, down_ref) = refs[:4], refs[4:]
    share = up_ref.shape[2]
    for r in range(4):
        at = lax.bitwise_xor(block_ref[0], r)
        for t in range(6):
            value = pieces[r][share * t : share * (t + 1), :].astype(F32)
            up_ref[t // 3, at, :, 256 * (t % 3) : 256 * (t % 3 + 1)] = value
        down_ref[at] = pieces[r][6 * share :, :192].astype(F32)


def finish_ffn(block, pieces):
    share = pieces[0].shape[0] // 10
    vmem = pl.BlockSpec(memory_space=pltpu.VMEM)
    return pl.pallas_call(
        finish_ffn_kernel,
        in_specs=[pl.BlockSpec(memory_space=pltpu.SMEM)] + [vmem] * 4,
        out_shape=[
            jax.ShapeDtypeStruct((2, 4, share, 768), F32),
            jax.ShapeDtypeStruct((4, 4 * share, 192), F32),
        ],
        cost_estimate=work(0.01),
        name="finish_ffn",
    )(block, *pieces)


def finish_mixer_kernel(place_ref, *refs):
    pieces, outs = refs[:4], refs[4:]
    in_ref, out_ref, mid_ref, gain_ref, bias_ref, taps_ref, fin_ref, fbias_ref, fout_ref = outs
    share = in_ref.shape[2]
    hidden, shard, cols = mid_ref.shape[0], gain_ref.shape[1], fout_ref.shape[1]
    block, chan_block, chan_start, hidden_start, fout_block, fout_start = [place_ref[i] for i in range(6)]
    start = 4 * share

    def turned(value, shift):
        return pltpu.roll(value, lax.rem(256 - shift, 256), axis=1)

    def of_block(rows, which):
        total = jnp.zeros((rows.stop - rows.start, 256), F32)
        for r in range(4):
            take = lax.bitwise_xor(block, r) == which
            total += jnp.where(take, pieces[r][rows, :].astype(F32), 0.0)
        return total

    for r in range(4):
        at = lax.bitwise_xor(block, r)
        for s in range(3):
            in_ref[s, at] = pieces[r][share * s : share * (s + 1), :192].astype(F32)
        out_ref[at] = pieces[r][3 * share : 4 * share, :192].astype(F32)
    mids = [piece[start : start + hidden, :128].astype(F32) for piece in pieces]
    mid_ref[...] = mids[0] + mids[1] + mids[2] + mids[3]
    fouts = of_block(slice(start + hidden, start + 2 * hidden), fout_block)
    fout_ref[...] = turned(fouts, fout_start)[:, :cols]
    rest = slice(start + 2 * hidden, start + 2 * hidden + 32)
    rows = turned(of_block(rest, chan_block), chan_start)[:, :shard]
    gain_ref[...] = rows[0:2]
    bias_ref[...] = rows[2:4]
    for j in range(3):
        taps_ref[j] = rows[4 + 3 * j : 7 + 3 * j]
    total = pieces[0][rest, :].astype(F32)
    for piece in pieces[1:]:
        total += piece[rest, :].astype(F32)
    filters = turned(total, hidden_start)[:, :hidden]
    fin_ref[...] = filters[13:18]
    fbias_ref[...] = filters[18:20]


def finish_mixer(place, pieces, share, hidden, shard, cols):
    vmem = pl.BlockSpec(memory_space=pltpu.VMEM)
    shapes = ((3, 4, share, 192), (4, share, 192), (hidden, 128), (2, shard), (2, shard))
    shapes += ((3, 3, shard), (5, hidden), (2, hidden), (hidden, cols))
    return pl.pallas_call(
        finish_mixer_kernel,
        in_specs=[pl.BlockSpec(memory_space=pltpu.SMEM)] + [vmem] * 4,
        out_shape=[jax.ShapeDtypeStruct(shape, F32) for shape in shapes],
        compiler_params=VMEM,
        cost_estimate=work(0.01),
        name="finish_mixer",
    )(place, *pieces)


def own_block_kernel(block_ref, in_ref, out_ref, up_ref, down_ref, order_ref, all_ref):
    share = out_ref.shape[1]
    pieces = [in_ref[i, 0] for i in range(3)] + [out_ref[0]]
    wide = [up_ref[g, 0, :, 256 * t : 256 * (t + 1)] for g in range(2) for t in range(3)]
    fill = lambda v: jnp.concatenate([v.astype(F32), jnp.zeros((v.shape[0], 64), F32)], axis=1)
    rows = [fill(v) for v in pieces] + [v.astype(F32) for v in wide] + [fill(down_ref[0])]
    all_ref[...] = jnp.concatenate(rows, axis=0).astype(BF16)


def own_block(block, in_weight, out_weight, up_weight, down_weight, order):
    share = out_weight.shape[1]
    width = out_weight.shape[2]
    return pl.pallas_call(
        own_block_kernel,
        grid_spec=pltpu.PrefetchScalarGridSpec(
            num_scalar_prefetch=1,
            grid=(1,),
            in_specs=[
                pl.BlockSpec((3, 1, share, width), lambda i, at: (0, at[0], 0, 0)),
                pl.BlockSpec((1, share, width), lambda i, at: (at[0], 0, 0)),
                pl.BlockSpec((2, 1, share, 4 * width), lambda i, at: (0, at[0], 0, 0)),
                pl.BlockSpec((1, 4 * share, width), lambda i, at: (at[0], 0, 0)),
                ANYWHERE,
            ],
            out_specs=pl.BlockSpec((14 * share, 256), lambda i, at: (0, 0)),
        ),
        out_shape=jax.ShapeDtypeStruct((14 * share, 256), BF16),
        compiler_params=VMEM,
        cost_estimate=work(0.5),
        name="own_block",
    )(block, in_weight, out_weight, up_weight, down_weight, order)


def lanes_twice(value):
    last = value[:, 128:]
    return jnp.concatenate(
        [value[:, :128], jnp.where(low_lanes(value.shape[0]), last, half_turn(last))], axis=1
    )


def rows_twice(value):
    return jnp.concatenate([value, value[128:192]], axis=0)


def whole_weights_kernel(
    all_ref, taps_ref, win_ref, wtaps_ref, wtapst_ref, wout_ref, woutt_ref, up_ref, upt_ref, down_ref, downt_ref
):
    count, tall, _ = all_ref.shape
    share = tall // 14
    parts = [all_ref[d].astype(F32) for d in range(count)]

    def assembled(start, size):
        return jnp.concatenate([part[start : start + size] for part in parts], axis=0)

    plain = jnp.concatenate([lanes_twice(assembled(share * s, share)) for s in range(3)], axis=1)
    win_ref[...] = plain.astype(BF16)
    for j in range(3):
        rows = slice(256 * j, 256 * (j + 1))
        scaled = rows_twice(plain * taps_ref[j : j + 1, :])
        wtaps_ref[rows, :] = scaled.astype(BF16)
        wtapst_ref[:, rows] = scaled.T.astype(BF16)
    out = rows_twice(lanes_twice(assembled(3 * share, share)))
    wout_ref[...] = out.astype(BF16)
    woutt_ref[...] = out.T.astype(BF16)
    for t in range(6):
        cols = slice(256 * t, 256 * (t + 1))
        up = rows_twice(assembled((4 + t) * share, share))
        up_ref[:, cols] = up.astype(BF16)
        upt_ref[cols, :] = up.T.astype(BF16)
    down = lanes_twice(assembled(10 * share, 4 * share))
    down_ref[...] = down.astype(BF16)
    downt_ref[...] = down.T.astype(BF16)


def whole_weights(gathered, taps):
    vmem = pl.BlockSpec(memory_space=pltpu.VMEM)
    shapes = ((192, 768), (768, 768), (768, 768), (256, 256), (256, 256))
    shapes += ((256, 1536), (1536, 256), (768, 256), (256, 768))
    return pl.pallas_call(
        whole_weights_kernel,
        in_specs=[vmem, vmem],
        out_shape=[jax.ShapeDtypeStruct(shape, BF16) for shape in shapes],
        compiler_params=VMEM,
        cost_estimate=work(1),
        name="whole_weights",
    )(gathered, taps)


def doubled(value, axis):
    return jnp.concatenate([value, lax.slice_in_dim(value, 128, 192, axis=axis)], axis=axis)


def pair_lanes(value):
    head, tail = value[:, :128], value[:, 128:]
    return jnp.concatenate([head, head, tail, tail], axis=1)


def at_block(value, block, axis):
    return lax.dynamic_index_in_dim(value, block, axis=axis, keepdims=False)


def per_device(
    tokens,
    lengths,
    cotangent,
    norm_gain,
    norm_bias,
    in_weight,
    conv_taps,
    filter_in,
    filter_mid,
    filter_bias,
    filter_out,
    out_weight,
    up_weight,
    down_weight,
):
    count, rows, features = tokens.shape
    blocks = in_weight.shape[1]
    data_size = lax.axis_size("dp")
    seq_size = lax.axis_size("seq")
    total = rows * seq_size
    groups = seq_size // blocks
    place = lax.axis_index("seq")
    block = place % blocks
    group = place // blocks
    width = features // blocks
    data_at = lax.axis_index("dp")
    block_at = block.astype(jnp.int32).reshape(1)

    def exchange(value):
        return lax.all_to_all(value, "seq", 0, 0, tiled=True)

    def shared(value):
        out = [value]
        for r in range(1, blocks):
            out.append(lax.ppermute(value, "seq", [(i, i ^ r) for i in range(seq_size)]))
        return out

    def gathered(value):
        out = [value]
        for r in range(1, data_size):
            out.append(lax.ppermute(value, "dp", [(i, i ^ r) for i in range(data_size)]))
        every = jnp.stack(out)
        return jnp.concatenate([lax.dynamic_slice_in_dim(every, data_at ^ i, 1, axis=0) for i in range(data_size)])

    def scattered(value):
        total = at_block(value, data_at, 0).astype(F32)
        for r in range(1, data_size):
            sent = at_block(value, data_at ^ r, 0)
            total += lax.ppermute(sent, "dp", [(i, i ^ r) for i in range(data_size)]).astype(F32)
        return total

    def over_groups(value, *others):
        step = 1
        while step < groups:
            pairs = [(i, i ^ (step * blocks)) for i in range(seq_size)]
            sent = value.astype(BF16)
            received = lax.ppermute(sent, "seq", pairs)
            if others:
                received = after(received, *others)
            value = sent.astype(F32) + received.astype(F32)
            step *= 2
        return value.astype(BF16)

    fout_parts = []
    for q in range(groups):
        pairs = [(groups * (i % blocks) + (i // blocks + q) % groups, i) for i in range(seq_size)]
        fout_parts.append(lax.ppermute(filter_out, "seq", pairs))
    fout_every = jnp.stack(fout_parts)
    fout_block = jnp.concatenate(
        [at_block(fout_every, (i - group) % groups, 0) for i in range(groups)], axis=1
    )

    packed_tokens = after(pack_tokens(tokens), *fout_parts)
    payload = exchange(packed_tokens)
    counts = lax.dynamic_slice_in_dim(lengths, 2 * group, 2, axis=0)

    small = jnp.concatenate(
        [
            norm_gain.reshape(-1),
            norm_bias.reshape(-1),
            conv_taps.reshape(-1),
            filter_in.reshape(-1),
            filter_bias.reshape(-1),
            filter_mid.reshape(-1),
            fout_block.reshape(-1),
        ]
    )
    small_size = -(-small.shape[0] // 2048) * 2048
    small = jnp.pad(small, (0, small_size - small.shape[0])).reshape(-1, 128)
    small_all = gathered(small).reshape(data_size, small_size)
    shard = features // data_size
    hidden_shard = filter_in.shape[1]
    cuts = np.cumsum(
        [0, 2 * shard, 2 * shard, 9 * shard, 5 * hidden_shard, 2 * hidden_shard, 128 * hidden_shard, width * hidden_shard]
    )
    pieces = [small_all[:, cuts[i] : cuts[i + 1]] for i in range(7)]

    def channels(piece, lead):
        whole = jnp.moveaxis(piece.reshape(data_size, lead, shard), 0, 1).reshape(lead, features)
        return lax.dynamic_slice_in_dim(whole, block * width, width, axis=1).astype(F32)

    gains = pair_lanes(channels(pieces[0], 2))
    offsets = pair_lanes(channels(pieces[1], 2))
    taps = channels(pieces[2], 9)
    fin = jnp.moveaxis(pieces[3].reshape(data_size, 5, hidden_shard), 0, 1).reshape(5, 128)
    fbias = jnp.moveaxis(pieces[4].reshape(data_size, 2, hidden_shard), 0, 1).reshape(2, 128)
    fmid = pieces[5].reshape(128, 128)
    fout = doubled(pieces[6].reshape(128, width), 1)
    fin_stack = jnp.concatenate([fin, fin, fin, jnp.zeros((1, 128), BF16)], axis=0)
    channel_ids = block * width + jnp.arange(width, dtype=jnp.int32)
    fast, slow = math.log(100.0) / 0.3, math.log(100.0) / 1.5
    rates = slow + (fast - slow) * channel_ids.astype(F32) / float(features - 1)
    rates = doubled(rates[None, :], 1)

    part = width // data_size
    large = own_block(block_at, in_weight, out_weight, up_weight, down_weight, packed_tokens)
    large_all = lax.all_gather(large, "dp", axis=0, tiled=False)
    taps_wide = doubled(taps, 1).reshape(3, 768)
    w_in_flat, w_taps, w_taps_t, w_out, w_out_t, w_up, w_up_t, w_down, w_down_t = whole_weights(large_all, taps_wide)

    first_np, second_np = stage_tables()
    full_first = jnp.asarray(first_np, BF16)
    full_last = jnp.asarray(np.swapaxes(first_np, 1, 2), BF16)
    second = jnp.asarray(second_np, BF16)
    third = jnp.asarray(second_np.T, BF16)
    tables = (full_first, second, third, full_last)
    feats = jnp.asarray(lag_table(total), BF16)

    hidden = make_filter(
        feats,
        fin_stack,
        fbias.astype(F32),
        jnp.concatenate([fmid, fmid, fmid], axis=0),
        jnp.concatenate([fout, fout], axis=0),
        rates,
        full_first,
        second,
    )
    spectrum = hidden[4]
    hidden = hidden[:4]

    cot = exchange(after(pack_cotangent(cotangent, spectrum), payload))
    short, spec, conv, middle, stats = mixer_forward(
        counts, payload, gains[0:1], offsets[0:1], w_taps, w_out, spectrum, tables
    )

    out, pair_low, normed_low, unit, norm = feed_forward(
        middle, shared(stats), gains[1:2], offsets[1:2], w_up, w_down
    )
    out = exchange(after(out, cot))
    q, sums, ffn, small_two = feed_back(
        cot, pair_low, normed_low, unit, gains[1:2], w_up_t, w_down_t, data_size
    )
    sums = shared(sums)
    ffn = scattered(ffn).astype(BF16)

    grad, cross, grads, back, small_one = mixer_backward(
        counts,
        norm,
        sums,
        w_out_t,
        gains[0:1],
        offsets[0:1],
        payload,
        w_taps_t,
        cot.reshape(total, 384),
        q,
        unit,
        conv,
        short,
        spec,
        spectrum,
        tables,
    )
    ffn = over_groups(ffn)
    back = exchange(after(back, out, ffn))
    ffn_pieces = shared(ffn)
    g_mixer, g_taps = mixer_grads(
        counts,
        payload,
        gains[0:1],
        offsets[0:1],
        jnp.pad(taps, ((0, 0), (0, 256 - width))),
        w_in_flat,
        grads,
        grad,
        conv,
        short,
        data_size,
    )
    out_tokens = unpack_out(out)
    grad_tokens = unpack_grad(back, tokens)
    own = filter_back(
        cross, hidden, feats, fmid.T, fout.T, rates, third, full_last, g_mixer, g_taps, small_one, small_two
    )
    own = over_groups(after(scattered(own).astype(BF16), out_tokens), grad_tokens)
    cols = features // seq_size
    places = [
        block,
        data_at * shard // width,
        data_at * shard % width,
        data_at * hidden_shard,
        place // groups,
        place % groups * cols,
    ]
    finished = finish_mixer(jnp.stack(places).astype(jnp.int32), shared(own), part, hidden_shard, shard, cols)
    grad_in, grad_outw, grad_mid, grad_gain, grad_bias, grad_taps, grad_fin, grad_fbias, grad_fout = finished
    grad_up, grad_down = finish_ffn(block_at, [after(ffn_pieces[0], own)] + ffn_pieces[1:])
    return (
        out_tokens,
        grad_tokens,
        grad_gain,
        grad_bias,
        grad_in,
        grad_taps,
        grad_fin,
        grad_mid,
        grad_fbias,
        grad_fout,
        grad_outw,
        grad_up,
        grad_down,
    )


def solution(mesh):
    placed = (
        P("dp", "seq", None),
        P("dp"),
        P("dp", "seq", None),
        P(None, "dp"),
        P(None, "dp"),
        P(None, None, "dp", None),
        P(None, None, "dp"),
        P(None, "dp"),
        P("dp", None),
        P(None, "dp"),
        P("dp", "seq"),
        P(None, "dp", None),
        P(None, None, "dp", None),
        P(None, "dp", None),
    )
    return jax.shard_map(
        per_device,
        mesh=mesh,
        in_specs=placed,
        out_specs=(
            P("dp", "seq", None),
            P("dp", "seq", None),
            P(None, "dp"),
            P(None, "dp"),
            P(None, None, "dp", None),
            P(None, None, "dp"),
            P(None, "dp"),
            P("dp", None),
            P(None, "dp"),
            P("dp", "seq"),
            P(None, "dp", None),
            P(None, None, "dp", None),
            P(None, "dp", None),
        ),
        check_vma=False,
    )
```

```python
import functools
import math

import jax
import jax.numpy as jnp
import numpy as np
from jax import lax
from jax.experimental import pallas as pl
from jax.experimental.pallas import tpu as pltpu
from jax.sharding import PartitionSpec as P

F32 = jnp.float32
BF16 = jnp.bfloat16
EPS = 1e-05
SINE_FREQ = 10.0
GROUP = 3
COLS = 128
HALF_ROWS = 16
FULL_ROWS = 32
FREQ_ROWS = 17
STAT_ROWS = 16
GROUPED = 2
VMEM = pltpu.CompilerParams(vmem_limit_bytes=56 * 1024 * 1024)
WIDE_VMEM = pltpu.CompilerParams(vmem_limit_bytes=60 * 1024 * 1024)


def stage_tables():
    k1 = np.arange(FREQ_ROWS)[:, None, None]
    t1 = np.arange(FULL_ROWS)[None, :, None]
    t2 = np.arange(COLS)[None, None, :]
    phase = 2.0 * np.pi * ((k1 * (t1 * COLS + t2)) % 4096) / 4096.0
    both = np.stack([np.cos(phase), -np.sin(phase)], axis=1)
    out = np.zeros((8, FREQ_ROWS, 2, 16, FULL_ROWS, 16), np.float32)
    for a in range(16):
        out[:, :, :, a, :, a] = np.moveaxis(both[..., a::16], -1, 0)
    first = out.reshape(8, FREQ_ROWS * 32, FULL_ROWS * 16)
    theta = 2.0 * np.pi * (np.outer(np.arange(COLS), np.arange(COLS)) % COLS) / COLS
    second = np.block([[np.cos(theta), np.sin(theta)], [-np.sin(theta), np.cos(theta)]])
    return first, second


def lag_table(seq_total):
    lags = np.arange(2 * seq_total)
    scaled = np.where(lags < seq_total, lags, lags - 2 * seq_total) / float(seq_total)
    feats = np.stack(
        [
            scaled,
            np.cos(np.pi * scaled),
            np.sin(np.pi * scaled),
            np.cos(2.0 * np.pi * scaled),
            np.sin(2.0 * np.pi * scaled),
        ],
        axis=1,
    ).astype(np.float32)
    parts, rest = [], feats
    for _ in range(3):
        piece = rest.astype(jnp.bfloat16)
        parts.append(piece.astype(np.float32))
        rest = rest - piece.astype(np.float32)
    table = np.zeros((2 * seq_total, 16), np.float32)
    table[:, :15] = np.concatenate(parts, axis=1)
    return table


def dot(a, b):
    return jnp.dot(a, b, preferred_element_type=F32)


def low_lanes(rows):
    return lax.broadcasted_iota(jnp.int32, (rows, 128), 1) < 64


def tiles(value):
    return [value[:, 128 * i : 128 * (i + 1)] for i in range(value.shape[1] // 128)]


def half_turn(value):
    return pltpu.roll(value, 64, axis=1)


def stacked(value):
    first, second, last = tiles(value)
    low = low_lanes(value.shape[0])
    zero = jnp.zeros_like(last)
    return jnp.concatenate(
        [
            jnp.concatenate([first, jnp.where(low, last, zero)], axis=1),
            jnp.concatenate([second, jnp.where(low, zero, last)], axis=1),
        ],
        axis=0,
    )


def packed(value):
    rows = value.shape[0] // 2
    low = low_lanes(rows)
    last = jnp.where(low, value[:rows, 128:], value[rows:, 128:])
    return jnp.concatenate([value[:rows, :128], value[rows:, :128], last], axis=1)


def pair_sum(value):
    first, second, last = tiles(value)
    low = low_lanes(value.shape[0])
    zero = jnp.zeros_like(last)
    return (
        jnp.sum(first + jnp.where(low, last, zero), axis=1, keepdims=True),
        jnp.sum(second + jnp.where(low, zero, last), axis=1, keepdims=True),
    )


def spread(col_a, col_b, rows):
    wide_a = jnp.broadcast_to(col_a, (rows, 128))
    wide_b = jnp.broadcast_to(col_b, (rows, 128))
    return jnp.concatenate([wide_a, wide_b, jnp.where(low_lanes(rows), wide_a, wide_b)], axis=1)


def to_rows(columns, rows):
    lane = lax.broadcasted_iota(jnp.int32, (rows, 128), 1)
    out = jnp.zeros((rows, 128), F32)
    for at, column in enumerate(columns):
        out = jnp.where(lane == at, jnp.broadcast_to(column, (rows, 128)), out)
    if rows % 128:
        out = jnp.concatenate([out, jnp.zeros((128 - rows, 128), F32)], axis=0)
    return out.T[:8, :rows]


def to_columns(values):
    rows = values.shape[1]
    if rows % 128:
        values = jnp.concatenate([values, jnp.zeros((8, 128 - rows), F32)], axis=1)
    tall = jnp.concatenate([values, jnp.zeros((120, values.shape[1]), F32)], axis=0)
    return tall.T[:rows]


def split_rows(values):
    high = values.astype(BF16).astype(F32)
    return jnp.concatenate([high, values - high], axis=0).astype(BF16)


def join_rows(values):
    wide = values.astype(F32)
    return wide[:8] + wide[8:]


def position_mask(start, rows, count_a, count_b):
    place = start + lax.broadcasted_iota(jnp.int32, (rows, 128), 0)
    keep_a = (place < count_a).astype(F32)
    keep_b = (place < count_b).astype(F32)
    return jnp.concatenate([keep_a, keep_b, jnp.where(low_lanes(rows), keep_a, keep_b)], axis=1)


def sine_pair(angle):
    turns = jnp.floor(angle * (1.0 / math.pi) + 0.5)
    rest = angle - turns * 3.140625
    rest = rest - turns * 9.675025939941406e-4
    rest = rest - turns * 1.5099579909783764e-7
    half = turns * 0.5
    sign = 1.0 - 4.0 * (half - jnp.floor(half))
    square = rest * rest
    sine = square * (-1.0 / 39916800.0) + 1.0 / 362880.0
    sine = sine * square - 1.0 / 5040.0
    sine = sine * square + 1.0 / 120.0
    sine = sine * square - 1.0 / 6.0
    sine = rest + rest * square * sine
    cosine = square * (1.0 / 479001600.0) - 1.0 / 3628800.0
    cosine = cosine * square + 1.0 / 40320.0
    cosine = cosine * square - 1.0 / 720.0
    cosine = cosine * square + 1.0 / 24.0
    cosine = cosine * square - 0.5
    cosine = 1.0 + square * cosine
    return sine * sign, cosine * sign


def normal_cdf(value):
    return 0.5 + 0.5 * lax.erf(value * math.sqrt(0.5))


def normal_density(value):
    return jnp.exp(value * value * -0.5) * (1.0 / math.sqrt(2.0 * math.pi))


def work(micros):
    return pl.CostEstimate(flops=int(micros * 1.15e9), bytes_accessed=0, transcendentals=0)


def pass_kernel(*refs):
    pass


def after(value, *others):
    anywhere = pl.BlockSpec(memory_space=pl.ANY)
    return pl.pallas_call(
        pass_kernel,
        in_specs=[anywhere] * (1 + len(others)),
        out_specs=anywhere,
        out_shape=jax.ShapeDtypeStruct(value.shape, value.dtype),
        input_output_aliases={0: 0},
        name="after",
    )(value, *others)


def pack_pair(a, b, block):
    rows = a.shape[0]
    low = low_lanes(rows)
    base = 3 * (block // 2)
    ta = [a[:, 128 * (base + i) : 128 * (base + i + 1)] for i in range(3)]
    tb = [b[:, 128 * (base + i) : 128 * (base + i + 1)] for i in range(3)]
    if block % 2 == 0:
        parts = [ta[0], tb[0], jnp.where(low, ta[1], half_turn(tb[1]))]
    else:
        parts = [
            jnp.where(low, half_turn(ta[1]), half_turn(ta[2])),
            jnp.where(low, half_turn(tb[1]), half_turn(tb[2])),
            jnp.where(low, half_turn(ta[2]), tb[2]),
        ]
    return jnp.concatenate(parts, axis=1)


def unpack_pairs(even, odd):
    low = low_lanes(even.shape[0])
    ea, eb, el = tiles(even)
    oa, ob, ol = tiles(odd)
    a = [ea, jnp.where(low, el, half_turn(oa)), jnp.where(low, half_turn(oa), half_turn(ol))]
    b = [eb, jnp.where(low, half_turn(el), half_turn(ob)), jnp.where(low, half_turn(ob), ol)]
    return jnp.concatenate(a, axis=1), jnp.concatenate(b, axis=1)


def row_stats(value):
    mean = jnp.mean(value, axis=1, keepdims=True)
    centred = value - mean
    variance = jnp.mean(centred * centred, axis=1, keepdims=True)
    return mean, lax.rsqrt(variance + EPS)


def pack_tokens_kernel(x_ref, out_ref):
    rows = x_ref.shape[1]
    a = x_ref[0].astype(F32)
    b = x_ref[1].astype(F32)
    stats = split_rows(to_rows(row_stats(a) + row_stats(b), rows))
    for block in range(4):
        out_ref[block, :rows, :] = pack_pair(a, b, block).astype(BF16)
        out_ref[block, rows:, :rows] = stats


def pack_tokens(tokens):
    count, rows, width = tokens.shape
    return pl.pallas_call(
        pack_tokens_kernel,
        grid=(count // 2,),
        in_specs=[pl.BlockSpec((2, rows, width), lambda i: (i, 0, 0))],
        out_specs=pl.BlockSpec((4, rows + STAT_ROWS, 384), lambda i: (i, 0, 0)),
        out_shape=jax.ShapeDtypeStruct((2 * count, rows + STAT_ROWS, 384), BF16),
        compiler_params=VMEM,
        cost_estimate=work(3.3),
        name="pack_tokens",
    )(tokens)


def pack_cotangent_kernel(x_ref, after_ref, out_ref):
    a = x_ref[0].astype(F32)
    b = x_ref[1].astype(F32)
    for block in range(4):
        out_ref[block] = pack_pair(a, b, block).astype(BF16)


def pack_cotangent(cotangent, after):
    count, rows, width = cotangent.shape
    return pl.pallas_call(
        pack_cotangent_kernel,
        grid=(count // 2,),
        in_specs=[
            pl.BlockSpec((2, rows, width), lambda i: (i, 0, 0)),
            pl.BlockSpec(memory_space=pl.ANY),
        ],
        out_specs=pl.BlockSpec((4, rows, 384), lambda i: (i, 0, 0)),
        out_shape=jax.ShapeDtypeStruct((2 * count, rows, 384), BF16),
        compiler_params=VMEM,
        cost_estimate=work(0.5),
        name="pack_cotangent",
    )(cotangent, after)


def transform_first(table_ref, data_ref, spec_ref):
    count, _, lanes = data_ref.shape

    def one(j, carry):
        start = pl.ds(pl.multiple_of(16 * j, 16), 16)
        block = data_ref[:, start, :].reshape(count * 16, lanes)
        part = dot(table_ref[j], block).astype(BF16)
        spec_ref[:, start, :] = part.reshape(2 * FREQ_ROWS, 16, lanes)
        return carry

    lax.fori_loop(0, 8, one, 0, unroll=True)


def frequency_weight(k1):
    edge = jnp.logical_or(k1 == 0, k1 == FREQ_ROWS - 1)
    return jnp.where(edge, 1.0 / 4096.0, 2.0 / 4096.0).astype(F32)


def make_filter_kernel(
    feat_ref,
    fin_ref,
    bias_ref,
    mid_ref,
    fout_ref,
    rate_ref,
    table_ref,
    second_ref,
    s1_ref,
    c1_ref,
    s2_ref,
    c2_ref,
    spec_ref,
    taps_ref,
    work_ref,
):
    step_rows = 256
    total = feat_ref.shape[0]

    def one(i, carry):
        rows = pl.ds(pl.multiple_of(i * step_rows, step_rows), step_rows)
        inner = dot(feat_ref[rows, :], fin_ref[...]) + bias_ref[0:1, :]
        s1, c1 = sine_pair(SINE_FREQ * inner)
        s1_ref[rows, :] = s1.astype(BF16)
        c1_ref[rows, :] = c1.astype(BF16)
        p1 = s1.astype(BF16)
        r1 = s1 - p1.astype(F32)
        p2 = r1.astype(BF16)
        p3 = (r1 - p2.astype(F32)).astype(BF16)
        outer = dot(jnp.concatenate([p1, p2, p3], axis=1), mid_ref[...]) + bias_ref[1:2, :]
        s2, c2 = sine_pair(SINE_FREQ * outer)
        s2_ref[rows, :] = s2.astype(BF16)
        c2_ref[rows, :] = c2.astype(BF16)
        q1 = s2.astype(BF16)
        q2 = (s2 - q1.astype(F32)).astype(BF16)
        raw = dot(jnp.concatenate([q1, q2], axis=1), fout_ref[...])
        lag = i * step_rows + lax.broadcasted_iota(jnp.int32, (step_rows, 256), 0)
        signed = jnp.where(lag < total // 2, lag, total - lag)
        distance = signed.astype(F32) * (2.0 / total)
        kernel = raw * jnp.exp(-distance * rate_ref[...])
        taps_ref[pl.ds(2 * i, 2), :, :] = kernel.astype(BF16).reshape(2, COLS, 256)
        return carry

    lax.fori_loop(0, total // step_rows, one, 0, unroll=True)
    transform_first(table_ref, taps_ref, work_ref)

    def second(k1, carry):
        part = work_ref[pl.ds(2 * k1, 2), :, :].reshape(256, 256)
        spec_ref[k1] = dot(second_ref[...], part) * frequency_weight(k1)
        return carry

    lax.fori_loop(0, FREQ_ROWS, second, 0, unroll=True)


def make_filter(feats, fin, bias, mid, fout, rate, table, second):
    total = feats.shape[0]
    hidden = jax.ShapeDtypeStruct((total, 128), BF16)
    return pl.pallas_call(
        make_filter_kernel,
        out_shape=(hidden,) * 4 + (jax.ShapeDtypeStruct((FREQ_ROWS, 256, 256), F32),),
        scratch_shapes=[
            pltpu.VMEM((FULL_ROWS, COLS, 256), BF16),
            pltpu.VMEM((2 * FREQ_ROWS, COLS, 256), BF16),
        ],
        compiler_params=VMEM,
        cost_estimate=work(2),
        name="make_filter",
    )(feats, fin, bias, mid, fout, rate, table, second)


def normed_pair(payload, rows, scales, offsets):
    value = payload[:rows].astype(F32)
    stats = to_columns(join_rows(payload[rows:, :rows]))
    mean = spread(stats[:, 0:1], stats[:, 2:3], rows)
    scale = spread(stats[:, 1:2], stats[:, 3:4], rows)
    unit = (value - mean) * scale
    return unit, scale, unit * scales + offsets


def filter_lanes(block):
    return jnp.concatenate([block[:, :128], block], axis=1)


def full_spec(shape):
    return pl.BlockSpec(shape, lambda i: (0,) * len(shape))


ANYWHERE = pl.BlockSpec(memory_space=pl.ANY)


def three_shifts(window, rows):
    return window[7 : 7 + rows], window[8 : 8 + rows], window[9 : 9 + rows]


def mixer_forward_kernel(
    counts_ref,
    x_ref,
    scales_ref,
    offsets_ref,
    w_ref,
    wout_ref,
    second_ref,
    third_ref,
    first_hbm,
    fourth_hbm,
    filter_hbm,
    short_hbm,
    spec_hbm,
    conv_hbm,
    middle_hbm,
    stats_ref,
    first_ref,
    fourth_ref,
    filter_ref,
    normed_ref,
    short_ref,
    values_ref,
    work_ref,
    spec_ref,
    conv_ref,
    gated_ref,
    middle_ref,
    in_sems,
    out_sems,
):
    chunks, tall, _ = x_ref.shape
    rows = tall - STAT_ROWS
    total = chunks * rows
    size = 256
    count_a, count_b = counts_ref[0], counts_ref[1]
    loads = [
        pltpu.make_async_copy(src, dst, in_sems.at[i])
        for i, (src, dst) in enumerate(
            (
                (first_hbm.at[:, :, pl.ds(0, HALF_ROWS * 16)], first_ref),
                (filter_hbm, filter_ref),
                (fourth_hbm.at[:, pl.ds(0, HALF_ROWS * 16), :], fourth_ref),
            )
        )
    ]
    stores = [
        pltpu.make_async_copy(src, dst, out_sems.at[i])
        for i, (src, dst) in enumerate(
            (
                (short_ref, short_hbm),
                (spec_ref, spec_hbm),
                (conv_ref, conv_hbm),
                (middle_ref, middle_hbm),
            )
        )
    ]
    for load in loads:
        load.start()

    edge = jnp.zeros((8, 384), F32)
    normed_ref[0:8, :] = edge
    normed_ref[8 + total :, :] = edge
    for c in range(chunks):
        _, _, normed = normed_pair(x_ref[c], rows, scales_ref[...], offsets_ref[...])
        keep = position_mask(c * rows, rows, count_a, count_b)
        normed_ref[8 + c * rows : 8 + (c + 1) * rows, :] = normed * keep
    for b in range(total // size):
        at = slice(size * b, size * (b + 1))
        window = normed_ref[size * b : size * (b + 1) + 16, :]
        wide = jnp.concatenate([stacked(v).astype(BF16) for v in three_shifts(window, size)], axis=1)
        out = dot(wide, w_ref[...])
        shorts = [packed(out[:, 256 * s : 256 * (s + 1)]) for s in range(3)]
        for s in range(3):
            short_ref[s, at, :] = shorts[s].astype(BF16)
        keep = position_mask(size * b, size, count_a, count_b)
        values = (shorts[2] * shorts[0] * keep).astype(BF16)
        values_ref[2 * b : 2 * b + 2, :, :] = values.reshape(2, COLS, 384)
    stores[0].start()

    loads[0].wait()
    transform_first(first_ref, values_ref, work_ref)
    loads[1].wait()

    def middle(k1, carry):
        part = work_ref[pl.ds(2 * k1, 2), :, :].reshape(256, 384)
        spec = dot(second_ref[...], part)
        spec_ref[k1] = spec.astype(BF16)
        re, im = spec[:128], spec[128:]
        block = filter_ref[k1]
        fre, fim = filter_lanes(block[:128]), filter_lanes(block[128:])
        prod = jnp.concatenate([re * fre - im * fim, re * fim + im * fre], axis=0).astype(BF16)
        work_ref[pl.ds(2 * k1, 2), :, :] = dot(third_ref[...], prod).astype(BF16).reshape(2, COLS, 384)
        return carry

    lax.fori_loop(0, FREQ_ROWS, middle, 0, unroll=True)
    stores[1].start()
    loads[2].wait()
    for j in range(8):
        part = work_ref[:, 16 * j : 16 * (j + 1), :].reshape(FREQ_ROWS * 32, 384)
        conv = dot(fourth_ref[j], part)
        for i in range(HALF_ROWS):
            at = slice(COLS * i + 16 * j, COLS * i + 16 * (j + 1))
            piece = conv[16 * i : 16 * (i + 1)]
            conv_ref[at, :] = piece.astype(BF16)
            gated_ref[at, :] = (piece * short_ref[1, at, :].astype(F32)).astype(BF16)
    stores[2].start()
    for c in range(chunks):
        at = slice(rows * c, rows * (c + 1))
        out = packed(dot(stacked(gated_ref[at, :]), wout_ref[...]))
        value = x_ref[c, :rows, :].astype(F32) + out
        middle_ref[at, :] = value
        sum_a, sum_b = pair_sum(value)
        mean_a, mean_b = sum_a * (1.0 / 192.0), sum_b * (1.0 / 192.0)
        centred = value - spread(mean_a, mean_b, rows)
        square_a, square_b = pair_sum(centred * centred)
        stats_ref[c] = to_rows((mean_a, square_a, mean_b, square_b), rows)
    stores[3].start()
    for store in stores:
        store.wait()


def mixer_forward(counts, payload, scales, offsets, weight, wout, spectrum, tables):
    chunks, tall, _ = payload.shape
    rows = tall - STAT_ROWS
    total = chunks * rows
    first, second, third, fourth = tables
    seq = (total, 384)
    wide = (FREQ_ROWS, 256, 384)
    return pl.pallas_call(
        mixer_forward_kernel,
        grid=(1,),
        in_specs=[pl.BlockSpec(memory_space=pltpu.SMEM)]
        + [full_spec(a.shape) for a in (payload, scales, offsets, weight, wout, second, third)]
        + [ANYWHERE] * 3,
        out_specs=[ANYWHERE] * 4 + [full_spec((chunks, 8, rows))],
        out_shape=[
            jax.ShapeDtypeStruct((3,) + seq, BF16),
            jax.ShapeDtypeStruct(wide, BF16),
            jax.ShapeDtypeStruct(seq, BF16),
            jax.ShapeDtypeStruct(seq, F32),
            jax.ShapeDtypeStruct((chunks, 8, rows), F32),
        ],
        scratch_shapes=[
            pltpu.VMEM(first.shape[:2] + (HALF_ROWS * 16,), BF16),
            pltpu.VMEM((8, HALF_ROWS * 16, fourth.shape[2]), BF16),
            pltpu.VMEM(spectrum.shape, F32),
            pltpu.VMEM((total + 16, 384), F32),
            pltpu.VMEM((3,) + seq, BF16),
            pltpu.VMEM((HALF_ROWS, COLS, 384), BF16),
            pltpu.VMEM((2 * FREQ_ROWS, COLS, 384), BF16),
            pltpu.VMEM(wide, BF16),
            pltpu.VMEM(seq, BF16),
            pltpu.VMEM(seq, BF16),
            pltpu.VMEM(seq, F32),
            pltpu.SemaphoreType.DMA((3,)),
            pltpu.SemaphoreType.DMA((4,)),
        ],
        compiler_params=VMEM,
        cost_estimate=work(25),
        name="mixer_forward",
    )(counts, payload, scales, offsets, weight, wout, second, third, first, fourth, spectrum)


def column_sums(value):
    return jnp.sum(value.reshape(value.shape[0] // 8, 8, value.shape[1]), axis=0)


def fold_rows(value):
    return jnp.concatenate([value[:128], value[128:192] + value[192:256]], axis=0)


def fold_lanes(value):
    last = value[:, 128:]
    summed = jnp.where(low_lanes(value.shape[0]), last + half_turn(last), jnp.zeros_like(last))
    return jnp.concatenate([value[:, :128], summed], axis=1)


def feed_forward_kernel(
    middle_ref,
    s0_ref,
    s1_ref,
    s2_ref,
    s3_ref,
    scales_ref,
    offsets_ref,
    up_ref,
    down_ref,
    out_ref,
    pair_ref,
    normed_ref,
    unit_ref,
    norm_ref,
):
    chunks, rows, _ = out_ref.shape
    for c in range(chunks):
        at_rows = slice(rows * c, rows * (c + 1))
        parts = [ref[c] for ref in (s0_ref, s1_ref, s2_ref, s3_ref)]
        mean = (parts[0] + parts[1] + parts[2] + parts[3]) * 0.25
        spread_sum = jnp.zeros_like(mean)
        for part in parts:
            gap = part - mean
            spread_sum += 192.0 * gap * gap
        squares = parts[0] + parts[1] + parts[2] + parts[3]
        scale_a = lax.rsqrt((squares[1:2] + spread_sum[0:1]) * (1.0 / 768.0) + EPS)
        scale_b = lax.rsqrt((squares[3:4] + spread_sum[2:3]) * (1.0 / 768.0) + EPS)
        norm = jnp.concatenate([mean[0:1], scale_a, mean[2:3], scale_b, jnp.zeros((4, rows), F32)], axis=0)
        norm_ref[c] = norm
        columns = to_columns(norm)
        middle = middle_ref[at_rows, :]
        unit = (middle - spread(columns[:, 0:1], columns[:, 2:3], rows)) * spread(columns[:, 1:2], columns[:, 3:4], rows)
        unit_ref[at_rows, :] = unit.astype(BF16)
        normed = stacked(unit * scales_ref[...] + offsets_ref[...]).astype(BF16)
        normed_ref[c] = normed
        hiddens = []
        width = 256
        for f in range(768 // width):
            at = slice(width * f, width * (f + 1))
            at_up = slice(768 + width * f, 768 + width * (f + 1))
            gate = dot(normed, up_ref[:, at])
            upper = dot(normed, up_ref[:, at_up])
            pair_ref[c, :, at] = gate.astype(BF16)
            pair_ref[c, :, at_up] = upper.astype(BF16)
            hiddens.append((gate * normal_cdf(gate) * upper).astype(BF16))
        down = dot(jnp.concatenate(hiddens, axis=1), down_ref[...])
        out_ref[c] = (middle + packed(down)).astype(BF16)


def feed_forward(middle, stats, scales, offsets, up, down):
    chunks, _, rows = stats[0].shape
    total = chunks * rows
    many = min(chunks, GROUPED)
    stat_spec = pl.BlockSpec((many, 8, rows), lambda i: (i, 0, 0))
    rows_spec = pl.BlockSpec((many * rows, 384), lambda i: (i, 0))
    return pl.pallas_call(
        feed_forward_kernel,
        grid=(chunks // many,),
        in_specs=[rows_spec] + [stat_spec] * 4 + [full_spec(a.shape) for a in (scales, offsets, up, down)],
        out_specs=[
            pl.BlockSpec((many, rows, 384), lambda i: (i, 0, 0)),
            pl.BlockSpec((many, 2 * rows, 1536), lambda i: (i, 0, 0)),
            pl.BlockSpec((many, 2 * rows, 256), lambda i: (i, 0, 0)),
            rows_spec,
            stat_spec,
        ],
        out_shape=[
            jax.ShapeDtypeStruct((chunks, rows, 384), BF16),
            jax.ShapeDtypeStruct((chunks, 2 * rows, 1536), BF16),
            jax.ShapeDtypeStruct((chunks, 2 * rows, 256), BF16),
            jax.ShapeDtypeStruct((total, 384), BF16),
            jax.ShapeDtypeStruct((chunks, 8, rows), F32),
        ],
        compiler_params=VMEM,
        cost_estimate=work(11),
        name="feed_forward",
    )(middle, *stats, scales, offsets, up, down)


def feed_back_kernel(
    cot_ref,
    pair_ref,
    normed_ref,
    unit_ref,
    scales_ref,
    upt_ref,
    downt_ref,
    q_ref,
    sums_ref,
    gffn_ref,
    small_ref,
    up_acc,
    down_acc,
):
    chunks, rows, _ = cot_ref.shape
    step = pl.program_id(0)

    @pl.when(step == 0)
    def _():
        small_ref[...] = jnp.zeros_like(small_ref)
        up_acc[...] = jnp.zeros_like(up_acc)
        down_acc[...] = jnp.zeros_like(down_acc)

    join = lambda parts: jnp.concatenate(parts, axis=0)
    cot = join([stacked(cot_ref[c]) for c in range(chunks)])
    size = 2 * rows * chunks
    grad_hidden = dot(cot, downt_ref[...])
    hidden, gates, uppers = [], [], []
    width = 256
    for f in range(768 // width):
        at = slice(width * f, width * (f + 1))
        at_up = slice(768 + width * f, 768 + width * (f + 1))
        gate = pair_ref[:, :, at].reshape(size, width).astype(F32)
        upper = pair_ref[:, :, at_up].reshape(size, width).astype(F32)
        cdf = normal_cdf(gate)
        active = gate * cdf
        hidden.append((active * upper).astype(BF16))
        gates.append((grad_hidden[:, at] * upper * (cdf + gate * normal_density(gate))).astype(BF16))
        uppers.append((grad_hidden[:, at] * active).astype(BF16))
    hidden = jnp.concatenate(hidden, axis=1)
    grads = jnp.concatenate(gates + uppers, axis=1)
    back = dot(grads, upt_ref[...])
    up_acc[...] += fold_rows(dot(normed_ref[...].reshape(size, 256).T, grads))
    down_acc[...] += dot(cot.T, hidden)
    for c in range(chunks):
        at_rows = slice(rows * c, rows * (c + 1))
        grad = packed(back[2 * rows * c : 2 * rows * (c + 1)])
        unit = unit_ref[at_rows, :].astype(F32)
        q = grad * scales_ref[...]
        q_ref[at_rows, :] = q.astype(BF16)
        sums_ref[c] = to_rows(pair_sum(q) + pair_sum(q * unit), rows)
        small_ref[0:8, :] += column_sums(grad * unit)
        small_ref[8:16, :] += column_sums(grad)

    @pl.when(step == pl.num_programs(0) - 1)
    def _():
        parts = gffn_ref.shape[0]
        share = 192 // parts
        down = fold_lanes(down_acc[...].T).astype(BF16)
        for d in range(parts):
            for t in range(6):
                value = up_acc[share * d : share * (d + 1), 256 * t : 256 * (t + 1)]
                gffn_ref[d, share * t : share * (t + 1), :] = value.astype(BF16)
            gffn_ref[d, 6 * share :, :] = down[4 * share * d : 4 * share * (d + 1)]


def feed_back(cot, pair, normed, unit, scales, upt, downt, parts):
    chunks, rows, _ = cot.shape
    total = chunks * rows
    many = min(chunks, GROUPED)
    rows_spec = pl.BlockSpec((many * rows, 384), lambda i: (i, 0))
    spec = lambda shape: pl.BlockSpec((many,) + shape[1:], lambda i: (i, 0, 0))
    stats = (chunks, 8, rows)
    return pl.pallas_call(
        feed_back_kernel,
        grid=(chunks // many,),
        in_specs=[spec(cot.shape), spec(pair.shape), spec(normed.shape), rows_spec]
        + [full_spec(a.shape) for a in (scales, upt, downt)],
        out_specs=[rows_spec, spec(stats), full_spec((parts, 1920 // parts, 256)), full_spec((16, 384))],
        out_shape=[
            jax.ShapeDtypeStruct((total, 384), BF16),
            jax.ShapeDtypeStruct(stats, F32),
            jax.ShapeDtypeStruct((parts, 1920 // parts, 256), BF16),
            jax.ShapeDtypeStruct((16, 384), F32),
        ],
        scratch_shapes=[pltpu.VMEM((192, 1536), F32), pltpu.VMEM((256, 768), F32)],
        compiler_params=VMEM,
        cost_estimate=work(2),
        name="feed_back",
    )(cot, pair, normed, unit, scales, upt, downt)


def mixer_backward_kernel(
    counts_ref,
    norm_ref,
    s0_ref,
    s1_ref,
    s2_ref,
    s3_ref,
    woutt_ref,
    second_ref,
    third_ref,
    scales_ref,
    offsets_ref,
    x_hbm,
    wt_hbm,
    cot_hbm,
    q_hbm,
    unit_hbm,
    conv_hbm,
    short_hbm,
    first_hbm,
    spec_hbm,
    filter_hbm,
    fourth_hbm,
    grad_hbm,
    cross_hbm,
    grads_hbm,
    out_ref,
    small_ref,
    x_ref,
    wt_ref,
    parts_ref,
    cot_ref,
    q_ref,
    unit_ref,
    conv_ref,
    short_ref,
    first_ref,
    spec_ref,
    filter_ref,
    fourth_ref,
    work_ref,
    cross_ref,
    grads_ref,
    in_sems,
    out_sems,
):
    chunks, _, rows = norm_ref.shape
    total = chunks * rows
    count_a, count_b = counts_ref[0], counts_ref[1]
    half = total // 2
    early, late = pl.ds(0, half), pl.ds(half, half)
    lanes = first_ref.shape[2]
    loads = [
        pltpu.make_async_copy(src, dst, in_sems.at[i])
        for i, (src, dst) in enumerate(
            [
                (src.at[part], dst.at[part])
                for part in (early, late)
                for src, dst in (
                    (cot_hbm, cot_ref),
                    (q_hbm, q_ref),
                    (unit_hbm, unit_ref),
                    (short_hbm.at[1], short_ref.at[1]),
                    (conv_hbm, conv_ref),
                )
            ]
            + [
                (first_hbm.at[:, :, pl.ds(0, lanes)], first_ref),
                (spec_hbm, spec_ref),
                (filter_hbm, filter_ref),
                (fourth_hbm.at[:, pl.ds(0, lanes), :], fourth_ref),
                (short_hbm.at[0], short_ref.at[0]),
                (short_hbm.at[2], short_ref.at[2]),
                (wt_hbm, wt_ref),
                (x_hbm, x_ref),
            ]
        )
    ]
    for load in loads:
        load.start()

    for c in range(chunks):
        if c == 0:
            for load in loads[0:5]:
                load.wait()
        if c == chunks // 2:
            for load in loads[5:10]:
                load.wait()
        at = slice(rows * c, rows * (c + 1))
        sums = (s0_ref[c] + s1_ref[c] + s2_ref[c] + s3_ref[c]) * (1.0 / 768.0)
        columns = to_columns(jnp.concatenate([sums[0:4], norm_ref[c][0:4]], axis=0))
        scale = spread(columns[:, 5:6], columns[:, 7:8], rows)
        mean_q = spread(columns[:, 0:1], columns[:, 1:2], rows)
        mean_qh = spread(columns[:, 2:3], columns[:, 3:4], rows)
        back = q_ref[at, :].astype(F32) - mean_q - unit_ref[at, :].astype(F32) * mean_qh
        grad = cot_ref[at, :].astype(F32) + scale * back
        cot_ref[at, :] = grad.astype(BF16)
        grad_gated = packed(dot(stacked(grad).astype(BF16), woutt_ref[...]))
        unit_ref[at, :] = (grad_gated * short_ref[1, at, :].astype(F32)).astype(BF16)
        grads_ref[1, at, :] = (grad_gated * conv_ref[at, :].astype(F32)).astype(BF16)
    stores = [
        pltpu.make_async_copy(src, dst, out_sems.at[i])
        for i, (src, dst) in enumerate(((cot_ref, grad_hbm), (cross_ref, cross_hbm), (grads_ref, grads_hbm)))
    ]
    stores[0].start()

    loads[10].wait()
    for j in range(8):
        block = jnp.concatenate(
            [unit_ref[COLS * i + 16 * j : COLS * i + 16 * (j + 1), :] for i in range(HALF_ROWS)], axis=0
        )
        part = dot(first_ref[j], block).astype(BF16)
        work_ref[:, 16 * j : 16 * (j + 1), :] = part.reshape(2 * FREQ_ROWS, 16, 384)
    for load in loads[11:13]:
        load.wait()

    def middle(k1, carry):
        part = work_ref[pl.ds(2 * k1, 2), :, :].reshape(256, 384)
        grad = dot(second_ref[...], part)
        re, im = grad[:128], grad[128:]
        spec = spec_ref[k1].astype(F32)
        vre, vim = spec[:128], spec[128:]
        cre = re * vre + im * vim
        cim = im * vre - re * vim
        weight = frequency_weight(k1)
        fold = lambda v: jnp.concatenate([v[:, :128] + v[:, 128:256], v[:, 256:]], axis=1)
        cross_ref[k1] = (jnp.concatenate([fold(cre), fold(cim)], axis=0) * weight).astype(BF16)
        block = filter_ref[k1]
        fre, fim = filter_lanes(block[:128]), filter_lanes(block[128:])
        prod = jnp.concatenate([re * fre + im * fim, im * fre - re * fim], axis=0).astype(BF16)
        work_ref[pl.ds(2 * k1, 2), :, :] = dot(third_ref[...], prod).astype(BF16).reshape(2, COLS, 384)
        return carry

    lax.fori_loop(0, FREQ_ROWS, middle, 0, unroll=True)
    stores[1].start()
    for load in loads[13:]:
        load.wait()
    for j in range(8):
        part = work_ref[:, 16 * j : 16 * (j + 1), :].reshape(FREQ_ROWS * 32, 384)
        grad_values = dot(fourth_ref[j], part)
        for i in range(HALF_ROWS):
            start = COLS * i + 16 * j
            at = slice(start, start + 16)
            piece = grad_values[16 * i : 16 * (i + 1)] * position_mask(start, 16, count_a, count_b)
            grads_ref[0, at, :] = (piece * short_ref[2, at, :].astype(F32)).astype(BF16)
            grads_ref[2, at, :] = (piece * short_ref[0, at, :].astype(F32)).astype(BF16)
    stores[2].start()

    size = 512
    edge = jnp.zeros((8, 384), F32)
    for j in range(3):
        parts_ref[j, 0:8, :] = edge
        parts_ref[j, 8 + total :, :] = edge
    for b in range(total // size):
        at = slice(size * b, size * (b + 1))
        wide = jnp.concatenate([stacked(grads_ref[s, at, :]) for s in range(3)], axis=1)
        out = dot(wide, wt_ref[...])
        for j in range(3):
            parts_ref[j, 8 + size * b : 8 + size * (b + 1), :] = packed(out[:, 256 * j : 256 * (j + 1)])
    gain = jnp.zeros((8, 384), F32)
    bias = jnp.zeros((8, 384), F32)
    for c in range(chunks):
        at = slice(rows * c, rows * (c + 1))
        ahead = parts_ref[0, rows * c : rows * (c + 1) + 16, :][9 : 9 + rows]
        here = parts_ref[1, 8 + rows * c : 8 + rows * (c + 1), :]
        behind = parts_ref[2, rows * c : rows * (c + 1) + 16, :][7 : 7 + rows]
        keep = position_mask(c * rows, rows, count_a, count_b)
        grad_normed = (ahead + here + behind) * keep
        unit, scale, _ = normed_pair(x_ref[c], rows, scales_ref[...], offsets_ref[...])
        gain += column_sums(grad_normed * unit)
        bias += column_sums(grad_normed)
        q = grad_normed * scales_ref[...]
        out_ref[c, :rows, :] = (cot_ref[at, :].astype(F32) + scale * q).astype(BF16)
        out_ref[c, rows:, :rows] = split_rows(to_rows(pair_sum(q) + pair_sum(q * unit), rows))
    small_ref[0:8, :] = gain
    small_ref[8:16, :] = bias
    for store in stores:
        store.wait()


def mixer_backward(
    counts, norm, sums, woutt, scales, offsets, payload, wt, cot, q, unit, conv, short, spec, spectrum, tables
):
    chunks, _, rows = norm.shape
    total = chunks * rows
    first, second, third, fourth = tables
    lanes = HALF_ROWS * 16
    seq = (total, 384)
    cross = (FREQ_ROWS, 256, 256)
    blocked = [norm, *sums, woutt, second, third, scales, offsets]
    return pl.pallas_call(
        mixer_backward_kernel,
        grid=(1,),
        in_specs=[pl.BlockSpec(memory_space=pltpu.SMEM)]
        + [full_spec(a.shape) for a in blocked]
        + [ANYWHERE] * 11,
        out_specs=[ANYWHERE] * 3 + [full_spec(payload.shape), full_spec((16, 384))],
        out_shape=[
            jax.ShapeDtypeStruct(seq, BF16),
            jax.ShapeDtypeStruct(cross, BF16),
            jax.ShapeDtypeStruct((3,) + seq, BF16),
            jax.ShapeDtypeStruct(payload.shape, BF16),
            jax.ShapeDtypeStruct((16, 384), F32),
        ],
        scratch_shapes=[
            pltpu.VMEM(payload.shape, BF16),
            pltpu.VMEM(wt.shape, BF16),
            pltpu.VMEM((3, total + 16, 384), F32),
        ]
        + [pltpu.VMEM(seq, BF16)] * 4
        + [
            pltpu.VMEM((3,) + seq, BF16),
            pltpu.VMEM(first.shape[:2] + (lanes,), BF16),
            pltpu.VMEM(spec.shape, BF16),
            pltpu.VMEM(spectrum.shape, F32),
            pltpu.VMEM((8, lanes, fourth.shape[2]), BF16),
            pltpu.VMEM((2 * FREQ_ROWS, COLS, 384), BF16),
            pltpu.VMEM(cross, BF16),
            pltpu.VMEM((3,) + seq, BF16),
            pltpu.SemaphoreType.DMA((18,)),
            pltpu.SemaphoreType.DMA((3,)),
        ],
        compiler_params=WIDE_VMEM,
        cost_estimate=work(4),
        name="mixer_backward",
    )(counts, *blocked, payload, wt, cot, q, unit, conv, short, first, spec, spectrum, fourth)


def mixer_grads_kernel(
    counts_ref,
    x_ref,
    scales_ref,
    offsets_ref,
    taps_ref,
    win_ref,
    grads_ref,
    grad_ref,
    conv_ref,
    short_ref,
    gin_ref,
    gtaps_ref,
    normed_ref,
    in_acc,
):
    chunks, tall, _ = x_ref.shape
    rows = tall - STAT_ROWS
    total = chunks * rows
    size = 512
    parts = gin_ref.shape[0]
    share = 192 // parts
    count_a, count_b = counts_ref[0], counts_ref[1]
    edge = jnp.zeros((8, 384), F32)
    normed_ref[0:8, :] = edge
    normed_ref[8 + total :, :] = edge
    for c in range(chunks):
        _, _, normed = normed_pair(x_ref[c], rows, scales_ref[...], offsets_ref[...])
        keep = position_mask(c * rows, rows, count_a, count_b)
        normed_ref[8 + c * rows : 8 + (c + 1) * rows, :] = normed * keep
    gout = jnp.zeros((192, 256), F32)
    for b in range(total // size):
        at = slice(size * b, size * (b + 1))
        wide_grads = jnp.concatenate([stacked(grads_ref[s, at, :]) for s in range(3)], axis=1)
        window = normed_ref[size * b : size * (b + 1) + 16, :]
        wide = jnp.concatenate([stacked(v).astype(BF16) for v in three_shifts(window, size)], axis=1)
        product = dot(wide.T, wide_grads)
        if b == 0:
            in_acc[...] = product
        else:
            in_acc[...] += product
        gated = (conv_ref[at, :].astype(F32) * short_ref[at, :].astype(F32)).astype(BF16)
        gout += fold_rows(dot(stacked(gated).T, stacked(grad_ref[at, :])))
    gout = fold_lanes(gout).astype(BF16)
    for d in range(parts):
        gin_ref[d, 3 * share :, :] = gout[share * d : share * (d + 1)]
    for s in range(3):
        lanes = slice(256 * s, 256 * (s + 1))
        total_in = jnp.zeros((192, 256), F32)
        for j in range(3):
            block = fold_lanes(fold_rows(in_acc[256 * j : 256 * (j + 1), lanes]))
            at = 3 * j + s
            total_in += block * taps_ref[at : at + 1, :]
            gtaps_ref[8 * at : 8 * (at + 1), :] = column_sums(block * win_ref[:, lanes].astype(F32))
        total_in = total_in.astype(BF16)
        for d in range(parts):
            gin_ref[d, share * s : share * (s + 1), :] = total_in[share * d : share * (d + 1)]


def mixer_grads(counts, payload, scales, offsets, taps, win, grads, grad, conv, short, parts):
    chunks, tall, _ = payload.shape
    total = chunks * (tall - STAT_ROWS)
    return pl.pallas_call(
        mixer_grads_kernel,
        grid=(1,),
        in_specs=[pl.BlockSpec(memory_space=pltpu.SMEM)]
        + [full_spec(a.shape) for a in (payload, scales, offsets, taps, win, grads, grad, conv)]
        + [pl.BlockSpec((None, total, 384), lambda i: (1, 0, 0))],
        out_specs=[full_spec((parts, 768 // parts, 256)), full_spec((72, 256))],
        out_shape=[
            jax.ShapeDtypeStruct((parts, 768 // parts, 256), BF16),
            jax.ShapeDtypeStruct((72, 256), F32),
        ],
        scratch_shapes=[pltpu.VMEM((total + 16, 384), F32), pltpu.VMEM((768, 768), F32)],
        compiler_params=VMEM,
        cost_estimate=work(0.01),
        name="mixer_grads",
    )(counts, payload, scales, offsets, taps, win, grads, grad, conv, short)


def filter_back_kernel(
    cross_ref,
    s1_ref,
    c1_ref,
    s2_ref,
    c2_ref,
    feat_ref,
    midt_ref,
    foutt_ref,
    rate_ref,
    third_ref,
    fourth_ref,
    mixer_ref,
    gtaps_ref,
    small_one_ref,
    small_two_ref,
    own_ref,
    gfin_ref,
    gmid_ref,
    gfout_ref,
    gbias_ref,
    work_ref,
    taps_ref,
):
    total = feat_ref.shape[0]
    step_rows = 256

    def second(k1, carry):
        work_ref[pl.ds(2 * k1, 2), :, :] = dot(third_ref[...], cross_ref[k1]).astype(BF16).reshape(2, COLS, 256)
        return carry

    lax.fori_loop(0, FREQ_ROWS, second, 0, unroll=True)

    def last(j, carry):
        start = pl.ds(pl.multiple_of(16 * j, 16), 16)
        part = work_ref[:, start, :].reshape(FREQ_ROWS * 32, 256)
        taps_ref[:, start, :] = dot(fourth_ref[j], part).reshape(FULL_ROWS, 16, 256)
        return carry

    lax.fori_loop(0, 8, last, 0, unroll=True)
    gfin_ref[...] = jnp.zeros_like(gfin_ref)
    gmid_ref[...] = jnp.zeros_like(gmid_ref)
    gfout_ref[...] = jnp.zeros_like(gfout_ref)
    gbias_ref[...] = jnp.zeros_like(gbias_ref)

    def one(i, carry):
        rows = pl.ds(pl.multiple_of(i * step_rows, step_rows), step_rows)
        lag = i * step_rows + lax.broadcasted_iota(jnp.int32, (step_rows, 256), 0)
        signed = jnp.where(lag < total // 2, lag, total - lag)
        distance = signed.astype(F32) * (2.0 / total)
        grad = taps_ref[pl.ds(2 * i, 2), :, :].reshape(step_rows, 256) * jnp.exp(-distance * rate_ref[...])
        grad = grad.astype(BF16)
        gfout_ref[...] += dot(s2_ref[rows, :].T, grad)
        grad_second = dot(grad, foutt_ref[...]) * (SINE_FREQ * c2_ref[rows, :].astype(F32))
        gbias_ref[8:16, :] += column_sums(grad_second)
        grad_second = grad_second.astype(BF16)
        gmid_ref[...] += dot(s1_ref[rows, :].T, grad_second)
        grad_first = dot(grad_second, midt_ref[...]) * (SINE_FREQ * c1_ref[rows, :].astype(F32))
        gbias_ref[0:8, :] += column_sums(grad_first)
        gfin_ref[...] += dot(feat_ref[rows, :].T, grad_first.astype(BF16))
        return carry

    lax.fori_loop(0, total // step_rows, one, 0, unroll=True)


    parts, tall, _ = mixer_ref.shape
    hidden = 128 // parts
    wide = lambda v: jnp.concatenate([v, jnp.zeros((v.shape[0], 128), F32)], axis=1)
    mid = wide(gmid_ref[...]).astype(BF16)
    fout = fold_lanes(gfout_ref[...]).astype(BF16)

    def channel_row(rows):
        row = jnp.sum(rows, axis=0, keepdims=True)
        joined = jnp.concatenate([row[:, :128] + row[:, 128:256], row[:, 256:]], axis=1)
        return fold_lanes(joined)

    same = [
        channel_row(small_one_ref[0:8, :]),
        channel_row(small_two_ref[0:8, :]),
        channel_row(small_one_ref[8:16, :]),
        channel_row(small_two_ref[8:16, :]),
    ]
    same += [jnp.sum(gtaps_ref[8 * i : 8 * (i + 1), :], axis=0, keepdims=True) for i in range(9)]
    same += [wide(gfin_ref[0:5, :] + gfin_ref[5:10, :] + gfin_ref[10:15, :])]
    same += [wide(jnp.sum(gbias_ref[8 * i : 8 * (i + 1), :], axis=0, keepdims=True)) for i in range(2)]
    same += [jnp.zeros((12, 256), F32)]
    same = jnp.concatenate(same, axis=0).astype(BF16)
    for d in range(parts):
        own_ref[d, :tall, :] = mixer_ref[d]
        own_ref[d, tall : tall + hidden, :] = mid[hidden * d : hidden * (d + 1)]
        own_ref[d, tall + hidden : tall + 2 * hidden, :] = fout[hidden * d : hidden * (d + 1)]
        own_ref[d, tall + 2 * hidden :, :] = same


def filter_back(cross, hidden, feats, midt, foutt, rate, third, fourth, mixer, gtaps, small_one, small_two):
    parts, tall, _ = mixer.shape
    return pl.pallas_call(
        filter_back_kernel,
        out_shape=jax.ShapeDtypeStruct((parts, tall + 256 // parts + 32, 256), BF16),
        scratch_shapes=[
            pltpu.VMEM((16, 128), F32),
            pltpu.VMEM((128, 128), F32),
            pltpu.VMEM((128, 256), F32),
            pltpu.VMEM((16, 128), F32),
            pltpu.VMEM((2 * FREQ_ROWS, COLS, 256), BF16),
            pltpu.VMEM((FULL_ROWS, COLS, 256), F32),
        ],
        compiler_params=VMEM,
        cost_estimate=work(0.01),
        name="filter_back",
    )(cross, *hidden, feats, midt, foutt, rate, third, fourth, mixer, gtaps, small_one, small_two)


def unpack_out_kernel(x_ref, out_ref):
    for even in (0, 2):
        a, b = unpack_pairs(x_ref[even].astype(F32), x_ref[even + 1].astype(F32))
        out_ref[0, :, 192 * even : 192 * even + 384] = a.astype(BF16)
        out_ref[1, :, 192 * even : 192 * even + 384] = b.astype(BF16)


def unpack_out(value):
    chunks, rows, _ = value.shape
    return pl.pallas_call(
        unpack_out_kernel,
        grid=(chunks // 4,),
        in_specs=[pl.BlockSpec((4, rows, 384), lambda i: (i, 0, 0))],
        out_specs=pl.BlockSpec((2, rows, 768), lambda i: (i, 0, 0)),
        out_shape=jax.ShapeDtypeStruct((chunks // 2, rows, 768), BF16),
        compiler_params=VMEM,
        cost_estimate=work(0.01),
        name="unpack_out",
    )(value)


def unpack_grad_kernel(x_ref, tokens_ref, out_ref):
    rows = tokens_ref.shape[1]
    sums = jnp.zeros((8, rows), F32)
    for block in range(4):
        sums += join_rows(x_ref[block, rows:, :rows])
    columns = to_columns(sums) * (1.0 / 768.0)
    wide = ([], [])
    for even in (0, 2):
        a, b = unpack_pairs(x_ref[even, :rows].astype(F32), x_ref[even + 1, :rows].astype(F32))
        wide[0].append(a)
        wide[1].append(b)
    for which in range(2):
        token = tokens_ref[which].astype(F32)
        mean, scale = row_stats(token)
        unit = (token - mean) * scale
        grad = jnp.concatenate(wide[which], axis=1)
        mean_q = columns[:, which : which + 1]
        mean_qh = columns[:, 2 + which : 3 + which]
        out_ref[which] = grad - scale * (mean_q + unit * mean_qh)


def unpack_grad(value, tokens):
    chunks, tall, _ = value.shape
    rows = tall - STAT_ROWS
    return pl.pallas_call(
        unpack_grad_kernel,
        grid=(chunks // 4,),
        in_specs=[
            pl.BlockSpec((4, tall, 384), lambda i: (i, 0, 0)),
            pl.BlockSpec((2, rows, 768), lambda i: (i, 0, 0)),
        ],
        out_specs=pl.BlockSpec((2, rows, 768), lambda i: (i, 0, 0)),
        out_shape=jax.ShapeDtypeStruct((chunks // 2, rows, 768), F32),
        compiler_params=VMEM,
        cost_estimate=work(8),
        name="unpack_grad",
    )(value, tokens)


def finish_ffn_kernel(block_ref, *refs):
    pieces, (up_ref, down_ref) = refs[:4], refs[4:]
    share = up_ref.shape[2]
    for r in range(4):
        at = lax.bitwise_xor(block_ref[0], r)
        for t in range(6):
            value = pieces[r][share * t : share * (t + 1), :].astype(F32)
            up_ref[t // 3, at, :, 256 * (t % 3) : 256 * (t % 3 + 1)] = value
        down_ref[at] = pieces[r][6 * share :, :192].astype(F32)


def finish_ffn(block, pieces):
    share = pieces[0].shape[0] // 10
    vmem = pl.BlockSpec(memory_space=pltpu.VMEM)
    return pl.pallas_call(
        finish_ffn_kernel,
        in_specs=[pl.BlockSpec(memory_space=pltpu.SMEM)] + [vmem] * 4,
        out_shape=[
            jax.ShapeDtypeStruct((2, 4, share, 768), F32),
            jax.ShapeDtypeStruct((4, 4 * share, 192), F32),
        ],
        cost_estimate=work(0.01),
        name="finish_ffn",
    )(block, *pieces)


def finish_mixer_kernel(place_ref, *refs):
    pieces, outs = refs[:4], refs[4:]
    in_ref, out_ref, mid_ref, gain_ref, bias_ref, taps_ref, fin_ref, fbias_ref, fout_ref = outs
    share = in_ref.shape[2]
    hidden, shard, cols = mid_ref.shape[0], gain_ref.shape[1], fout_ref.shape[1]
    block, chan_block, chan_start, hidden_start, fout_block, fout_start = [place_ref[i] for i in range(6)]
    start = 4 * share

    def turned(value, shift):
        return pltpu.roll(value, lax.rem(256 - shift, 256), axis=1)

    def of_block(rows, which):
        total = jnp.zeros((rows.stop - rows.start, 256), F32)
        for r in range(4):
            take = lax.bitwise_xor(block, r) == which
            total += jnp.where(take, pieces[r][rows, :].astype(F32), 0.0)
        return total

    for r in range(4):
        at = lax.bitwise_xor(block, r)
        for s in range(3):
            in_ref[s, at] = pieces[r][share * s : share * (s + 1), :192].astype(F32)
        out_ref[at] = pieces[r][3 * share : 4 * share, :192].astype(F32)
    mids = [piece[start : start + hidden, :128].astype(F32) for piece in pieces]
    mid_ref[...] = mids[0] + mids[1] + mids[2] + mids[3]
    fouts = of_block(slice(start + hidden, start + 2 * hidden), fout_block)
    fout_ref[...] = turned(fouts, fout_start)[:, :cols]
    rest = slice(start + 2 * hidden, start + 2 * hidden + 32)
    rows = turned(of_block(rest, chan_block), chan_start)[:, :shard]
    gain_ref[...] = rows[0:2]
    bias_ref[...] = rows[2:4]
    for j in range(3):
        taps_ref[j] = rows[4 + 3 * j : 7 + 3 * j]
    total = pieces[0][rest, :].astype(F32)
    for piece in pieces[1:]:
        total += piece[rest, :].astype(F32)
    filters = turned(total, hidden_start)[:, :hidden]
    fin_ref[...] = filters[13:18]
    fbias_ref[...] = filters[18:20]


def finish_mixer(place, pieces, share, hidden, shard, cols):
    vmem = pl.BlockSpec(memory_space=pltpu.VMEM)
    shapes = ((3, 4, share, 192), (4, share, 192), (hidden, 128), (2, shard), (2, shard))
    shapes += ((3, 3, shard), (5, hidden), (2, hidden), (hidden, cols))
    return pl.pallas_call(
        finish_mixer_kernel,
        in_specs=[pl.BlockSpec(memory_space=pltpu.SMEM)] + [vmem] * 4,
        out_shape=[jax.ShapeDtypeStruct(shape, F32) for shape in shapes],
        compiler_params=VMEM,
        cost_estimate=work(0.01),
        name="finish_mixer",
    )(place, *pieces)


def own_block_kernel(block_ref, in_ref, out_ref, up_ref, down_ref, order_ref, all_ref):
    share = out_ref.shape[1]
    pieces = [in_ref[i, 0] for i in range(3)] + [out_ref[0]]
    wide = [up_ref[g, 0, :, 256 * t : 256 * (t + 1)] for g in range(2) for t in range(3)]
    fill = lambda v: jnp.concatenate([v.astype(F32), jnp.zeros((v.shape[0], 64), F32)], axis=1)
    rows = [fill(v) for v in pieces] + [v.astype(F32) for v in wide] + [fill(down_ref[0])]
    all_ref[...] = jnp.concatenate(rows, axis=0).astype(BF16)


def own_block(block, in_weight, out_weight, up_weight, down_weight, order):
    share = out_weight.shape[1]
    width = out_weight.shape[2]
    return pl.pallas_call(
        own_block_kernel,
        grid_spec=pltpu.PrefetchScalarGridSpec(
            num_scalar_prefetch=1,
            grid=(1,),
            in_specs=[
                pl.BlockSpec((3, 1, share, width), lambda i, at: (0, at[0], 0, 0)),
                pl.BlockSpec((1, share, width), lambda i, at: (at[0], 0, 0)),
                pl.BlockSpec((2, 1, share, 4 * width), lambda i, at: (0, at[0], 0, 0)),
                pl.BlockSpec((1, 4 * share, width), lambda i, at: (at[0], 0, 0)),
                ANYWHERE,
            ],
            out_specs=pl.BlockSpec((14 * share, 256), lambda i, at: (0, 0)),
        ),
        out_shape=jax.ShapeDtypeStruct((14 * share, 256), BF16),
        compiler_params=VMEM,
        cost_estimate=work(0.5),
        name="own_block",
    )(block, in_weight, out_weight, up_weight, down_weight, order)


def lanes_twice(value):
    last = value[:, 128:]
    return jnp.concatenate(
        [value[:, :128], jnp.where(low_lanes(value.shape[0]), last, half_turn(last))], axis=1
    )


def rows_twice(value):
    return jnp.concatenate([value, value[128:192]], axis=0)


def whole_weights_kernel(
    all_ref, taps_ref, win_ref, wtaps_ref, wtapst_ref, wout_ref, woutt_ref, up_ref, upt_ref, down_ref, downt_ref
):
    count, tall, _ = all_ref.shape
    share = tall // 14
    parts = [all_ref[d].astype(F32) for d in range(count)]

    def assembled(start, size):
        return jnp.concatenate([part[start : start + size] for part in parts], axis=0)

    plain = jnp.concatenate([lanes_twice(assembled(share * s, share)) for s in range(3)], axis=1)
    win_ref[...] = plain.astype(BF16)
    for j in range(3):
        rows = slice(256 * j, 256 * (j + 1))
        scaled = rows_twice(plain * taps_ref[j : j + 1, :])
        wtaps_ref[rows, :] = scaled.astype(BF16)
        wtapst_ref[:, rows] = scaled.T.astype(BF16)
    out = rows_twice(lanes_twice(assembled(3 * share, share)))
    wout_ref[...] = out.astype(BF16)
    woutt_ref[...] = out.T.astype(BF16)
    for t in range(6):
        cols = slice(256 * t, 256 * (t + 1))
        up = rows_twice(assembled((4 + t) * share, share))
        up_ref[:, cols] = up.astype(BF16)
        upt_ref[cols, :] = up.T.astype(BF16)
    down = lanes_twice(assembled(10 * share, 4 * share))
    down_ref[...] = down.astype(BF16)
    downt_ref[...] = down.T.astype(BF16)


def whole_weights(gathered, taps):
    vmem = pl.BlockSpec(memory_space=pltpu.VMEM)
    shapes = ((192, 768), (768, 768), (768, 768), (256, 256), (256, 256))
    shapes += ((256, 1536), (1536, 256), (768, 256), (256, 768))
    return pl.pallas_call(
        whole_weights_kernel,
        in_specs=[vmem, vmem],
        out_shape=[jax.ShapeDtypeStruct(shape, BF16) for shape in shapes],
        compiler_params=VMEM,
        cost_estimate=work(1),
        name="whole_weights",
    )(gathered, taps)


def doubled(value, axis):
    return jnp.concatenate([value, lax.slice_in_dim(value, 128, 192, axis=axis)], axis=axis)


def pair_lanes(value):
    head, tail = value[:, :128], value[:, 128:]
    return jnp.concatenate([head, head, tail, tail], axis=1)


def at_block(value, block, axis):
    return lax.dynamic_index_in_dim(value, block, axis=axis, keepdims=False)


def per_device(
    tokens,
    lengths,
    cotangent,
    norm_gain,
    norm_bias,
    in_weight,
    conv_taps,
    filter_in,
    filter_mid,
    filter_bias,
    filter_out,
    out_weight,
    up_weight,
    down_weight,
):
    count, rows, features = tokens.shape
    blocks = in_weight.shape[1]
    data_size = lax.axis_size("dp")
    seq_size = lax.axis_size("seq")
    total = rows * seq_size
    groups = seq_size // blocks
    place = lax.axis_index("seq")
    block = place % blocks
    group = place // blocks
    width = features // blocks
    data_at = lax.axis_index("dp")
    block_at = block.astype(jnp.int32).reshape(1)

    def exchange(value):
        return lax.all_to_all(value, "seq", 0, 0, tiled=True)

    def shared(value):
        out = [value]
        for r in range(1, blocks):
            out.append(lax.ppermute(value, "seq", [(i, i ^ r) for i in range(seq_size)]))
        return out

    def gathered(value):
        out = [value]
        for r in range(1, data_size):
            out.append(lax.ppermute(value, "dp", [(i, i ^ r) for i in range(data_size)]))
        every = jnp.stack(out)
        return jnp.concatenate([lax.dynamic_slice_in_dim(every, data_at ^ i, 1, axis=0) for i in range(data_size)])

    def scattered(value, *others):
        total = at_block(value, data_at, 0).astype(F32)
        for r in range(1, data_size):
            sent = at_block(value, data_at ^ r, 0)
            received = lax.ppermute(sent, "dp", [(i, i ^ r) for i in range(data_size)])
            if others and r == data_size - 1:
                received = after(received, *others)
            total += received.astype(F32)
        return total

    def over_groups(value, *others):
        step = 1
        while step < groups:
            pairs = [(i, i ^ (step * blocks)) for i in range(seq_size)]
            sent = value.astype(BF16)
            received = lax.ppermute(sent, "seq", pairs)
            if others:
                received = after(received, *others)
            value = sent.astype(F32) + received.astype(F32)
            step *= 2
        return value.astype(BF16)

    fout_parts = []
    for q in range(groups):
        pairs = [(groups * (i % blocks) + (i // blocks + q) % groups, i) for i in range(seq_size)]
        fout_parts.append(lax.ppermute(filter_out, "seq", pairs))
    fout_every = jnp.stack(fout_parts)
    fout_block = jnp.concatenate(
        [at_block(fout_every, (i - group) % groups, 0) for i in range(groups)], axis=1
    )

    packed_tokens = after(pack_tokens(tokens), *fout_parts)
    payload = exchange(packed_tokens)
    counts = lax.dynamic_slice_in_dim(lengths, 2 * group, 2, axis=0)

    small = jnp.concatenate(
        [
            norm_gain.reshape(-1),
            norm_bias.reshape(-1),
            conv_taps.reshape(-1),
            filter_in.reshape(-1),
            filter_bias.reshape(-1),
            filter_mid.reshape(-1),
            fout_block.reshape(-1),
        ]
    )
    small_size = -(-small.shape[0] // 2048) * 2048
    small = jnp.pad(small, (0, small_size - small.shape[0])).reshape(-1, 128)
    small_all = gathered(small).reshape(data_size, small_size)
    shard = features // data_size
    hidden_shard = filter_in.shape[1]
    cuts = np.cumsum(
        [0, 2 * shard, 2 * shard, 9 * shard, 5 * hidden_shard, 2 * hidden_shard, 128 * hidden_shard, width * hidden_shard]
    )
    pieces = [small_all[:, cuts[i] : cuts[i + 1]] for i in range(7)]

    def channels(piece, lead):
        whole = jnp.moveaxis(piece.reshape(data_size, lead, shard), 0, 1).reshape(lead, features)
        return lax.dynamic_slice_in_dim(whole, block * width, width, axis=1).astype(F32)

    gains = pair_lanes(channels(pieces[0], 2))
    offsets = pair_lanes(channels(pieces[1], 2))
    taps = channels(pieces[2], 9)
    fin = jnp.moveaxis(pieces[3].reshape(data_size, 5, hidden_shard), 0, 1).reshape(5, 128)
    fbias = jnp.moveaxis(pieces[4].reshape(data_size, 2, hidden_shard), 0, 1).reshape(2, 128)
    fmid = pieces[5].reshape(128, 128)
    fout = doubled(pieces[6].reshape(128, width), 1)
    fin_stack = jnp.concatenate([fin, fin, fin, jnp.zeros((1, 128), BF16)], axis=0)
    channel_ids = block * width + jnp.arange(width, dtype=jnp.int32)
    fast, slow = math.log(100.0) / 0.3, math.log(100.0) / 1.5
    rates = slow + (fast - slow) * channel_ids.astype(F32) / float(features - 1)
    rates = doubled(rates[None, :], 1)

    part = width // data_size
    large = own_block(block_at, in_weight, out_weight, up_weight, down_weight, packed_tokens)
    large_all = lax.all_gather(large, "dp", axis=0, tiled=False)
    taps_wide = doubled(taps, 1).reshape(3, 768)
    w_in_flat, w_taps, w_taps_t, w_out, w_out_t, w_up, w_up_t, w_down, w_down_t = whole_weights(large_all, taps_wide)

    first_np, second_np = stage_tables()
    full_first = jnp.asarray(first_np, BF16)
    full_last = jnp.asarray(np.swapaxes(first_np, 1, 2), BF16)
    second = jnp.asarray(second_np, BF16)
    third = jnp.asarray(second_np.T, BF16)
    tables = (full_first, second, third, full_last)
    feats = jnp.asarray(lag_table(total), BF16)

    hidden = make_filter(
        feats,
        fin_stack,
        fbias.astype(F32),
        jnp.concatenate([fmid, fmid, fmid], axis=0),
        jnp.concatenate([fout, fout], axis=0),
        rates,
        full_first,
        second,
    )
    spectrum = hidden[4]
    hidden = hidden[:4]

    cot = exchange(pack_cotangent(cotangent, spectrum))
    short, spec, conv, middle, stats = mixer_forward(
        counts, payload, gains[0:1], offsets[0:1], w_taps, w_out, spectrum, tables
    )

    out, pair_low, normed_low, unit, norm = feed_forward(
        middle, shared(stats), gains[1:2], offsets[1:2], w_up, w_down
    )
    out = exchange(after(out, cot))
    q, sums, ffn, small_two = feed_back(
        cot, pair_low, normed_low, unit, gains[1:2], w_up_t, w_down_t, data_size
    )
    sums = shared(sums)
    ffn = scattered(ffn).astype(BF16)

    grad, cross, grads, back, small_one = mixer_backward(
        counts,
        norm,
        sums,
        w_out_t,
        gains[0:1],
        offsets[0:1],
        payload,
        w_taps_t,
        cot.reshape(total, 384),
        q,
        unit,
        conv,
        short,
        spec,
        spectrum,
        tables,
    )
    ffn = over_groups(ffn)
    back = exchange(after(back, out, ffn))
    ffn_pieces = shared(ffn)
    g_mixer, g_taps = mixer_grads(
        counts,
        payload,
        gains[0:1],
        offsets[0:1],
        jnp.pad(taps, ((0, 0), (0, 256 - width))),
        w_in_flat,
        grads,
        grad,
        conv,
        short,
        data_size,
    )
    out_tokens = unpack_out(out)
    grad_tokens = unpack_grad(back, tokens)
    own = filter_back(
        cross, hidden, feats, fmid.T, fout.T, rates, third, full_last, g_mixer, g_taps, small_one, small_two
    )
    own = over_groups(scattered(own, out_tokens), grad_tokens)
    cols = features // seq_size
    places = [
        block,
        data_at * shard // width,
        data_at * shard % width,
        data_at * hidden_shard,
        place // groups,
        place % groups * cols,
    ]
    finished = finish_mixer(jnp.stack(places).astype(jnp.int32), shared(own), part, hidden_shard, shard, cols)
    grad_in, grad_outw, grad_mid, grad_gain, grad_bias, grad_taps, grad_fin, grad_fbias, grad_fout = finished
    grad_up, grad_down = finish_ffn(block_at, [after(ffn_pieces[0], own)] + ffn_pieces[1:])
    return (
        out_tokens,
        grad_tokens,
        grad_gain,
        grad_bias,
        grad_in,
        grad_taps,
        grad_fin,
        grad_mid,
        grad_fbias,
        grad_fout,
        grad_outw,
        grad_up,
        grad_down,
    )


def solution(mesh):
    placed = (
        P("dp", "seq", None),
        P("dp"),
        P("dp", "seq", None),
        P(None, "dp"),
        P(None, "dp"),
        P(None, None, "dp", None),
        P(None, None, "dp"),
        P(None, "dp"),
        P("dp", None),
        P(None, "dp"),
        P("dp", "seq"),
        P(None, "dp", None),
        P(None, None, "dp", None),
        P(None, "dp", None),
    )
    return jax.shard_map(
        per_device,
        mesh=mesh,
        in_specs=placed,
        out_specs=(
            P("dp", "seq", None),
            P("dp", "seq", None),
            P(None, "dp"),
            P(None, "dp"),
            P(None, None, "dp", None),
            P(None, None, "dp"),
            P(None, "dp"),
            P("dp", None),
            P(None, "dp"),
            P("dp", "seq"),
            P(None, "dp", None),
            P(None, None, "dp", None),
            P(None, "dp", None),
        ),
        check_vma=False,
    )
```

```python
import functools
import math

import jax
import jax.numpy as jnp
import numpy as np
from jax import lax
from jax.experimental import pallas as pl
from jax.experimental.pallas import tpu as pltpu
from jax.sharding import PartitionSpec as P

F32 = jnp.float32
BF16 = jnp.bfloat16
EPS = 1e-05
SINE_FREQ = 10.0
GROUP = 3
COLS = 128
HALF_ROWS = 16
FULL_ROWS = 32
FREQ_ROWS = 17
STAT_ROWS = 16
GROUPED = 2
VMEM = pltpu.CompilerParams(vmem_limit_bytes=56 * 1024 * 1024)
WIDE_VMEM = pltpu.CompilerParams(vmem_limit_bytes=60 * 1024 * 1024)


def stage_tables():
    k1 = np.arange(FREQ_ROWS)[:, None, None]
    t1 = np.arange(FULL_ROWS)[None, :, None]
    t2 = np.arange(COLS)[None, None, :]
    phase = 2.0 * np.pi * ((k1 * (t1 * COLS + t2)) % 4096) / 4096.0
    both = np.stack([np.cos(phase), -np.sin(phase)], axis=1)
    out = np.zeros((8, FREQ_ROWS, 2, 16, FULL_ROWS, 16), np.float32)
    for a in range(16):
        out[:, :, :, a, :, a] = np.moveaxis(both[..., a::16], -1, 0)
    first = out.reshape(8, FREQ_ROWS * 32, FULL_ROWS * 16)
    theta = 2.0 * np.pi * (np.outer(np.arange(COLS), np.arange(COLS)) % COLS) / COLS
    second = np.block([[np.cos(theta), np.sin(theta)], [-np.sin(theta), np.cos(theta)]])
    return first, second


def lag_table(seq_total):
    lags = np.arange(2 * seq_total)
    scaled = np.where(lags < seq_total, lags, lags - 2 * seq_total) / float(seq_total)
    feats = np.stack(
        [
            scaled,
            np.cos(np.pi * scaled),
            np.sin(np.pi * scaled),
            np.cos(2.0 * np.pi * scaled),
            np.sin(2.0 * np.pi * scaled),
        ],
        axis=1,
    ).astype(np.float32)
    parts, rest = [], feats
    for _ in range(3):
        piece = rest.astype(jnp.bfloat16)
        parts.append(piece.astype(np.float32))
        rest = rest - piece.astype(np.float32)
    table = np.zeros((2 * seq_total, 16), np.float32)
    table[:, :15] = np.concatenate(parts, axis=1)
    return table


def dot(a, b):
    return jnp.dot(a, b, preferred_element_type=F32)


def low_lanes(rows):
    return lax.broadcasted_iota(jnp.int32, (rows, 128), 1) < 64


def tiles(value):
    return [value[:, 128 * i : 128 * (i + 1)] for i in range(value.shape[1] // 128)]


def half_turn(value):
    return pltpu.roll(value, 64, axis=1)


def stacked(value):
    first, second, last = tiles(value)
    low = low_lanes(value.shape[0])
    zero = jnp.zeros_like(last)
    return jnp.concatenate(
        [
            jnp.concatenate([first, jnp.where(low, last, zero)], axis=1),
            jnp.concatenate([second, jnp.where(low, zero, last)], axis=1),
        ],
        axis=0,
    )


def packed(value):
    rows = value.shape[0] // 2
    low = low_lanes(rows)
    last = jnp.where(low, value[:rows, 128:], value[rows:, 128:])
    return jnp.concatenate([value[:rows, :128], value[rows:, :128], last], axis=1)


def pair_sum(value):
    first, second, last = tiles(value)
    low = low_lanes(value.shape[0])
    zero = jnp.zeros_like(last)
    return (
        jnp.sum(first + jnp.where(low, last, zero), axis=1, keepdims=True),
        jnp.sum(second + jnp.where(low, zero, last), axis=1, keepdims=True),
    )


def spread(col_a, col_b, rows):
    wide_a = jnp.broadcast_to(col_a, (rows, 128))
    wide_b = jnp.broadcast_to(col_b, (rows, 128))
    return jnp.concatenate([wide_a, wide_b, jnp.where(low_lanes(rows), wide_a, wide_b)], axis=1)


def to_rows(columns, rows):
    lane = lax.broadcasted_iota(jnp.int32, (rows, 128), 1)
    out = jnp.zeros((rows, 128), F32)
    for at, column in enumerate(columns):
        out = jnp.where(lane == at, jnp.broadcast_to(column, (rows, 128)), out)
    if rows % 128:
        out = jnp.concatenate([out, jnp.zeros((128 - rows, 128), F32)], axis=0)
    return out.T[:8, :rows]


def to_columns(values):
    rows = values.shape[1]
    if rows % 128:
        values = jnp.concatenate([values, jnp.zeros((8, 128 - rows), F32)], axis=1)
    tall = jnp.concatenate([values, jnp.zeros((120, values.shape[1]), F32)], axis=0)
    return tall.T[:rows]


def split_rows(values):
    high = values.astype(BF16).astype(F32)
    return jnp.concatenate([high, values - high], axis=0).astype(BF16)


def join_rows(values):
    wide = values.astype(F32)
    return wide[:8] + wide[8:]


def position_mask(start, rows, count_a, count_b):
    place = start + lax.broadcasted_iota(jnp.int32, (rows, 128), 0)
    keep_a = (place < count_a).astype(F32)
    keep_b = (place < count_b).astype(F32)
    return jnp.concatenate([keep_a, keep_b, jnp.where(low_lanes(rows), keep_a, keep_b)], axis=1)


def sine_pair(angle):
    turns = jnp.floor(angle * (1.0 / math.pi) + 0.5)
    rest = angle - turns * 3.140625
    rest = rest - turns * 9.675025939941406e-4
    rest = rest - turns * 1.5099579909783764e-7
    half = turns * 0.5
    sign = 1.0 - 4.0 * (half - jnp.floor(half))
    square = rest * rest
    sine = square * (-1.0 / 39916800.0) + 1.0 / 362880.0
    sine = sine * square - 1.0 / 5040.0
    sine = sine * square + 1.0 / 120.0
    sine = sine * square - 1.0 / 6.0
    sine = rest + rest * square * sine
    cosine = square * (1.0 / 479001600.0) - 1.0 / 3628800.0
    cosine = cosine * square + 1.0 / 40320.0
    cosine = cosine * square - 1.0 / 720.0
    cosine = cosine * square + 1.0 / 24.0
    cosine = cosine * square - 0.5
    cosine = 1.0 + square * cosine
    return sine * sign, cosine * sign


def normal_cdf(value):
    return 0.5 + 0.5 * lax.erf(value * math.sqrt(0.5))


def normal_density(value):
    return jnp.exp(value * value * -0.5) * (1.0 / math.sqrt(2.0 * math.pi))


def work(micros):
    return pl.CostEstimate(flops=int(micros * 1.15e9), bytes_accessed=0, transcendentals=0)


def pass_kernel(*refs):
    pass


def after(value, *others):
    anywhere = pl.BlockSpec(memory_space=pl.ANY)
    return pl.pallas_call(
        pass_kernel,
        in_specs=[anywhere] * (1 + len(others)),
        out_specs=anywhere,
        out_shape=jax.ShapeDtypeStruct(value.shape, value.dtype),
        input_output_aliases={0: 0},
        name="after",
    )(value, *others)


def pack_pair(a, b, block):
    rows = a.shape[0]
    low = low_lanes(rows)
    base = 3 * (block // 2)
    ta = [a[:, 128 * (base + i) : 128 * (base + i + 1)] for i in range(3)]
    tb = [b[:, 128 * (base + i) : 128 * (base + i + 1)] for i in range(3)]
    if block % 2 == 0:
        parts = [ta[0], tb[0], jnp.where(low, ta[1], half_turn(tb[1]))]
    else:
        parts = [
            jnp.where(low, half_turn(ta[1]), half_turn(ta[2])),
            jnp.where(low, half_turn(tb[1]), half_turn(tb[2])),
            jnp.where(low, half_turn(ta[2]), tb[2]),
        ]
    return jnp.concatenate(parts, axis=1)


def unpack_pairs(even, odd):
    low = low_lanes(even.shape[0])
    ea, eb, el = tiles(even)
    oa, ob, ol = tiles(odd)
    a = [ea, jnp.where(low, el, half_turn(oa)), jnp.where(low, half_turn(oa), half_turn(ol))]
    b = [eb, jnp.where(low, half_turn(el), half_turn(ob)), jnp.where(low, half_turn(ob), ol)]
    return jnp.concatenate(a, axis=1), jnp.concatenate(b, axis=1)


def row_stats(value):
    mean = jnp.mean(value, axis=1, keepdims=True)
    centred = value - mean
    variance = jnp.mean(centred * centred, axis=1, keepdims=True)
    return mean, lax.rsqrt(variance + EPS)


def pack_tokens_kernel(x_ref, out_ref):
    rows = x_ref.shape[1]
    a = x_ref[0].astype(F32)
    b = x_ref[1].astype(F32)
    stats = split_rows(to_rows(row_stats(a) + row_stats(b), rows))
    for block in range(4):
        out_ref[block, :rows, :] = pack_pair(a, b, block).astype(BF16)
        out_ref[block, rows:, :rows] = stats


def pack_tokens(tokens):
    count, rows, width = tokens.shape
    return pl.pallas_call(
        pack_tokens_kernel,
        grid=(count // 2,),
        in_specs=[pl.BlockSpec((2, rows, width), lambda i: (i, 0, 0))],
        out_specs=pl.BlockSpec((4, rows + STAT_ROWS, 384), lambda i: (i, 0, 0)),
        out_shape=jax.ShapeDtypeStruct((2 * count, rows + STAT_ROWS, 384), BF16),
        compiler_params=VMEM,
        cost_estimate=work(3.3),
        name="pack_tokens",
    )(tokens)


def pack_cotangent_kernel(x_ref, after_ref, out_ref):
    a = x_ref[0].astype(F32)
    b = x_ref[1].astype(F32)
    for block in range(4):
        out_ref[block] = pack_pair(a, b, block).astype(BF16)


def pack_cotangent(cotangent, after):
    count, rows, width = cotangent.shape
    return pl.pallas_call(
        pack_cotangent_kernel,
        grid=(count // 2,),
        in_specs=[
            pl.BlockSpec((2, rows, width), lambda i: (i, 0, 0)),
            pl.BlockSpec(memory_space=pl.ANY),
        ],
        out_specs=pl.BlockSpec((4, rows, 384), lambda i: (i, 0, 0)),
        out_shape=jax.ShapeDtypeStruct((2 * count, rows, 384), BF16),
        compiler_params=VMEM,
        cost_estimate=work(0.5),
        name="pack_cotangent",
    )(cotangent, after)


def transform_first(table_ref, data_ref, spec_ref):
    count, _, lanes = data_ref.shape

    def one(j, carry):
        start = pl.ds(pl.multiple_of(16 * j, 16), 16)
        block = data_ref[:, start, :].reshape(count * 16, lanes)
        part = dot(table_ref[j], block).astype(BF16)
        spec_ref[:, start, :] = part.reshape(2 * FREQ_ROWS, 16, lanes)
        return carry

    lax.fori_loop(0, 8, one, 0, unroll=True)


def frequency_weight(k1):
    edge = jnp.logical_or(k1 == 0, k1 == FREQ_ROWS - 1)
    return jnp.where(edge, 1.0 / 4096.0, 2.0 / 4096.0).astype(F32)


def make_filter_kernel(
    feat_ref,
    fin_ref,
    bias_ref,
    mid_ref,
    fout_ref,
    rate_ref,
    table_ref,
    second_ref,
    s1_ref,
    c1_ref,
    s2_ref,
    c2_ref,
    spec_ref,
    taps_ref,
    work_ref,
):
    step_rows = 256
    total = feat_ref.shape[0]

    def one(i, carry):
        rows = pl.ds(pl.multiple_of(i * step_rows, step_rows), step_rows)
        inner = dot(feat_ref[rows, :], fin_ref[...]) + bias_ref[0:1, :]
        s1, c1 = sine_pair(SINE_FREQ * inner)
        s1_ref[rows, :] = s1.astype(BF16)
        c1_ref[rows, :] = c1.astype(BF16)
        p1 = s1.astype(BF16)
        r1 = s1 - p1.astype(F32)
        p2 = r1.astype(BF16)
        p3 = (r1 - p2.astype(F32)).astype(BF16)
        outer = dot(jnp.concatenate([p1, p2, p3], axis=1), mid_ref[...]) + bias_ref[1:2, :]
        s2, c2 = sine_pair(SINE_FREQ * outer)
        s2_ref[rows, :] = s2.astype(BF16)
        c2_ref[rows, :] = c2.astype(BF16)
        q1 = s2.astype(BF16)
        q2 = (s2 - q1.astype(F32)).astype(BF16)
        raw = dot(jnp.concatenate([q1, q2], axis=1), fout_ref[...])
        lag = i * step_rows + lax.broadcasted_iota(jnp.int32, (step_rows, 256), 0)
        signed = jnp.where(lag < total // 2, lag, total - lag)
        distance = signed.astype(F32) * (2.0 / total)
        kernel = raw * jnp.exp(-distance * rate_ref[...])
        taps_ref[pl.ds(2 * i, 2), :, :] = kernel.astype(BF16).reshape(2, COLS, 256)
        return carry

    lax.fori_loop(0, total // step_rows, one, 0, unroll=True)
    transform_first(table_ref, taps_ref, work_ref)

    def second(k1, carry):
        part = work_ref[pl.ds(2 * k1, 2), :, :].reshape(256, 256)
        spec_ref[k1] = (dot(second_ref[...], part) * frequency_weight(k1)).astype(BF16)
        return carry

    lax.fori_loop(0, FREQ_ROWS, second, 0, unroll=True)


def make_filter(feats, fin, bias, mid, fout, rate, table, second):
    total = feats.shape[0]
    hidden = jax.ShapeDtypeStruct((total, 128), BF16)
    return pl.pallas_call(
        make_filter_kernel,
        out_shape=(hidden,) * 4 + (jax.ShapeDtypeStruct((FREQ_ROWS, 256, 256), BF16),),
        scratch_shapes=[
            pltpu.VMEM((FULL_ROWS, COLS, 256), BF16),
            pltpu.VMEM((2 * FREQ_ROWS, COLS, 256), BF16),
        ],
        compiler_params=VMEM,
        cost_estimate=work(2),
        name="make_filter",
    )(feats, fin, bias, mid, fout, rate, table, second)


def normed_pair(payload, rows, scales, offsets):
    value = payload[:rows].astype(F32)
    stats = to_columns(join_rows(payload[rows:, :rows]))
    mean = spread(stats[:, 0:1], stats[:, 2:3], rows)
    scale = spread(stats[:, 1:2], stats[:, 3:4], rows)
    unit = (value - mean) * scale
    return unit, scale, unit * scales + offsets


def filter_lanes(block):
    return jnp.concatenate([block[:, :128], block], axis=1)


def full_spec(shape):
    return pl.BlockSpec(shape, lambda i: (0,) * len(shape))


ANYWHERE = pl.BlockSpec(memory_space=pl.ANY)


def three_shifts(window, rows):
    return window[7 : 7 + rows], window[8 : 8 + rows], window[9 : 9 + rows]


def mixer_forward_kernel(
    counts_ref,
    x_ref,
    scales_ref,
    offsets_ref,
    w_ref,
    wout_ref,
    second_ref,
    third_ref,
    first_hbm,
    fourth_hbm,
    filter_hbm,
    short_hbm,
    spec_hbm,
    conv_hbm,
    middle_hbm,
    stats_ref,
    first_ref,
    fourth_ref,
    filter_ref,
    normed_ref,
    short_ref,
    values_ref,
    work_ref,
    spec_ref,
    conv_ref,
    gated_ref,
    middle_ref,
    in_sems,
    out_sems,
):
    chunks, tall, _ = x_ref.shape
    rows = tall - STAT_ROWS
    total = chunks * rows
    size = 256
    count_a, count_b = counts_ref[0], counts_ref[1]
    loads = [
        pltpu.make_async_copy(src, dst, in_sems.at[i])
        for i, (src, dst) in enumerate(
            (
                (first_hbm.at[:, :, pl.ds(0, HALF_ROWS * 16)], first_ref),
                (filter_hbm, filter_ref),
                (fourth_hbm.at[:, pl.ds(0, HALF_ROWS * 16), :], fourth_ref),
            )
        )
    ]
    stores = [
        pltpu.make_async_copy(src, dst, out_sems.at[i])
        for i, (src, dst) in enumerate(
            (
                (short_ref, short_hbm),
                (spec_ref, spec_hbm),
                (conv_ref, conv_hbm),
                (middle_ref, middle_hbm),
            )
        )
    ]
    for load in loads:
        load.start()

    edge = jnp.zeros((8, 384), F32)
    normed_ref[0:8, :] = edge
    normed_ref[8 + total :, :] = edge
    for c in range(chunks):
        _, _, normed = normed_pair(x_ref[c], rows, scales_ref[...], offsets_ref[...])
        keep = position_mask(c * rows, rows, count_a, count_b)
        normed_ref[8 + c * rows : 8 + (c + 1) * rows, :] = normed * keep
    for b in range(total // size):
        at = slice(size * b, size * (b + 1))
        window = normed_ref[size * b : size * (b + 1) + 16, :]
        wide = jnp.concatenate([stacked(v).astype(BF16) for v in three_shifts(window, size)], axis=1)
        out = dot(wide, w_ref[...])
        shorts = [packed(out[:, 256 * s : 256 * (s + 1)]) for s in range(3)]
        for s in range(3):
            short_ref[s, at, :] = shorts[s].astype(BF16)
        keep = position_mask(size * b, size, count_a, count_b)
        values = (shorts[2] * shorts[0] * keep).astype(BF16)
        values_ref[2 * b : 2 * b + 2, :, :] = values.reshape(2, COLS, 384)
    stores[0].start()

    loads[0].wait()
    transform_first(first_ref, values_ref, work_ref)
    loads[1].wait()

    def middle(k1, carry):
        part = work_ref[pl.ds(2 * k1, 2), :, :].reshape(256, 384)
        spec = dot(second_ref[...], part)
        spec_ref[k1] = spec.astype(BF16)
        re, im = spec[:128], spec[128:]
        block = filter_ref[k1].astype(F32)
        fre, fim = filter_lanes(block[:128]), filter_lanes(block[128:])
        prod = jnp.concatenate([re * fre - im * fim, re * fim + im * fre], axis=0).astype(BF16)
        work_ref[pl.ds(2 * k1, 2), :, :] = dot(third_ref[...], prod).astype(BF16).reshape(2, COLS, 384)
        return carry

    lax.fori_loop(0, FREQ_ROWS, middle, 0, unroll=True)
    stores[1].start()
    loads[2].wait()
    for j in range(8):
        part = work_ref[:, 16 * j : 16 * (j + 1), :].reshape(FREQ_ROWS * 32, 384)
        conv = dot(fourth_ref[j], part)
        for i in range(HALF_ROWS):
            at = slice(COLS * i + 16 * j, COLS * i + 16 * (j + 1))
            piece = conv[16 * i : 16 * (i + 1)]
            conv_ref[at, :] = piece.astype(BF16)
            gated_ref[at, :] = (piece * short_ref[1, at, :].astype(F32)).astype(BF16)
    stores[2].start()
    for c in range(chunks):
        at = slice(rows * c, rows * (c + 1))
        out = packed(dot(stacked(gated_ref[at, :]), wout_ref[...]))
        value = x_ref[c, :rows, :].astype(F32) + out
        middle_ref[at, :] = value
        sum_a, sum_b = pair_sum(value)
        mean_a, mean_b = sum_a * (1.0 / 192.0), sum_b * (1.0 / 192.0)
        centred = value - spread(mean_a, mean_b, rows)
        square_a, square_b = pair_sum(centred * centred)
        stats_ref[c] = to_rows((mean_a, square_a, mean_b, square_b), rows)
    stores[3].start()
    for store in stores:
        store.wait()


def mixer_forward(counts, payload, scales, offsets, weight, wout, spectrum, tables):
    chunks, tall, _ = payload.shape
    rows = tall - STAT_ROWS
    total = chunks * rows
    first, second, third, fourth = tables
    seq = (total, 384)
    wide = (FREQ_ROWS, 256, 384)
    return pl.pallas_call(
        mixer_forward_kernel,
        grid=(1,),
        in_specs=[pl.BlockSpec(memory_space=pltpu.SMEM)]
        + [full_spec(a.shape) for a in (payload, scales, offsets, weight, wout, second, third)]
        + [ANYWHERE] * 3,
        out_specs=[ANYWHERE] * 4 + [full_spec((chunks, 8, rows))],
        out_shape=[
            jax.ShapeDtypeStruct((3,) + seq, BF16),
            jax.ShapeDtypeStruct(wide, BF16),
            jax.ShapeDtypeStruct(seq, BF16),
            jax.ShapeDtypeStruct(seq, F32),
            jax.ShapeDtypeStruct((chunks, 8, rows), F32),
        ],
        scratch_shapes=[
            pltpu.VMEM(first.shape[:2] + (HALF_ROWS * 16,), BF16),
            pltpu.VMEM((8, HALF_ROWS * 16, fourth.shape[2]), BF16),
            pltpu.VMEM(spectrum.shape, BF16),
            pltpu.VMEM((total + 16, 384), F32),
            pltpu.VMEM((3,) + seq, BF16),
            pltpu.VMEM((HALF_ROWS, COLS, 384), BF16),
            pltpu.VMEM((2 * FREQ_ROWS, COLS, 384), BF16),
            pltpu.VMEM(wide, BF16),
            pltpu.VMEM(seq, BF16),
            pltpu.VMEM(seq, BF16),
            pltpu.VMEM(seq, F32),
            pltpu.SemaphoreType.DMA((3,)),
            pltpu.SemaphoreType.DMA((4,)),
        ],
        compiler_params=VMEM,
        cost_estimate=work(25),
        name="mixer_forward",
    )(counts, payload, scales, offsets, weight, wout, second, third, first, fourth, spectrum)


def column_sums(value):
    return jnp.sum(value.reshape(value.shape[0] // 8, 8, value.shape[1]), axis=0)


def fold_rows(value):
    return jnp.concatenate([value[:128], value[128:192] + value[192:256]], axis=0)


def fold_lanes(value):
    last = value[:, 128:]
    summed = jnp.where(low_lanes(value.shape[0]), last + half_turn(last), jnp.zeros_like(last))
    return jnp.concatenate([value[:, :128], summed], axis=1)


def feed_forward_kernel(
    middle_ref,
    s0_ref,
    s1_ref,
    s2_ref,
    s3_ref,
    scales_ref,
    offsets_ref,
    up_ref,
    down_ref,
    out_ref,
    pair_ref,
    normed_ref,
    unit_ref,
    norm_ref,
):
    chunks, rows, _ = out_ref.shape
    for c in range(chunks):
        at_rows = slice(rows * c, rows * (c + 1))
        parts = [ref[c] for ref in (s0_ref, s1_ref, s2_ref, s3_ref)]
        mean = (parts[0] + parts[1] + parts[2] + parts[3]) * 0.25
        spread_sum = jnp.zeros_like(mean)
        for part in parts:
            gap = part - mean
            spread_sum += 192.0 * gap * gap
        squares = parts[0] + parts[1] + parts[2] + parts[3]
        scale_a = lax.rsqrt((squares[1:2] + spread_sum[0:1]) * (1.0 / 768.0) + EPS)
        scale_b = lax.rsqrt((squares[3:4] + spread_sum[2:3]) * (1.0 / 768.0) + EPS)
        norm = jnp.concatenate([mean[0:1], scale_a, mean[2:3], scale_b, jnp.zeros((4, rows), F32)], axis=0)
        norm_ref[c] = norm
        columns = to_columns(norm)
        middle = middle_ref[at_rows, :]
        unit = (middle - spread(columns[:, 0:1], columns[:, 2:3], rows)) * spread(columns[:, 1:2], columns[:, 3:4], rows)
        unit_ref[at_rows, :] = unit.astype(BF16)
        normed = stacked(unit * scales_ref[...] + offsets_ref[...]).astype(BF16)
        normed_ref[c] = normed
        hiddens = []
        width = 256
        for f in range(768 // width):
            at = slice(width * f, width * (f + 1))
            at_up = slice(768 + width * f, 768 + width * (f + 1))
            gate = dot(normed, up_ref[:, at])
            upper = dot(normed, up_ref[:, at_up])
            pair_ref[c, :, at] = gate.astype(BF16)
            pair_ref[c, :, at_up] = upper.astype(BF16)
            hiddens.append((gate * normal_cdf(gate) * upper).astype(BF16))
        down = dot(jnp.concatenate(hiddens, axis=1), down_ref[...])
        out_ref[c] = (middle + packed(down)).astype(BF16)


def feed_forward(middle, stats, scales, offsets, up, down):
    chunks, _, rows = stats[0].shape
    total = chunks * rows
    many = min(chunks, GROUPED)
    stat_spec = pl.BlockSpec((many, 8, rows), lambda i: (i, 0, 0))
    rows_spec = pl.BlockSpec((many * rows, 384), lambda i: (i, 0))
    return pl.pallas_call(
        feed_forward_kernel,
        grid=(chunks // many,),
        in_specs=[rows_spec] + [stat_spec] * 4 + [full_spec(a.shape) for a in (scales, offsets, up, down)],
        out_specs=[
            pl.BlockSpec((many, rows, 384), lambda i: (i, 0, 0)),
            pl.BlockSpec((many, 2 * rows, 1536), lambda i: (i, 0, 0)),
            pl.BlockSpec((many, 2 * rows, 256), lambda i: (i, 0, 0)),
            rows_spec,
            stat_spec,
        ],
        out_shape=[
            jax.ShapeDtypeStruct((chunks, rows, 384), BF16),
            jax.ShapeDtypeStruct((chunks, 2 * rows, 1536), BF16),
            jax.ShapeDtypeStruct((chunks, 2 * rows, 256), BF16),
            jax.ShapeDtypeStruct((total, 384), BF16),
            jax.ShapeDtypeStruct((chunks, 8, rows), F32),
        ],
        compiler_params=VMEM,
        cost_estimate=work(11),
        name="feed_forward",
    )(middle, *stats, scales, offsets, up, down)


def feed_back_kernel(
    cot_ref,
    pair_ref,
    normed_ref,
    unit_ref,
    scales_ref,
    upt_ref,
    downt_ref,
    q_ref,
    sums_ref,
    gffn_ref,
    small_ref,
    up_acc,
    down_acc,
):
    chunks, rows, _ = cot_ref.shape
    step = pl.program_id(0)

    @pl.when(step == 0)
    def _():
        small_ref[...] = jnp.zeros_like(small_ref)
        up_acc[...] = jnp.zeros_like(up_acc)
        down_acc[...] = jnp.zeros_like(down_acc)

    join = lambda parts: jnp.concatenate(parts, axis=0)
    cot = join([stacked(cot_ref[c]) for c in range(chunks)])
    size = 2 * rows * chunks
    grad_hidden = dot(cot, downt_ref[...])
    hidden, gates, uppers = [], [], []
    width = 256
    for f in range(768 // width):
        at = slice(width * f, width * (f + 1))
        at_up = slice(768 + width * f, 768 + width * (f + 1))
        gate = pair_ref[:, :, at].reshape(size, width).astype(F32)
        upper = pair_ref[:, :, at_up].reshape(size, width).astype(F32)
        cdf = normal_cdf(gate)
        active = gate * cdf
        hidden.append((active * upper).astype(BF16))
        gates.append((grad_hidden[:, at] * upper * (cdf + gate * normal_density(gate))).astype(BF16))
        uppers.append((grad_hidden[:, at] * active).astype(BF16))
    hidden = jnp.concatenate(hidden, axis=1)
    grads = jnp.concatenate(gates + uppers, axis=1)
    back = dot(grads, upt_ref[...])
    up_acc[...] += fold_rows(dot(normed_ref[...].reshape(size, 256).T, grads))
    down_acc[...] += dot(cot.T, hidden)
    for c in range(chunks):
        at_rows = slice(rows * c, rows * (c + 1))
        grad = packed(back[2 * rows * c : 2 * rows * (c + 1)])
        unit = unit_ref[at_rows, :].astype(F32)
        q = grad * scales_ref[...]
        q_ref[at_rows, :] = q.astype(BF16)
        sums_ref[c] = to_rows(pair_sum(q) + pair_sum(q * unit), rows)
        small_ref[0:8, :] += column_sums(grad * unit)
        small_ref[8:16, :] += column_sums(grad)

    @pl.when(step == pl.num_programs(0) - 1)
    def _():
        parts = gffn_ref.shape[0]
        share = 192 // parts
        down = fold_lanes(down_acc[...].T).astype(BF16)
        for d in range(parts):
            for t in range(6):
                value = up_acc[share * d : share * (d + 1), 256 * t : 256 * (t + 1)]
                gffn_ref[d, share * t : share * (t + 1), :] = value.astype(BF16)
            gffn_ref[d, 6 * share :, :] = down[4 * share * d : 4 * share * (d + 1)]


def feed_back(cot, pair, normed, unit, scales, upt, downt, parts):
    chunks, rows, _ = cot.shape
    total = chunks * rows
    many = min(chunks, GROUPED)
    rows_spec = pl.BlockSpec((many * rows, 384), lambda i: (i, 0))
    spec = lambda shape: pl.BlockSpec((many,) + shape[1:], lambda i: (i, 0, 0))
    stats = (chunks, 8, rows)
    return pl.pallas_call(
        feed_back_kernel,
        grid=(chunks // many,),
        in_specs=[spec(cot.shape), spec(pair.shape), spec(normed.shape), rows_spec]
        + [full_spec(a.shape) for a in (scales, upt, downt)],
        out_specs=[rows_spec, spec(stats), full_spec((parts, 1920 // parts, 256)), full_spec((16, 384))],
        out_shape=[
            jax.ShapeDtypeStruct((total, 384), BF16),
            jax.ShapeDtypeStruct(stats, F32),
            jax.ShapeDtypeStruct((parts, 1920 // parts, 256), BF16),
            jax.ShapeDtypeStruct((16, 384), F32),
        ],
        scratch_shapes=[pltpu.VMEM((192, 1536), F32), pltpu.VMEM((256, 768), F32)],
        compiler_params=VMEM,
        cost_estimate=work(2),
        name="feed_back",
    )(cot, pair, normed, unit, scales, upt, downt)


def mixer_backward_kernel(
    counts_ref,
    norm_ref,
    s0_ref,
    s1_ref,
    s2_ref,
    s3_ref,
    woutt_ref,
    second_ref,
    third_ref,
    scales_ref,
    offsets_ref,
    x_hbm,
    wt_hbm,
    cot_hbm,
    q_hbm,
    unit_hbm,
    conv_hbm,
    short_hbm,
    first_hbm,
    spec_hbm,
    filter_hbm,
    fourth_hbm,
    grad_hbm,
    cross_hbm,
    grads_hbm,
    out_ref,
    small_ref,
    x_ref,
    wt_ref,
    parts_ref,
    cot_ref,
    q_ref,
    unit_ref,
    conv_ref,
    short_ref,
    first_ref,
    spec_ref,
    filter_ref,
    fourth_ref,
    work_ref,
    cross_ref,
    grads_ref,
    in_sems,
    out_sems,
):
    chunks, _, rows = norm_ref.shape
    total = chunks * rows
    count_a, count_b = counts_ref[0], counts_ref[1]
    half = total // 2
    early, late = pl.ds(0, half), pl.ds(half, half)
    lanes = first_ref.shape[2]
    loads = [
        pltpu.make_async_copy(src, dst, in_sems.at[i])
        for i, (src, dst) in enumerate(
            [
                (src.at[part], dst.at[part])
                for part in (early, late)
                for src, dst in (
                    (cot_hbm, cot_ref),
                    (q_hbm, q_ref),
                    (unit_hbm, unit_ref),
                    (short_hbm.at[1], short_ref.at[1]),
                    (conv_hbm, conv_ref),
                )
            ]
            + [
                (first_hbm.at[:, :, pl.ds(0, lanes)], first_ref),
                (spec_hbm, spec_ref),
                (filter_hbm, filter_ref),
                (fourth_hbm.at[:, pl.ds(0, lanes), :], fourth_ref),
                (short_hbm.at[0], short_ref.at[0]),
                (short_hbm.at[2], short_ref.at[2]),
                (wt_hbm, wt_ref),
                (x_hbm, x_ref),
            ]
        )
    ]
    for load in loads:
        load.start()

    for c in range(chunks):
        if c == 0:
            for load in loads[0:5]:
                load.wait()
        if c == chunks // 2:
            for load in loads[5:10]:
                load.wait()
        at = slice(rows * c, rows * (c + 1))
        sums = (s0_ref[c] + s1_ref[c] + s2_ref[c] + s3_ref[c]) * (1.0 / 768.0)
        columns = to_columns(jnp.concatenate([sums[0:4], norm_ref[c][0:4]], axis=0))
        scale = spread(columns[:, 5:6], columns[:, 7:8], rows)
        mean_q = spread(columns[:, 0:1], columns[:, 1:2], rows)
        mean_qh = spread(columns[:, 2:3], columns[:, 3:4], rows)
        back = q_ref[at, :].astype(F32) - mean_q - unit_ref[at, :].astype(F32) * mean_qh
        grad = cot_ref[at, :].astype(F32) + scale * back
        cot_ref[at, :] = grad.astype(BF16)
        grad_gated = packed(dot(stacked(grad).astype(BF16), woutt_ref[...]))
        unit_ref[at, :] = (grad_gated * short_ref[1, at, :].astype(F32)).astype(BF16)
        grads_ref[1, at, :] = (grad_gated * conv_ref[at, :].astype(F32)).astype(BF16)
    stores = [
        pltpu.make_async_copy(src, dst, out_sems.at[i])
        for i, (src, dst) in enumerate(((cot_ref, grad_hbm), (cross_ref, cross_hbm), (grads_ref, grads_hbm)))
    ]
    stores[0].start()

    loads[10].wait()
    for j in range(8):
        block = jnp.concatenate(
            [unit_ref[COLS * i + 16 * j : COLS * i + 16 * (j + 1), :] for i in range(HALF_ROWS)], axis=0
        )
        part = dot(first_ref[j], block).astype(BF16)
        work_ref[:, 16 * j : 16 * (j + 1), :] = part.reshape(2 * FREQ_ROWS, 16, 384)
    for load in loads[11:13]:
        load.wait()

    def middle(k1, carry):
        part = work_ref[pl.ds(2 * k1, 2), :, :].reshape(256, 384)
        grad = dot(second_ref[...], part)
        re, im = grad[:128], grad[128:]
        spec = spec_ref[k1].astype(F32)
        vre, vim = spec[:128], spec[128:]
        cre = re * vre + im * vim
        cim = im * vre - re * vim
        weight = frequency_weight(k1)
        fold = lambda v: jnp.concatenate([v[:, :128] + v[:, 128:256], v[:, 256:]], axis=1)
        cross_ref[k1] = (jnp.concatenate([fold(cre), fold(cim)], axis=0) * weight).astype(BF16)
        block = filter_ref[k1].astype(F32)
        fre, fim = filter_lanes(block[:128]), filter_lanes(block[128:])
        prod = jnp.concatenate([re * fre + im * fim, im * fre - re * fim], axis=0).astype(BF16)
        work_ref[pl.ds(2 * k1, 2), :, :] = dot(third_ref[...], prod).astype(BF16).reshape(2, COLS, 384)
        return carry

    lax.fori_loop(0, FREQ_ROWS, middle, 0, unroll=True)
    stores[1].start()
    for load in loads[13:]:
        load.wait()
    for j in range(8):
        part = work_ref[:, 16 * j : 16 * (j + 1), :].reshape(FREQ_ROWS * 32, 384)
        grad_values = dot(fourth_ref[j], part)
        for i in range(HALF_ROWS):
            start = COLS * i + 16 * j
            at = slice(start, start + 16)
            piece = grad_values[16 * i : 16 * (i + 1)] * position_mask(start, 16, count_a, count_b)
            grads_ref[0, at, :] = (piece * short_ref[2, at, :].astype(F32)).astype(BF16)
            grads_ref[2, at, :] = (piece * short_ref[0, at, :].astype(F32)).astype(BF16)
    stores[2].start()

    size = 512
    edge = jnp.zeros((8, 384), F32)
    for j in range(3):
        parts_ref[j, 0:8, :] = edge
        parts_ref[j, 8 + total :, :] = edge
    for b in range(total // size):
        at = slice(size * b, size * (b + 1))
        wide = jnp.concatenate([stacked(grads_ref[s, at, :]) for s in range(3)], axis=1)
        out = dot(wide, wt_ref[...])
        for j in range(3):
            parts_ref[j, 8 + size * b : 8 + size * (b + 1), :] = packed(out[:, 256 * j : 256 * (j + 1)])
    gain = jnp.zeros((8, 384), F32)
    bias = jnp.zeros((8, 384), F32)
    for c in range(chunks):
        at = slice(rows * c, rows * (c + 1))
        ahead = parts_ref[0, rows * c : rows * (c + 1) + 16, :][9 : 9 + rows]
        here = parts_ref[1, 8 + rows * c : 8 + rows * (c + 1), :]
        behind = parts_ref[2, rows * c : rows * (c + 1) + 16, :][7 : 7 + rows]
        keep = position_mask(c * rows, rows, count_a, count_b)
        grad_normed = (ahead + here + behind) * keep
        unit, scale, _ = normed_pair(x_ref[c], rows, scales_ref[...], offsets_ref[...])
        gain += column_sums(grad_normed * unit)
        bias += column_sums(grad_normed)
        q = grad_normed * scales_ref[...]
        out_ref[c, :rows, :] = (cot_ref[at, :].astype(F32) + scale * q).astype(BF16)
        out_ref[c, rows:, :rows] = split_rows(to_rows(pair_sum(q) + pair_sum(q * unit), rows))
    small_ref[0:8, :] = gain
    small_ref[8:16, :] = bias
    for store in stores:
        store.wait()


def mixer_backward(
    counts, norm, sums, woutt, scales, offsets, payload, wt, cot, q, unit, conv, short, spec, spectrum, tables
):
    chunks, _, rows = norm.shape
    total = chunks * rows
    first, second, third, fourth = tables
    lanes = HALF_ROWS * 16
    seq = (total, 384)
    cross = (FREQ_ROWS, 256, 256)
    blocked = [norm, *sums, woutt, second, third, scales, offsets]
    return pl.pallas_call(
        mixer_backward_kernel,
        grid=(1,),
        in_specs=[pl.BlockSpec(memory_space=pltpu.SMEM)]
        + [full_spec(a.shape) for a in blocked]
        + [ANYWHERE] * 11,
        out_specs=[ANYWHERE] * 3 + [full_spec(payload.shape), full_spec((16, 384))],
        out_shape=[
            jax.ShapeDtypeStruct(seq, BF16),
            jax.ShapeDtypeStruct(cross, BF16),
            jax.ShapeDtypeStruct((3,) + seq, BF16),
            jax.ShapeDtypeStruct(payload.shape, BF16),
            jax.ShapeDtypeStruct((16, 384), F32),
        ],
        scratch_shapes=[
            pltpu.VMEM(payload.shape, BF16),
            pltpu.VMEM(wt.shape, BF16),
            pltpu.VMEM((3, total + 16, 384), F32),
        ]
        + [pltpu.VMEM(seq, BF16)] * 4
        + [
            pltpu.VMEM((3,) + seq, BF16),
            pltpu.VMEM(first.shape[:2] + (lanes,), BF16),
            pltpu.VMEM(spec.shape, BF16),
            pltpu.VMEM(spectrum.shape, BF16),
            pltpu.VMEM((8, lanes, fourth.shape[2]), BF16),
            pltpu.VMEM((2 * FREQ_ROWS, COLS, 384), BF16),
            pltpu.VMEM(cross, BF16),
            pltpu.VMEM((3,) + seq, BF16),
            pltpu.SemaphoreType.DMA((18,)),
            pltpu.SemaphoreType.DMA((3,)),
        ],
        compiler_params=WIDE_VMEM,
        cost_estimate=work(4),
        name="mixer_backward",
    )(counts, *blocked, payload, wt, cot, q, unit, conv, short, first, spec, spectrum, fourth)


def mixer_grads_kernel(
    counts_ref,
    x_ref,
    scales_ref,
    offsets_ref,
    taps_ref,
    win_ref,
    grads_ref,
    grad_ref,
    conv_ref,
    short_ref,
    gin_ref,
    gtaps_ref,
    normed_ref,
    in_acc,
):
    chunks, tall, _ = x_ref.shape
    rows = tall - STAT_ROWS
    total = chunks * rows
    size = 512
    parts = gin_ref.shape[0]
    share = 192 // parts
    count_a, count_b = counts_ref[0], counts_ref[1]
    edge = jnp.zeros((8, 384), F32)
    normed_ref[0:8, :] = edge
    normed_ref[8 + total :, :] = edge
    for c in range(chunks):
        _, _, normed = normed_pair(x_ref[c], rows, scales_ref[...], offsets_ref[...])
        keep = position_mask(c * rows, rows, count_a, count_b)
        normed_ref[8 + c * rows : 8 + (c + 1) * rows, :] = normed * keep
    gout = jnp.zeros((192, 256), F32)
    for b in range(total // size):
        at = slice(size * b, size * (b + 1))
        wide_grads = jnp.concatenate([stacked(grads_ref[s, at, :]) for s in range(3)], axis=1)
        window = normed_ref[size * b : size * (b + 1) + 16, :]
        wide = jnp.concatenate([stacked(v).astype(BF16) for v in three_shifts(window, size)], axis=1)
        product = dot(wide.T, wide_grads)
        if b == 0:
            in_acc[...] = product
        else:
            in_acc[...] += product
        gated = (conv_ref[at, :].astype(F32) * short_ref[at, :].astype(F32)).astype(BF16)
        gout += fold_rows(dot(stacked(gated).T, stacked(grad_ref[at, :])))
    gout = fold_lanes(gout).astype(BF16)
    for d in range(parts):
        gin_ref[d, 3 * share :, :] = gout[share * d : share * (d + 1)]
    for s in range(3):
        lanes = slice(256 * s, 256 * (s + 1))
        total_in = jnp.zeros((192, 256), F32)
        for j in range(3):
            block = fold_lanes(fold_rows(in_acc[256 * j : 256 * (j + 1), lanes]))
            at = 3 * j + s
            total_in += block * taps_ref[at : at + 1, :]
            gtaps_ref[8 * at : 8 * (at + 1), :] = column_sums(block * win_ref[:, lanes].astype(F32))
        total_in = total_in.astype(BF16)
        for d in range(parts):
            gin_ref[d, share * s : share * (s + 1), :] = total_in[share * d : share * (d + 1)]


def mixer_grads(counts, payload, scales, offsets, taps, win, grads, grad, conv, short, parts):
    chunks, tall, _ = payload.shape
    total = chunks * (tall - STAT_ROWS)
    return pl.pallas_call(
        mixer_grads_kernel,
        grid=(1,),
        in_specs=[pl.BlockSpec(memory_space=pltpu.SMEM)]
        + [full_spec(a.shape) for a in (payload, scales, offsets, taps, win, grads, grad, conv)]
        + [pl.BlockSpec((None, total, 384), lambda i: (1, 0, 0))],
        out_specs=[full_spec((parts, 768 // parts, 256)), full_spec((72, 256))],
        out_shape=[
            jax.ShapeDtypeStruct((parts, 768 // parts, 256), BF16),
            jax.ShapeDtypeStruct((72, 256), F32),
        ],
        scratch_shapes=[pltpu.VMEM((total + 16, 384), F32), pltpu.VMEM((768, 768), F32)],
        compiler_params=VMEM,
        cost_estimate=work(0.01),
        name="mixer_grads",
    )(counts, payload, scales, offsets, taps, win, grads, grad, conv, short)


def filter_back_kernel(
    cross_ref,
    s1_ref,
    c1_ref,
    s2_ref,
    c2_ref,
    feat_ref,
    midt_ref,
    foutt_ref,
    rate_ref,
    third_ref,
    fourth_ref,
    mixer_ref,
    gtaps_ref,
    small_one_ref,
    small_two_ref,
    own_ref,
    gfin_ref,
    gmid_ref,
    gfout_ref,
    gbias_ref,
    work_ref,
    taps_ref,
):
    total = feat_ref.shape[0]
    step_rows = 256

    def second(k1, carry):
        work_ref[pl.ds(2 * k1, 2), :, :] = dot(third_ref[...], cross_ref[k1]).astype(BF16).reshape(2, COLS, 256)
        return carry

    lax.fori_loop(0, FREQ_ROWS, second, 0, unroll=True)

    def last(j, carry):
        start = pl.ds(pl.multiple_of(16 * j, 16), 16)
        part = work_ref[:, start, :].reshape(FREQ_ROWS * 32, 256)
        taps_ref[:, start, :] = dot(fourth_ref[j], part).reshape(FULL_ROWS, 16, 256)
        return carry

    lax.fori_loop(0, 8, last, 0, unroll=True)
    gfin_ref[...] = jnp.zeros_like(gfin_ref)
    gmid_ref[...] = jnp.zeros_like(gmid_ref)
    gfout_ref[...] = jnp.zeros_like(gfout_ref)
    gbias_ref[...] = jnp.zeros_like(gbias_ref)

    def one(i, carry):
        rows = pl.ds(pl.multiple_of(i * step_rows, step_rows), step_rows)
        lag = i * step_rows + lax.broadcasted_iota(jnp.int32, (step_rows, 256), 0)
        signed = jnp.where(lag < total // 2, lag, total - lag)
        distance = signed.astype(F32) * (2.0 / total)
        grad = taps_ref[pl.ds(2 * i, 2), :, :].reshape(step_rows, 256) * jnp.exp(-distance * rate_ref[...])
        grad = grad.astype(BF16)
        gfout_ref[...] += dot(s2_ref[rows, :].T, grad)
        grad_second = dot(grad, foutt_ref[...]) * (SINE_FREQ * c2_ref[rows, :].astype(F32))
        gbias_ref[8:16, :] += column_sums(grad_second)
        grad_second = grad_second.astype(BF16)
        gmid_ref[...] += dot(s1_ref[rows, :].T, grad_second)
        grad_first = dot(grad_second, midt_ref[...]) * (SINE_FREQ * c1_ref[rows, :].astype(F32))
        gbias_ref[0:8, :] += column_sums(grad_first)
        gfin_ref[...] += dot(feat_ref[rows, :].T, grad_first.astype(BF16))
        return carry

    lax.fori_loop(0, total // step_rows, one, 0, unroll=True)


    parts, tall, _ = mixer_ref.shape
    hidden = 128 // parts
    wide = lambda v: jnp.concatenate([v, jnp.zeros((v.shape[0], 128), F32)], axis=1)
    mid = wide(gmid_ref[...]).astype(BF16)
    fout = fold_lanes(gfout_ref[...]).astype(BF16)

    def channel_row(rows):
        row = jnp.sum(rows, axis=0, keepdims=True)
        joined = jnp.concatenate([row[:, :128] + row[:, 128:256], row[:, 256:]], axis=1)
        return fold_lanes(joined)

    same = [
        channel_row(small_one_ref[0:8, :]),
        channel_row(small_two_ref[0:8, :]),
        channel_row(small_one_ref[8:16, :]),
        channel_row(small_two_ref[8:16, :]),
    ]
    same += [jnp.sum(gtaps_ref[8 * i : 8 * (i + 1), :], axis=0, keepdims=True) for i in range(9)]
    same += [wide(gfin_ref[0:5, :] + gfin_ref[5:10, :] + gfin_ref[10:15, :])]
    same += [wide(jnp.sum(gbias_ref[8 * i : 8 * (i + 1), :], axis=0, keepdims=True)) for i in range(2)]
    same += [jnp.zeros((12, 256), F32)]
    same = jnp.concatenate(same, axis=0).astype(BF16)
    for d in range(parts):
        own_ref[d, :tall, :] = mixer_ref[d]
        own_ref[d, tall : tall + hidden, :] = mid[hidden * d : hidden * (d + 1)]
        own_ref[d, tall + hidden : tall + 2 * hidden, :] = fout[hidden * d : hidden * (d + 1)]
        own_ref[d, tall + 2 * hidden :, :] = same


def filter_back(cross, hidden, feats, midt, foutt, rate, third, fourth, mixer, gtaps, small_one, small_two):
    parts, tall, _ = mixer.shape
    return pl.pallas_call(
        filter_back_kernel,
        out_shape=jax.ShapeDtypeStruct((parts, tall + 256 // parts + 32, 256), BF16),
        scratch_shapes=[
            pltpu.VMEM((16, 128), F32),
            pltpu.VMEM((128, 128), F32),
            pltpu.VMEM((128, 256), F32),
            pltpu.VMEM((16, 128), F32),
            pltpu.VMEM((2 * FREQ_ROWS, COLS, 256), BF16),
            pltpu.VMEM((FULL_ROWS, COLS, 256), F32),
        ],
        compiler_params=VMEM,
        cost_estimate=work(0.01),
        name="filter_back",
    )(cross, *hidden, feats, midt, foutt, rate, third, fourth, mixer, gtaps, small_one, small_two)


def unpack_out_kernel(x_ref, out_ref):
    for even in (0, 2):
        a, b = unpack_pairs(x_ref[even].astype(F32), x_ref[even + 1].astype(F32))
        out_ref[0, :, 192 * even : 192 * even + 384] = a.astype(BF16)
        out_ref[1, :, 192 * even : 192 * even + 384] = b.astype(BF16)


def unpack_out(value):
    chunks, rows, _ = value.shape
    return pl.pallas_call(
        unpack_out_kernel,
        grid=(chunks // 4,),
        in_specs=[pl.BlockSpec((4, rows, 384), lambda i: (i, 0, 0))],
        out_specs=pl.BlockSpec((2, rows, 768), lambda i: (i, 0, 0)),
        out_shape=jax.ShapeDtypeStruct((chunks // 2, rows, 768), BF16),
        compiler_params=VMEM,
        cost_estimate=work(0.01),
        name="unpack_out",
    )(value)


def unpack_grad_kernel(x_ref, tokens_ref, out_ref):
    rows = tokens_ref.shape[1]
    sums = jnp.zeros((8, rows), F32)
    for block in range(4):
        sums += join_rows(x_ref[block, rows:, :rows])
    columns = to_columns(sums) * (1.0 / 768.0)
    wide = ([], [])
    for even in (0, 2):
        a, b = unpack_pairs(x_ref[even, :rows].astype(F32), x_ref[even + 1, :rows].astype(F32))
        wide[0].append(a)
        wide[1].append(b)
    for which in range(2):
        token = tokens_ref[which].astype(F32)
        mean, scale = row_stats(token)
        unit = (token - mean) * scale
        grad = jnp.concatenate(wide[which], axis=1)
        mean_q = columns[:, which : which + 1]
        mean_qh = columns[:, 2 + which : 3 + which]
        out_ref[which] = grad - scale * (mean_q + unit * mean_qh)


def unpack_grad(value, tokens):
    chunks, tall, _ = value.shape
    rows = tall - STAT_ROWS
    return pl.pallas_call(
        unpack_grad_kernel,
        grid=(chunks // 4,),
        in_specs=[
            pl.BlockSpec((4, tall, 384), lambda i: (i, 0, 0)),
            pl.BlockSpec((2, rows, 768), lambda i: (i, 0, 0)),
        ],
        out_specs=pl.BlockSpec((2, rows, 768), lambda i: (i, 0, 0)),
        out_shape=jax.ShapeDtypeStruct((chunks // 2, rows, 768), F32),
        compiler_params=VMEM,
        cost_estimate=work(8),
        name="unpack_grad",
    )(value, tokens)


def finish_ffn_kernel(block_ref, *refs):
    pieces, (up_ref, down_ref) = refs[:4], refs[4:]
    share = up_ref.shape[2]
    for r in range(4):
        at = lax.bitwise_xor(block_ref[0], r)
        for t in range(6):
            value = pieces[r][share * t : share * (t + 1), :].astype(F32)
            up_ref[t // 3, at, :, 256 * (t % 3) : 256 * (t % 3 + 1)] = value
        down_ref[at] = pieces[r][6 * share :, :192].astype(F32)


def finish_ffn(block, pieces):
    share = pieces[0].shape[0] // 10
    vmem = pl.BlockSpec(memory_space=pltpu.VMEM)
    return pl.pallas_call(
        finish_ffn_kernel,
        in_specs=[pl.BlockSpec(memory_space=pltpu.SMEM)] + [vmem] * 4,
        out_shape=[
            jax.ShapeDtypeStruct((2, 4, share, 768), F32),
            jax.ShapeDtypeStruct((4, 4 * share, 192), F32),
        ],
        cost_estimate=work(0.01),
        name="finish_ffn",
    )(block, *pieces)


def finish_mixer_kernel(place_ref, *refs):
    pieces, outs = refs[:4], refs[4:]
    in_ref, out_ref, mid_ref, gain_ref, bias_ref, taps_ref, fin_ref, fbias_ref, fout_ref = outs
    share = in_ref.shape[2]
    hidden, shard, cols = mid_ref.shape[0], gain_ref.shape[1], fout_ref.shape[1]
    block, chan_block, chan_start, hidden_start, fout_block, fout_start = [place_ref[i] for i in range(6)]
    start = 4 * share

    def turned(value, shift):
        return pltpu.roll(value, lax.rem(256 - shift, 256), axis=1)

    def of_block(rows, which):
        total = jnp.zeros((rows.stop - rows.start, 256), F32)
        for r in range(4):
            take = lax.bitwise_xor(block, r) == which
            total += jnp.where(take, pieces[r][rows, :].astype(F32), 0.0)
        return total

    for r in range(4):
        at = lax.bitwise_xor(block, r)
        for s in range(3):
            in_ref[s, at] = pieces[r][share * s : share * (s + 1), :192].astype(F32)
        out_ref[at] = pieces[r][3 * share : 4 * share, :192].astype(F32)
    mids = [piece[start : start + hidden, :128].astype(F32) for piece in pieces]
    mid_ref[...] = mids[0] + mids[1] + mids[2] + mids[3]
    fouts = of_block(slice(start + hidden, start + 2 * hidden), fout_block)
    fout_ref[...] = turned(fouts, fout_start)[:, :cols]
    rest = slice(start + 2 * hidden, start + 2 * hidden + 32)
    rows = turned(of_block(rest, chan_block), chan_start)[:, :shard]
    gain_ref[...] = rows[0:2]
    bias_ref[...] = rows[2:4]
    for j in range(3):
        taps_ref[j] = rows[4 + 3 * j : 7 + 3 * j]
    total = pieces[0][rest, :].astype(F32)
    for piece in pieces[1:]:
        total += piece[rest, :].astype(F32)
    filters = turned(total, hidden_start)[:, :hidden]
    fin_ref[...] = filters[13:18]
    fbias_ref[...] = filters[18:20]


def finish_mixer(place, pieces, share, hidden, shard, cols):
    vmem = pl.BlockSpec(memory_space=pltpu.VMEM)
    shapes = ((3, 4, share, 192), (4, share, 192), (hidden, 128), (2, shard), (2, shard))
    shapes += ((3, 3, shard), (5, hidden), (2, hidden), (hidden, cols))
    return pl.pallas_call(
        finish_mixer_kernel,
        in_specs=[pl.BlockSpec(memory_space=pltpu.SMEM)] + [vmem] * 4,
        out_shape=[jax.ShapeDtypeStruct(shape, F32) for shape in shapes],
        compiler_params=VMEM,
        cost_estimate=work(0.01),
        name="finish_mixer",
    )(place, *pieces)


def own_block_kernel(block_ref, in_ref, out_ref, up_ref, down_ref, order_ref, all_ref):
    share = out_ref.shape[1]
    pieces = [in_ref[i, 0] for i in range(3)] + [out_ref[0]]
    wide = [up_ref[g, 0, :, 256 * t : 256 * (t + 1)] for g in range(2) for t in range(3)]
    fill = lambda v: jnp.concatenate([v.astype(F32), jnp.zeros((v.shape[0], 64), F32)], axis=1)
    rows = [fill(v) for v in pieces] + [v.astype(F32) for v in wide] + [fill(down_ref[0])]
    all_ref[...] = jnp.concatenate(rows, axis=0).astype(BF16)


def own_block(block, in_weight, out_weight, up_weight, down_weight, order):
    share = out_weight.shape[1]
    width = out_weight.shape[2]
    return pl.pallas_call(
        own_block_kernel,
        grid_spec=pltpu.PrefetchScalarGridSpec(
            num_scalar_prefetch=1,
            grid=(1,),
            in_specs=[
                pl.BlockSpec((3, 1, share, width), lambda i, at: (0, at[0], 0, 0)),
                pl.BlockSpec((1, share, width), lambda i, at: (at[0], 0, 0)),
                pl.BlockSpec((2, 1, share, 4 * width), lambda i, at: (0, at[0], 0, 0)),
                pl.BlockSpec((1, 4 * share, width), lambda i, at: (at[0], 0, 0)),
                ANYWHERE,
            ],
            out_specs=pl.BlockSpec((14 * share, 256), lambda i, at: (0, 0)),
        ),
        out_shape=jax.ShapeDtypeStruct((14 * share, 256), BF16),
        compiler_params=VMEM,
        cost_estimate=work(0.5),
        name="own_block",
    )(block, in_weight, out_weight, up_weight, down_weight, order)


def lanes_twice(value):
    last = value[:, 128:]
    return jnp.concatenate(
        [value[:, :128], jnp.where(low_lanes(value.shape[0]), last, half_turn(last))], axis=1
    )


def rows_twice(value):
    return jnp.concatenate([value, value[128:192]], axis=0)


def whole_weights_kernel(
    all_ref, taps_ref, win_ref, wtaps_ref, wtapst_ref, wout_ref, woutt_ref, up_ref, upt_ref, down_ref, downt_ref
):
    count, tall, _ = all_ref.shape
    share = tall // 14
    parts = [all_ref[d].astype(F32) for d in range(count)]

    def assembled(start, size):
        return jnp.concatenate([part[start : start + size] for part in parts], axis=0)

    plain = jnp.concatenate([lanes_twice(assembled(share * s, share)) for s in range(3)], axis=1)
    win_ref[...] = plain.astype(BF16)
    for j in range(3):
        rows = slice(256 * j, 256 * (j + 1))
        scaled = rows_twice(plain * taps_ref[j : j + 1, :])
        wtaps_ref[rows, :] = scaled.astype(BF16)
        wtapst_ref[:, rows] = scaled.T.astype(BF16)
    out = rows_twice(lanes_twice(assembled(3 * share, share)))
    wout_ref[...] = out.astype(BF16)
    woutt_ref[...] = out.T.astype(BF16)
    for t in range(6):
        cols = slice(256 * t, 256 * (t + 1))
        up = rows_twice(assembled((4 + t) * share, share))
        up_ref[:, cols] = up.astype(BF16)
        upt_ref[cols, :] = up.T.astype(BF16)
    down = lanes_twice(assembled(10 * share, 4 * share))
    down_ref[...] = down.astype(BF16)
    downt_ref[...] = down.T.astype(BF16)


def whole_weights(gathered, taps):
    vmem = pl.BlockSpec(memory_space=pltpu.VMEM)
    shapes = ((192, 768), (768, 768), (768, 768), (256, 256), (256, 256))
    shapes += ((256, 1536), (1536, 256), (768, 256), (256, 768))
    return pl.pallas_call(
        whole_weights_kernel,
        in_specs=[vmem, vmem],
        out_shape=[jax.ShapeDtypeStruct(shape, BF16) for shape in shapes],
        compiler_params=VMEM,
        cost_estimate=work(1),
        name="whole_weights",
    )(gathered, taps)


def doubled(value, axis):
    return jnp.concatenate([value, lax.slice_in_dim(value, 128, 192, axis=axis)], axis=axis)


def pair_lanes(value):
    head, tail = value[:, :128], value[:, 128:]
    return jnp.concatenate([head, head, tail, tail], axis=1)


def at_block(value, block, axis):
    return lax.dynamic_index_in_dim(value, block, axis=axis, keepdims=False)


def per_device(
    tokens,
    lengths,
    cotangent,
    norm_gain,
    norm_bias,
    in_weight,
    conv_taps,
    filter_in,
    filter_mid,
    filter_bias,
    filter_out,
    out_weight,
    up_weight,
    down_weight,
):
    count, rows, features = tokens.shape
    blocks = in_weight.shape[1]
    data_size = lax.axis_size("dp")
    seq_size = lax.axis_size("seq")
    total = rows * seq_size
    groups = seq_size // blocks
    place = lax.axis_index("seq")
    block = place % blocks
    group = place // blocks
    width = features // blocks
    data_at = lax.axis_index("dp")
    block_at = block.astype(jnp.int32).reshape(1)

    def exchange(value):
        return lax.all_to_all(value, "seq", 0, 0, tiled=True)

    def shared(value):
        out = [value]
        for r in range(1, blocks):
            out.append(lax.ppermute(value, "seq", [(i, i ^ r) for i in range(seq_size)]))
        return out

    def gathered(value):
        out = [value]
        for r in range(1, data_size):
            out.append(lax.ppermute(value, "dp", [(i, i ^ r) for i in range(data_size)]))
        every = jnp.stack(out)
        return jnp.concatenate([lax.dynamic_slice_in_dim(every, data_at ^ i, 1, axis=0) for i in range(data_size)])

    def scattered(value, *others):
        total = at_block(value, data_at, 0).astype(F32)
        for r in range(1, data_size):
            sent = at_block(value, data_at ^ r, 0)
            received = lax.ppermute(sent, "dp", [(i, i ^ r) for i in range(data_size)])
            if others and r == data_size - 1:
                received = after(received, *others)
            total += received.astype(F32)
        return total

    def over_groups(value, *others):
        step = 1
        while step < groups:
            pairs = [(i, i ^ (step * blocks)) for i in range(seq_size)]
            sent = value.astype(BF16)
            received = lax.ppermute(sent, "seq", pairs)
            if others:
                received = after(received, *others)
            value = sent.astype(F32) + received.astype(F32)
            step *= 2
        return value.astype(BF16)

    fout_parts = []
    for q in range(groups):
        pairs = [(groups * (i % blocks) + (i // blocks + q) % groups, i) for i in range(seq_size)]
        fout_parts.append(lax.ppermute(filter_out, "seq", pairs))
    fout_every = jnp.stack(fout_parts)
    fout_block = jnp.concatenate(
        [at_block(fout_every, (i - group) % groups, 0) for i in range(groups)], axis=1
    )

    packed_tokens = after(pack_tokens(tokens), *fout_parts)
    payload = exchange(packed_tokens)
    counts = lax.dynamic_slice_in_dim(lengths, 2 * group, 2, axis=0)

    small = jnp.concatenate(
        [
            norm_gain.reshape(-1),
            norm_bias.reshape(-1),
            conv_taps.reshape(-1),
            filter_in.reshape(-1),
            filter_bias.reshape(-1),
            filter_mid.reshape(-1),
            fout_block.reshape(-1),
        ]
    )
    small_size = -(-small.shape[0] // 2048) * 2048
    small = jnp.pad(small, (0, small_size - small.shape[0])).reshape(-1, 128)
    small_all = gathered(small).reshape(data_size, small_size)
    shard = features // data_size
    hidden_shard = filter_in.shape[1]
    cuts = np.cumsum(
        [0, 2 * shard, 2 * shard, 9 * shard, 5 * hidden_shard, 2 * hidden_shard, 128 * hidden_shard, width * hidden_shard]
    )
    pieces = [small_all[:, cuts[i] : cuts[i + 1]] for i in range(7)]

    def channels(piece, lead):
        whole = jnp.moveaxis(piece.reshape(data_size, lead, shard), 0, 1).reshape(lead, features)
        return lax.dynamic_slice_in_dim(whole, block * width, width, axis=1).astype(F32)

    gains = pair_lanes(channels(pieces[0], 2))
    offsets = pair_lanes(channels(pieces[1], 2))
    taps = channels(pieces[2], 9)
    fin = jnp.moveaxis(pieces[3].reshape(data_size, 5, hidden_shard), 0, 1).reshape(5, 128)
    fbias = jnp.moveaxis(pieces[4].reshape(data_size, 2, hidden_shard), 0, 1).reshape(2, 128)
    fmid = pieces[5].reshape(128, 128)
    fout = doubled(pieces[6].reshape(128, width), 1)
    fin_stack = jnp.concatenate([fin, fin, fin, jnp.zeros((1, 128), BF16)], axis=0)
    channel_ids = block * width + jnp.arange(width, dtype=jnp.int32)
    fast, slow = math.log(100.0) / 0.3, math.log(100.0) / 1.5
    rates = slow + (fast - slow) * channel_ids.astype(F32) / float(features - 1)
    rates = doubled(rates[None, :], 1)

    part = width // data_size
    large = own_block(block_at, in_weight, out_weight, up_weight, down_weight, packed_tokens)
    large_all = lax.all_gather(large, "dp", axis=0, tiled=False)
    taps_wide = doubled(taps, 1).reshape(3, 768)
    w_in_flat, w_taps, w_taps_t, w_out, w_out_t, w_up, w_up_t, w_down, w_down_t = whole_weights(large_all, taps_wide)

    first_np, second_np = stage_tables()
    full_first = jnp.asarray(first_np, BF16)
    full_last = jnp.asarray(np.swapaxes(first_np, 1, 2), BF16)
    second = jnp.asarray(second_np, BF16)
    third = jnp.asarray(second_np.T, BF16)
    tables = (full_first, second, third, full_last)
    feats = jnp.asarray(lag_table(total), BF16)

    hidden = make_filter(
        feats,
        fin_stack,
        fbias.astype(F32),
        jnp.concatenate([fmid, fmid, fmid], axis=0),
        jnp.concatenate([fout, fout], axis=0),
        rates,
        full_first,
        second,
    )
    spectrum = hidden[4]
    hidden = hidden[:4]

    cot = exchange(pack_cotangent(cotangent, spectrum))
    short, spec, conv, middle, stats = mixer_forward(
        counts, payload, gains[0:1], offsets[0:1], w_taps, w_out, spectrum, tables
    )

    out, pair_low, normed_low, unit, norm = feed_forward(
        middle, shared(stats), gains[1:2], offsets[1:2], w_up, w_down
    )
    out = exchange(after(out, cot))
    q, sums, ffn, small_two = feed_back(
        cot, pair_low, normed_low, unit, gains[1:2], w_up_t, w_down_t, data_size
    )
    sums = shared(sums)
    ffn = scattered(ffn).astype(BF16)

    grad, cross, grads, back, small_one = mixer_backward(
        counts,
        norm,
        sums,
        w_out_t,
        gains[0:1],
        offsets[0:1],
        payload,
        w_taps_t,
        cot.reshape(total, 384),
        q,
        unit,
        conv,
        short,
        spec,
        spectrum,
        tables,
    )
    ffn = over_groups(ffn)
    back = exchange(after(back, out, ffn))
    ffn_pieces = shared(ffn)
    g_mixer, g_taps = mixer_grads(
        counts,
        payload,
        gains[0:1],
        offsets[0:1],
        jnp.pad(taps, ((0, 0), (0, 256 - width))),
        w_in_flat,
        grads,
        grad,
        conv,
        short,
        data_size,
    )
    out_tokens = unpack_out(out)
    grad_tokens = unpack_grad(back, tokens)
    own = filter_back(
        cross, hidden, feats, fmid.T, fout.T, rates, third, full_last, g_mixer, g_taps, small_one, small_two
    )
    own = over_groups(scattered(own, out_tokens), grad_tokens)
    cols = features // seq_size
    places = [
        block,
        data_at * shard // width,
        data_at * shard % width,
        data_at * hidden_shard,
        place // groups,
        place % groups * cols,
    ]
    finished = finish_mixer(jnp.stack(places).astype(jnp.int32), shared(own), part, hidden_shard, shard, cols)
    grad_in, grad_outw, grad_mid, grad_gain, grad_bias, grad_taps, grad_fin, grad_fbias, grad_fout = finished
    grad_up, grad_down = finish_ffn(block_at, [after(ffn_pieces[0], own)] + ffn_pieces[1:])
    return (
        out_tokens,
        grad_tokens,
        grad_gain,
        grad_bias,
        grad_in,
        grad_taps,
        grad_fin,
        grad_mid,
        grad_fbias,
        grad_fout,
        grad_outw,
        grad_up,
        grad_down,
    )


def solution(mesh):
    placed = (
        P("dp", "seq", None),
        P("dp"),
        P("dp", "seq", None),
        P(None, "dp"),
        P(None, "dp"),
        P(None, None, "dp", None),
        P(None, None, "dp"),
        P(None, "dp"),
        P("dp", None),
        P(None, "dp"),
        P("dp", "seq"),
        P(None, "dp", None),
        P(None, None, "dp", None),
        P(None, "dp", None),
    )
    return jax.shard_map(
        per_device,
        mesh=mesh,
        in_specs=placed,
        out_specs=(
            P("dp", "seq", None),
            P("dp", "seq", None),
            P(None, "dp"),
            P(None, "dp"),
            P(None, None, "dp", None),
            P(None, None, "dp"),
            P(None, "dp"),
            P("dp", None),
            P(None, "dp"),
            P("dp", "seq"),
            P(None, "dp", None),
            P(None, None, "dp", None),
            P(None, "dp", None),
        ),
        check_vma=False,
    )
```
